32 devices in a mesh: gz: 4 (over x, core), ty: 2 (over y), tx: 4 (over z).
Axes of the slice: x: 2, y: 2, z: 4, core: 2. Of those that a mesh axis runs over, the one named last changes fastest.
Arguments:
- images: bfloat16 [4, 1024, 2048], P('gz', 'ty', 'tx'), may hold values from -40 to 40, as said below
- boundary: bfloat16 [1024, 2048], P('ty', 'tx'), may hold values from -40 to 40, as said below
- anchor: float32 [4, 256, 512], P('gz', 'ty', 'tx'), may hold values from 0.02 to 0.5
Outputs:
- mesh_shift: float32 [4, 2, 256, 512], P('gz', None, 'ty', 'tx')
- drift: float32 [4, 2, 4, 2, 128], P('gz', 'ty', 'tx')
The draws below stay inside these ranges and needn't reach their ends.
Inputs may be any that keep to these rules, and one draw needn't show every extreme that they name: `images`: pixel intensities. `boundary`: pixel intensities.
All inputs are finite; a program needn't handle non-finite values.
Results may differ from the reference program's by a relative error of at most 0.0003.
Values may be sent and summed in bfloat16 or wider, within the bound.
No kernel may reach another device: no remote copies, remote signals or barrier semaphores. Data moves between devices by JAX's collectives and lax.ppermute only.
A program may use at most 64 MiB of HBM per device.

```python
import math
import jax
import jax.numpy as jnp
from jax import lax

PATCH = 128
STRIDE = 4
SWEEPS = 32
TILE = 512
NODES = 128
NZ = 4
NY = 1024
NX = 2048
MY = 256
MX = 512
N_TY = 2
N_TX = 4


def box_blur(field):
    rows_sum = field
    for lag_index in range(1, 8):
        rows_sum = rows_sum + jnp.roll(field, lag_index, axis=0)
    both_sum = rows_sum
    for lag_index in range(1, 8):
        both_sum = both_sum + jnp.roll(rows_sum, lag_index, axis=1)
    return both_sum * 0.125


def layer_texture(key, layer):
    layer_key = jax.random.fold_in(jax.random.fold_in(key, 23), layer)
    white_noise = jax.random.normal(layer_key, (NY, NX), jnp.float32)
    return box_blur(white_noise)


def expand_patches(values):
    return jnp.repeat(jnp.repeat(values, PATCH, axis=0), PATCH, axis=1)


def volume_views(key, first, count):
    subkeys = jax.random.split(jax.random.fold_in(key, 11), 3)
    grid_rows = NY // PATCH
    grid_cols = NX // PATCH
    segment = jnp.cumsum(jax.random.randint(subkeys[0], (NZ + 1, 2), -3, 4), axis=0).astype(jnp.int32)
    oblique = jax.random.randint(subkeys[1], (NZ + 3, 2, grid_rows, grid_cols), -2, 3).astype(jnp.int32)
    row_index = jnp.arange(NY, dtype=jnp.int32)[:, None]
    col_index = jnp.arange(NX, dtype=jnp.int32)[None, :]

    def section_view(section):
        total = jnp.zeros((NY, NX), jnp.float32)
        moves = lax.dynamic_index_in_dim(segment, section, 0, keepdims=False)
        for depth in (-1, 0, 1):
            layer = section + depth + 1
            texture = layer_texture(key, layer)
            slope = lax.dynamic_index_in_dim(oblique, layer, 0, keepdims=False)
            row_move = moves[0] - depth * expand_patches(slope[0])
            col_move = moves[1] - depth * expand_patches(slope[1])
            source = (row_index - row_move) % NY * NX + (col_index - col_move) % NX
            total = total + jnp.take(texture.reshape(-1), source.reshape(-1)).reshape(NY, NX)
        return total
    shared = lax.map(section_view, first + jnp.arange(count, dtype=jnp.int32))
    noise_key = jax.random.fold_in(subkeys[2], first)
    noise = math.sqrt(0.52) * jax.random.normal(noise_key, (count, NY, NX), jnp.float32)
    values = 0.4 * shared + noise
    return jnp.clip(values, -40.0, 40.0)


def draw_images(key, part):
    return volume_views(key, 1, NZ).astype(jnp.bfloat16)


def draw_boundary(key, part):
    return volume_views(key, 0, 1)[0].astype(jnp.bfloat16)


def levels(key, dims, cuts, smallest, largest):
    def one(dim, blocks):
        draws = jax.random.uniform(jax.random.fold_in(jax.random.fold_in(key, 6), dim), (blocks,), jnp.float32, smallest / len(cuts), largest / len(cuts))
        return jnp.repeat(jnp.exp(draws), dims[dim] // blocks).reshape((-1,) + (1,) * (len(dims) - dim - 1))

    factor_of = one(*cuts[0])
    for cut in cuts[1:]:
        factor_of = factor_of * one(*cut)
    return factor_of


def setup_inputs(seed: int = 0) -> dict:
    arg_keys = jax.random.split(jax.random.key(seed), 4)
    images = draw_images(jax.random.fold_in(arg_keys[3], 71), 0)
    boundary = draw_boundary(jax.random.fold_in(arg_keys[3], 71), 0)
    anchor = jnp.clip(jnp.exp(math.log(0.5) - 3.218876 * jax.random.uniform(arg_keys[2], (NZ, MY, MX), jnp.float32) ** levels(arg_keys[2], (NZ, MY, MX), ((0, 4), (1, 2), (2, 4)), -0.2, 0.2)), 0.02, 0.5)
    return dict(images=images, boundary=boundary, anchor=anchor)


highest = lax.Precision.HIGHEST


def hat_weight(offset):
    return jnp.maximum(0.0, 1.0 - jnp.abs(offset))


def spread_table(nodes, patches):
    node_pos = (jnp.arange(nodes, dtype=jnp.float32) + 0.5) * STRIDE / PATCH - 0.5
    centers = jnp.arange(patches, dtype=jnp.float32)
    weights = hat_weight(node_pos[:, None] - centers[None, :])
    return weights / jnp.sum(weights, axis=1, keepdims=True)


def soft_flow(correlation):
    leading = correlation.shape[:-2]
    scores = (correlation / PATCH).reshape(leading + (PATCH * PATCH,))
    weights = jax.nn.softmax(scores, axis=-1).reshape(leading + (PATCH, PATCH))
    lagged = jnp.arange(PATCH, dtype=jnp.int32)
    signed = jnp.where(lagged < PATCH // 2, lagged, lagged - PATCH).astype(jnp.float32)
    along_rows = jnp.sum(weights * signed[:, None], axis=(-2, -1))
    along_cols = jnp.sum(weights * signed[None, :], axis=(-2, -1))
    return jnp.stack([along_rows, along_cols], axis=-1) / STRIDE


def reference(images, boundary, anchor):
    grid_rows = NY // PATCH
    grid_cols = NX // PATCH
    stacked = jnp.concatenate([boundary[None], images], axis=0)
    pixels = stacked.astype(jnp.float32).reshape(NZ + 1, grid_rows, PATCH, grid_cols, PATCH).transpose(0, 1, 3, 2, 4)
    spectra = jnp.fft.fft2(pixels)
    sections = jnp.arange(NZ, dtype=jnp.int32)

    def flows_at(distance):
        def one_section(section):
            earlier = lax.dynamic_index_in_dim(spectra, jnp.maximum(section + 1 - distance, 0).astype(jnp.int32), 0, keepdims=False)
            current = lax.dynamic_index_in_dim(spectra, (section + 1).astype(jnp.int32), 0, keepdims=False)
            correlation = jnp.fft.ifft2(jnp.conj(earlier) * current).real
            return jnp.where(section + 1 >= distance, soft_flow(correlation), 0.0)
        return lax.map(one_section, sections)

    nearer = flows_at(1)
    farther = flows_at(2)
    before = jnp.concatenate([jnp.zeros_like(nearer[:1]), nearer[:-1]], axis=0)
    position = sections[:, None, None, None]
    patch_target = jnp.where(position <= 1, nearer, 0.5 * (nearer + farther - before))
    per_tile = TILE // PATCH
    table = spread_table(NODES, per_tile)
    tiled = patch_target.reshape(NZ, N_TY, per_tile, N_TX, per_tile, 2)
    target = jnp.einsum('ip,zypxqc,jq->zcyixj', table, tiled, table, precision=highest).reshape(NZ, 2, MY, MX)
    weight = anchor[:, None]

    def sweep(counter, mesh):
        padded = jnp.pad(mesh, ((0, 0), (0, 0), (1, 1), (1, 1)))
        beside_all = padded[:, :, 2:, 1:-1] + padded[:, :, :-2, 1:-1] + padded[:, :, 1:-1, 2:] + padded[:, :, 1:-1, :-2]
        return (beside_all + weight * target) / (4.0 + weight)

    mesh_shift = lax.fori_loop(0, SWEEPS, sweep, target)
    blocks = mesh_shift.reshape(NZ, 2, N_TY, NODES, N_TX, NODES)
    down_rows = jnp.mean(blocks[:, 0], axis=4).transpose(0, 1, 3, 2)
    across = jnp.mean(blocks[:, 1], axis=2)
    profile = jnp.stack([down_rows, across], axis=3)
    ramp = jnp.arange(NODES, dtype=jnp.float32)
    landing = jnp.clip(ramp + profile, 0.0, NODES - 1.0)
    maps = hat_weight(landing[..., None] - ramp)
    start = jnp.broadcast_to(jnp.eye(NODES, dtype=jnp.float32), maps.shape[1:])

    def compose_step(carry, section_maps):
        joined = jnp.einsum('yxcij,yxcjk->yxcik', carry, section_maps, precision=highest)
        placed = jnp.einsum('yxcij,j->yxci', joined, ramp, precision=highest) - ramp
        return joined, placed

    outcome = lax.scan(compose_step, start, maps)
    return mesh_shift, outcome[1]
```

```python
import math

import jax
import jax.numpy as jnp
import numpy as np
from jax import lax
from jax.experimental import pallas as pl
from jax.experimental.pallas import tpu as pltpu
from jax.sharding import PartitionSpec as P

PATCH = 128
STRIDE = 4
SWEEPS = 32
HALF = PATCH // 2
BF16 = jnp.bfloat16
F32 = jnp.float32


def split_table(table):
    high = table.astype(BF16)
    low = (table - high.astype(np.float64)).astype(BF16)
    return (high, low)


def transform_tables():
    counter = np.arange(PATCH)
    phase = (counter[:, None] * counter[None, :] % PATCH) * (2.0 * math.pi / PATCH)
    basis = np.concatenate([np.cos(phase[:HALF]), np.sin(phase[:HALF])])
    basis[HALF] = np.cos(phase[HALF])
    gains = np.full(PATCH, 2.0)
    gains[0] = gains[HALF] = 1.0
    inverse = basis.T * gains / PATCH
    forward_pair = np.zeros((2, PATCH, 2, 2, HALF))
    inverse_pair = np.zeros((2, 2, HALF, 2, PATCH))
    for side in range(2):
        forward_pair[side, :, :, side] = basis.T.reshape(PATCH, 2, HALF)
        inverse_pair[:, side, :, side] = inverse.T.reshape(2, HALF, PATCH)
    forward_pair = forward_pair.reshape(2 * PATCH, 2 * PATCH)
    inverse_pair = inverse_pair.reshape(2 * PATCH, 2 * PATCH)
    right_high, right_low = split_table(forward_pair)
    back_high, back_low = split_table(inverse_pair)
    left_high, left_low = split_table(basis)
    undo_high, undo_low = split_table(inverse / PATCH)
    rights = np.stack([right_high, right_low, back_high, back_low])
    lefts = np.stack(
        [
            np.concatenate([left_high, left_high, left_low], axis=1),
            np.concatenate([undo_high, undo_high, undo_low], axis=1),
        ]
    )
    return (rights, lefts)


def halves(value):
    high = value.astype(BF16)
    return (high, (value - high.astype(F32)).astype(BF16))


def dot(left, right):
    return jnp.dot(left, right, preferred_element_type=F32)


def left_transform(table, value):
    high, low = halves(value)
    return dot(table, jnp.concatenate([high, low, high], axis=0))


def quarters(spec):
    return (
        (spec[:HALF, :PATCH], spec[:HALF, PATCH:]),
        (spec[HALF:, :PATCH], spec[HALF:, PATCH:]),
    )


def cross_operand(spec):
    (cc, cs), (sc, ss) = quarters(spec)
    first_row = lax.broadcasted_iota(jnp.int32, (HALF, PATCH), 0) == 0
    first_lane = lax.broadcasted_iota(jnp.int32, (HALF, PATCH), 1) % HALF == 0

    def lanes(cosine, sine):
        return (cosine, jnp.where(first_lane, sine, cosine), jnp.where(first_lane, 0.0, sine))

    return (
        lanes(cc, cs),
        lanes(jnp.where(first_row, sc, cc), jnp.where(first_row, ss, cs)),
        lanes(jnp.where(first_row, 0.0, sc), jnp.where(first_row, 0.0, ss)),
    )


def cross(operand, spec):
    (row_c, row_d, row_s) = operand
    (bc, bs) = quarters(spec)

    def cosine(a, b):
        return a[0] * b[0] + a[2] * b[1]

    def sine(a, b):
        return a[1] * b[1] - a[2] * b[0]

    cc = cosine(row_c, bc) + cosine(row_s, bs)
    cs = sine(row_c, bc) + sine(row_s, bs)
    sc = cosine(row_d, bs) - cosine(row_s, bc)
    ss = sine(row_d, bs) - sine(row_s, bc)
    return jnp.concatenate(
        [jnp.concatenate([cc, cs], axis=1), jnp.concatenate([sc, ss], axis=1)], axis=0
    )


def flows_kernel(prior_ref, own_ref, later_ref, rights_ref, lefts_ref, out_ref, stats_ref):
    rows, cols = own_ref.shape
    per_row = cols // (2 * PATCH)
    blocks = rows // PATCH * per_row
    patches = 2 * blocks

    def block_step(block, carry):
        row = pl.multiple_of(block // per_row * PATCH, PATCH)
        col = pl.multiple_of(block % per_row * (2 * PATCH), 2 * PATCH)
        window = (pl.ds(row, PATCH), pl.ds(col, 2 * PATCH))
        pixels = jnp.concatenate([ref[window] for ref in (prior_ref, own_ref, later_ref)], axis=0)
        right = dot(pixels, rights_ref[0]) + dot(pixels, rights_ref[1])
        wide = jnp.concatenate([right[:PATCH], right[PATCH : 2 * PATCH], right[2 * PATCH :]], axis=1)
        spec = left_transform(lefts_ref[0], wide)
        prior, own, later = (spec[:, i * 2 * PATCH : (i + 1) * 2 * PATCH] for i in range(3))
        operand = cross_operand(prior)
        products = jnp.concatenate([cross(operand, own), cross(operand, later)], axis=0)
        high, low = halves(products)
        back = dot(high, rights_ref[2]) + dot(low, rights_ref[2]) + dot(high, rights_ref[3])
        back = jnp.concatenate([back[:PATCH], back[PATCH:]], axis=1)
        scores = left_transform(lefts_ref[1], back)
        groups = scores.reshape(PATCH // 8, 8, 4 * PATCH)
        peak = jnp.max(groups, axis=0)
        total = jnp.zeros_like(peak)
        moment = jnp.zeros_like(peak)
        for group in range(PATCH // 8):
            weight = jnp.exp(groups[group] - peak)
            shift = 8 * group - (PATCH if group >= PATCH // 16 else 0)
            total = total + weight
            moment = moment + float(shift) * weight
        for pair in range(2):
            for side in range(2):
                lanes = slice((2 * pair + side) * PATCH, (2 * pair + side + 1) * PATCH)
                slot = pair * patches + 2 * block + side
                stats_ref[0, slot] = peak[:, lanes]
                stats_ref[1, slot] = total[:, lanes]
                stats_ref[2, slot] = moment[:, lanes]
        return carry

    lax.fori_loop(0, blocks, block_step, 0)
    peak = stats_ref[0]
    best = jnp.max(jnp.max(peak, axis=1, keepdims=True), axis=2, keepdims=True)
    scale = jnp.exp(peak - best)
    total = scale * stats_ref[1]
    within = lax.broadcasted_iota(jnp.int32, peak.shape, 1).astype(F32)
    moment = scale * stats_ref[2] + within * total
    total = jnp.sum(total, axis=1)
    lane = lax.broadcasted_iota(jnp.int32, total.shape, 1)
    signed = jnp.where(lane < HALF, lane, lane - PATCH).astype(F32)
    mass = jnp.sum(total, axis=1, keepdims=True) * STRIDE
    along_rows = jnp.sum(jnp.sum(moment, axis=1), axis=1, keepdims=True) / mass
    along_cols = jnp.sum(total * signed, axis=1, keepdims=True) / mass
    lane = lax.broadcasted_iota(jnp.int32, out_ref.shape, 1)
    near_rows, near_cols = along_rows[:patches], along_cols[:patches]
    out = jnp.where(lane == 0, near_rows, near_cols)
    out = jnp.where(lane == 2, along_rows[patches:] - near_rows, out)
    out_ref[...] = jnp.where(lane == 3, along_cols[patches:] - near_cols, out)


def flows(prior, own, later):
    rights, lefts = transform_tables()
    patches = own.shape[0] // PATCH * (own.shape[1] // PATCH)
    return pl.pallas_call(
        flows_kernel,
        out_shape=jax.ShapeDtypeStruct((patches, PATCH), F32),
        scratch_shapes=[pltpu.VMEM((3, 2 * patches, 8, PATCH), F32)],
        compiler_params=pltpu.CompilerParams(vmem_limit_bytes=32 * 2**20),
        name="flows",
    )(prior, own, later, jnp.asarray(rights), jnp.asarray(lefts))


def spread_weights(nodes, patches):
    node_pos = (np.arange(nodes) + 0.5) * STRIDE / PATCH - 0.5
    weights = np.maximum(0.0, 1.0 - np.abs(node_pos[:, None] - np.arange(patches)[None, :]))
    return weights / weights.sum(axis=1, keepdims=True)


def ring_tables(nodes, patches):
    span = np.arange(nodes + 2 * SWEEPS) - SWEEPS
    lane_node = np.concatenate([span[SWEEPS:], span, span[:SWEEPS]])
    spread = spread_weights(nodes, patches)

    def wide(positions):
        table = np.zeros((len(positions), 3, patches))
        for tile in range(3):
            at = positions - (tile - 1) * nodes
            hit = (at >= 0) & (at < nodes)
            table[hit, tile] = spread[at[hit]]
        return table

    shape = (3, 3, patches, patches)
    rows = wide(span)[:, None, :, :, None]
    cols = wide(lane_node).transpose(1, 2, 0)[:, None, None]
    left = np.broadcast_to(rows, (len(span),) + shape).reshape(len(span), -1)
    right = np.broadcast_to(cols, shape + (len(lane_node),)).reshape(-1, len(lane_node))
    return (left.astype(BF16), right.astype(np.float32), lane_node.astype(np.int32)[None])


def relax_kernel(
    place_ref, own_ref, even_ref, odd_ref, anchor_ref, even_anchor_ref, odd_anchor_ref,
    left_ref, right_ref, lane_node_ref, mesh_ref, profile_ref, work_ref, gain_ref, base_ref,
):
    rows, lanes = work_ref.shape
    nodes = mesh_ref.shape[1]
    turn = nodes // 2
    at_even = place_ref[2] == 1

    def beside(even, odd):
        return (jnp.where(at_even, odd, even), jnp.where(at_even, even, odd))

    before, after = beside(even_ref[...], odd_ref[...])
    sources = jnp.concatenate([before, own_ref[...], after], axis=0)
    first = lax.broadcasted_iota(jnp.int32, (1, lanes), 1)
    second = (first >= nodes + SWEEPS) & (first < lanes - SWEEPS)
    spread = jnp.where(second, sources[:, 1:2], sources[:, 0:1]) * right_ref[...]
    target = jnp.zeros((rows, lanes), F32)
    for piece in range(3):
        part = spread.astype(BF16)
        target = target + dot(left_ref[...], part)
        spread = spread - part.astype(F32)
    own = anchor_ref[...]
    before, after = beside(even_anchor_ref[...], odd_anchor_ref[...])
    lane = lax.broadcasted_iota(jnp.int32, own.shape, 1)
    turned = pltpu.roll(own, turn, 1)
    middle = jnp.where(lane < turn, jnp.where(lane < SWEEPS, after, pltpu.roll(before, turn, 1)), turned)
    last = jnp.where(lane < turn, turned, jnp.where(lane < turn + SWEEPS, pltpu.roll(after, turn, 1), before))
    weight = jnp.concatenate([own, middle, last], axis=1)
    row_node = lax.broadcasted_iota(jnp.int32, (rows, lanes), 0) - SWEEPS + place_ref[0]
    col_node = lane_node_ref[...] + place_ref[1]
    inside = (row_node >= 0) & (row_node < place_ref[3]) & (col_node >= 0) & (col_node < place_ref[4])
    gain = jnp.where(inside, 1.0 / (4.0 + weight), 0.0)
    gain_ref[...] = gain
    base_ref[...] = gain * weight * target
    work_ref[...] = jnp.where(inside, target, 0.0)
    group = 8
    for step in range(SWEEPS // group):
        window = slice(step * group, rows - step * group)
        count = rows - 2 * step * group

        def sweep(counter, carry):
            mesh = work_ref[window]
            around = pltpu.roll(mesh, 1, 0) + pltpu.roll(mesh, count - 1, 0)
            around = around + pltpu.roll(mesh, 1, 1) + pltpu.roll(mesh, lanes - 1, 1)
            work_ref[window] = gain_ref[window] * around + base_ref[window]
            return carry

        lax.fori_loop(0, group, sweep, 0)
    final = work_ref[SWEEPS : SWEEPS + nodes]
    down = final[:, :nodes]
    tail = pltpu.roll(final[:, nodes:], turn, 1)
    across = tail[:, nodes:]
    mesh_ref[0] = down
    mesh_ref[1] = across
    share = 1.0 / nodes
    down_mean = jnp.sum(jnp.transpose(down), axis=0, keepdims=True) * share
    across_mean = jnp.sum(across, axis=0, keepdims=True) * share
    row = lax.broadcasted_iota(jnp.int32, profile_ref.shape, 0)
    ramp = lax.broadcasted_iota(jnp.int32, profile_ref.shape, 1).astype(F32)
    profile = jnp.where(row == 0, down_mean, across_mean)
    profile_ref[...] = jnp.clip(ramp + profile, 0.0, nodes - 1.0)


def relax(place, targets, anchors, nodes, patches):
    left, right, lane_node = ring_tables(nodes, patches)
    rows, lanes = left.shape[0], right.shape[1]
    vmem = pl.BlockSpec(memory_space=pltpu.VMEM)
    return pl.pallas_call(
        relax_kernel,
        out_shape=(
            jax.ShapeDtypeStruct((2, nodes, nodes), F32),
            jax.ShapeDtypeStruct((8, nodes), F32),
        ),
        in_specs=[pl.BlockSpec(memory_space=pltpu.SMEM)] + [vmem] * 9,
        out_specs=(vmem, vmem),
        scratch_shapes=[pltpu.VMEM((rows, lanes), F32)] * 3,
        compiler_params=pltpu.CompilerParams(vmem_limit_bytes=32 * 2**20),
        name="relax",
    )(place, *targets, *anchors, jnp.asarray(left), jnp.asarray(right), jnp.asarray(lane_node))


def compose_kernel(place_ref, landings_ref, out_ref):
    count = landings_ref.shape[0]
    nodes = landings_ref.shape[2]
    ramp = lax.broadcasted_iota(jnp.int32, out_ref.shape, 1).astype(F32)
    value = landings_ref[count - 1]
    for section in range(count - 2, -1, -1):
        landing = landings_ref[section]
        floor = jnp.minimum(jnp.floor(landing), nodes - 2.0)
        index = floor.astype(jnp.int32)
        share = landing - floor
        below = jnp.take_along_axis(value, index, axis=1)
        above = jnp.take_along_axis(value, index + 1, axis=1)
        joined = (1.0 - share) * below + share * above
        value = jnp.where(place_ref[5] > section, joined, landing)
    out_ref[...] = value - ramp


def compose(place, landings):
    vmem = pl.BlockSpec(memory_space=pltpu.VMEM)
    return pl.pallas_call(
        compose_kernel,
        out_shape=jax.ShapeDtypeStruct(landings.shape[1:], F32),
        in_specs=[pl.BlockSpec(memory_space=pltpu.SMEM), vmem],
        out_specs=vmem,
        name="compose",
    )(place, landings)


def swap_pairs(value, axis, first, spare):
    count, other = lax.axis_size(axis), lax.axis_size(spare)
    axes = ("gz", "ty", "tx")
    flip = axes.index(axis) > axes.index(spare)

    def place(here, beside):
        return beside * count + here if flip else here * other + beside

    moves = []
    for here in range(count):
        there = ((here + first) ^ 1) - first
        for beside in range(other):
            target = place(there, beside) if 0 <= there < count else place(here, beside ^ 1)
            moves.append((place(here, beside), target))
    return lax.ppermute(value, (spare, axis) if flip else (axis, spare), moves)


def local(images, boundary, anchor):
    nodes = anchor.shape[1]
    own = images[0]
    patches = own.shape[0] // PATCH
    section, ty, tx = (lax.axis_index(axis) for axis in ("gz", "ty", "tx"))
    sections = lax.axis_size("gz")
    n_ty, n_tx = lax.axis_size("ty"), lax.axis_size("tx")
    place = jnp.stack(
        [ty * nodes, tx * nodes, 1 - tx % 2, n_ty * nodes, n_tx * nodes, section]
    ).astype(jnp.int32)
    even = section % 2 == 0
    chip = swap_pairs(own, "gz", 0, "ty")
    far = swap_pairs(own, "gz", 1, "ty")
    prior = jnp.where(even, jnp.where(section == 0, boundary, far), chip)
    later = jnp.where(even, chip, far)
    up, down = rows_beside(anchor[0])
    rows = jnp.concatenate([up[nodes - SWEEPS :], anchor[0], down[:SWEEPS]], axis=0)
    anchors = (rows, swap_pairs(rows, "tx", 0, "gz"), swap_pairs(rows, "tx", 1, "gz"))
    flow = flows(prior, own, later)
    turn = [(i, (i + 1) % sections) for i in range(sections)]
    up, down = rows_beside(flow)
    before = lax.ppermute(flow, "gz", turn)
    flow = jnp.concatenate([up, flow, down], axis=0)
    up, down = rows_beside(before)
    before = jnp.concatenate([up, before, down], axis=0)
    column = jnp.where(section <= 1, flow[:, 0:2], 0.5 * (flow[:, 0:2] + before[:, 2:4]))
    column = jnp.pad(column, ((0, 0), (0, PATCH - 2)))
    targets = (column, swap_pairs(column, "tx", 0, "gz"), swap_pairs(column, "tx", 1, "gz"))
    mesh, landing = relax(place, targets, anchors, nodes, patches)
    landings = lax.all_gather(landing, "gz", axis=0)
    drift = compose(place, landings)
    return (mesh[None], drift[:2].reshape(1, 1, 1, 2, nodes))


def rows_beside(value):
    count = lax.axis_size("ty")
    if count == 2:
        other = swap_pairs(value, "ty", 0, "gz")
        return (other, other)
    even = swap_pairs(value, "ty", 0, "gz")
    odd = swap_pairs(value, "ty", 1, "gz")
    at_even = lax.axis_index("ty") % 2 == 0
    return (jnp.where(at_even, odd, even), jnp.where(at_even, even, odd))


def solution(mesh):
    return jax.shard_map(
        local,
        mesh=mesh,
        in_specs=(P("gz", "ty", "tx"), P("ty", "tx"), P("gz", "ty", "tx")),
        out_specs=(P("gz", None, "ty", "tx"), P("gz", "ty", "tx", None, None)),
        check_vma=False,
    )
```

```python
import math

import jax
import jax.numpy as jnp
import numpy as np
from jax import lax
from jax.experimental import pallas as pl
from jax.experimental.pallas import tpu as pltpu
from jax.sharding import PartitionSpec as P

PATCH = 128
STRIDE = 4
SWEEPS = 32
HALF = PATCH // 2
BF16 = jnp.bfloat16
F32 = jnp.float32


def split_table(table):
    high = table.astype(BF16)
    low = (table - high.astype(np.float64)).astype(BF16)
    return (high, low)


def transform_tables():
    counter = np.arange(PATCH)
    phase = (counter[:, None] * counter[None, :] % PATCH) * (2.0 * math.pi / PATCH)
    basis = np.concatenate([np.cos(phase[:HALF]), np.sin(phase[:HALF])])
    basis[HALF] = np.cos(phase[HALF])
    gains = np.full(PATCH, 2.0)
    gains[0] = gains[HALF] = 1.0
    inverse = basis.T * gains / PATCH
    forward_pair = np.zeros((2, PATCH, 2, 2, HALF))
    inverse_pair = np.zeros((2, 2, HALF, 2, PATCH))
    for side in range(2):
        forward_pair[side, :, :, side] = basis.T.reshape(PATCH, 2, HALF)
        inverse_pair[:, side, :, side] = inverse.T.reshape(2, HALF, PATCH)
    forward_pair = forward_pair.reshape(2 * PATCH, 2 * PATCH)
    inverse_pair = inverse_pair.reshape(2 * PATCH, 2 * PATCH)
    right_high, right_low = split_table(forward_pair)
    back_high, back_low = split_table(inverse_pair)
    left_high, left_low = split_table(basis)
    undo_high, undo_low = split_table(inverse / PATCH)
    rights = np.stack([right_high, right_low, back_high, back_low])
    lefts = np.stack(
        [
            np.concatenate([left_high, left_high, left_low], axis=1),
            np.concatenate([undo_high, undo_high, undo_low], axis=1),
        ]
    )
    return (rights, lefts)


def halves(value):
    high = value.astype(BF16)
    return (high, (value - high.astype(F32)).astype(BF16))


def dot(left, right):
    return jnp.dot(left, right, preferred_element_type=F32)


def left_transform(table, value):
    high, low = halves(value)
    return dot(table, jnp.concatenate([high, low, high], axis=0))


def quarters(spec):
    return (
        (spec[:HALF, :PATCH], spec[:HALF, PATCH:]),
        (spec[HALF:, :PATCH], spec[HALF:, PATCH:]),
    )


def cross_operand(spec):
    (cc, cs), (sc, ss) = quarters(spec)
    first_row = lax.broadcasted_iota(jnp.int32, (HALF, PATCH), 0) == 0
    first_lane = lax.broadcasted_iota(jnp.int32, (HALF, PATCH), 1) % HALF == 0

    def lanes(cosine, sine):
        return (cosine, jnp.where(first_lane, sine, cosine), jnp.where(first_lane, 0.0, sine))

    return (
        lanes(cc, cs),
        lanes(jnp.where(first_row, sc, cc), jnp.where(first_row, ss, cs)),
        lanes(jnp.where(first_row, 0.0, sc), jnp.where(first_row, 0.0, ss)),
    )


def cross(operand, spec):
    (row_c, row_d, row_s) = operand
    (bc, bs) = quarters(spec)

    def cosine(a, b):
        return a[0] * b[0] + a[2] * b[1]

    def sine(a, b):
        return a[1] * b[1] - a[2] * b[0]

    cc = cosine(row_c, bc) + cosine(row_s, bs)
    cs = sine(row_c, bc) + sine(row_s, bs)
    sc = cosine(row_d, bs) - cosine(row_s, bc)
    ss = sine(row_d, bs) - sine(row_s, bc)
    return jnp.concatenate(
        [jnp.concatenate([cc, cs], axis=1), jnp.concatenate([sc, ss], axis=1)], axis=0
    )


def windows(rows, cols):
    wide = 2 * PATCH
    return [(slice(r, r + PATCH), slice(c, c + wide)) for r in range(0, rows, PATCH) for c in range(0, cols, wide)]


def side_by_side(value):
    return jnp.concatenate([value[i : i + PATCH] for i in range(0, value.shape[0], PATCH)], axis=1)


def forward(pixels, rights_ref, lefts_ref):
    right = dot(pixels, rights_ref[0]) + dot(pixels, rights_ref[1])
    return left_transform(lefts_ref[0], side_by_side(right))


def spectra_kernel(own_ref, near_ref, rights_ref, lefts_ref, own_out, near_out):
    for image, out in ((own_ref, own_out), (near_ref, near_out)):
        pixels = jnp.concatenate([image[window] for window in windows(*image.shape)], axis=0)
        out[...] = forward(pixels, rights_ref, lefts_ref)


def flows_kernel(
    place_ref, far_ref, edge_ref, own_spec, near_spec, rights_ref, lefts_ref, out_ref, stats_ref
):
    wide = 2 * PATCH
    spots = windows(*far_ref.shape)
    blocks = len(spots)
    patches = 2 * blocks
    at_edge = place_ref[5] == 0
    at_even = place_ref[5] % 2 == 0
    pixels = jnp.concatenate(
        [jnp.where(at_edge, edge_ref[spot].astype(F32), far_ref[spot].astype(F32)).astype(BF16) for spot in spots], axis=0
    )
    spec = forward(pixels, rights_ref, lefts_ref)
    products = []
    for block in range(blocks):
        lanes = slice(block * wide, (block + 1) * wide)
        far, near = spec[:, lanes], near_spec[:, lanes]
        operand = cross_operand(jnp.where(at_even, far, near))
        products.append(cross(operand, own_spec[:, lanes]))
        products.append(cross(operand, jnp.where(at_even, near, far)))
    high, low = halves(jnp.concatenate(products, axis=0))
    back = dot(high, rights_ref[2]) + dot(low, rights_ref[2]) + dot(high, rights_ref[3])
    scores = left_transform(lefts_ref[1], side_by_side(back))
    groups = scores.reshape(PATCH // 8, 8, 2 * blocks * wide)
    peak = jnp.max(groups, axis=0)
    total = jnp.zeros_like(peak)
    moment = jnp.zeros_like(peak)
    for group in range(PATCH // 8):
        weight = jnp.exp(groups[group] - peak)
        shift = 8 * group - (PATCH if group >= PATCH // 16 else 0)
        total = total + weight
        moment = moment + float(shift) * weight
    for block in range(blocks):
        for pair in range(2):
            for side in range(2):
                at = (2 * block + pair) * 2 + side
                lanes = slice(at * PATCH, (at + 1) * PATCH)
                slot = pair * patches + 2 * block + side
                stats_ref[0, slot] = peak[:, lanes]
                stats_ref[1, slot] = total[:, lanes]
                stats_ref[2, slot] = moment[:, lanes]
    peak = stats_ref[0]
    best = jnp.max(jnp.max(peak, axis=1, keepdims=True), axis=2, keepdims=True)
    scale = jnp.exp(peak - best)
    total = scale * stats_ref[1]
    within = lax.broadcasted_iota(jnp.int32, peak.shape, 1).astype(F32)
    moment = scale * stats_ref[2] + within * total
    total = jnp.sum(total, axis=1)
    lane = lax.broadcasted_iota(jnp.int32, total.shape, 1)
    signed = jnp.where(lane < HALF, lane, lane - PATCH).astype(F32)
    mass = jnp.sum(total, axis=1, keepdims=True) * STRIDE
    along_rows = jnp.sum(jnp.sum(moment, axis=1), axis=1, keepdims=True) / mass
    along_cols = jnp.sum(total * signed, axis=1, keepdims=True) / mass
    lane = lax.broadcasted_iota(jnp.int32, out_ref.shape, 1)
    near_rows, near_cols = along_rows[:patches], along_cols[:patches]
    out = jnp.where(lane == 0, near_rows, near_cols)
    out = jnp.where(lane == 2, along_rows[patches:] - near_rows, out)
    out_ref[...] = jnp.where(lane == 3, along_cols[patches:] - near_cols, out)


VMEM = pl.BlockSpec(memory_space=pltpu.VMEM)
SMEM = pl.BlockSpec(memory_space=pltpu.SMEM)
PARAMS = pltpu.CompilerParams(vmem_limit_bytes=40 * 2**20)


def spectra(own, near, rights, lefts):
    count = own.shape[0] // PATCH * (own.shape[1] // PATCH)
    spec = jax.ShapeDtypeStruct((PATCH, count * PATCH), F32)
    return pl.pallas_call(
        spectra_kernel,
        out_shape=(spec, spec),
        in_specs=[VMEM] * 4,
        out_specs=(VMEM, VMEM),
        compiler_params=PARAMS,
        cost_estimate=pl.CostEstimate(flops=3 * 10**9, bytes_accessed=3 * 2**20, transcendentals=0),
        name="spectra",
    )(own, near, rights, lefts)


def flows(place, far, edge, own_spec, near_spec, rights, lefts):
    patches = far.shape[0] // PATCH * (far.shape[1] // PATCH)
    return pl.pallas_call(
        flows_kernel,
        out_shape=jax.ShapeDtypeStruct((patches, PATCH), F32),
        in_specs=[SMEM] + [VMEM] * 6,
        out_specs=VMEM,
        scratch_shapes=[pltpu.VMEM((3, 2 * patches, 8, PATCH), F32)],
        compiler_params=PARAMS,
        cost_estimate=pl.CostEstimate(flops=4 * 10**9, bytes_accessed=3 * 2**20, transcendentals=0),
        name="flows",
    )(place, far, edge, own_spec, near_spec, rights, lefts)


def spread_weights(nodes, patches):
    node_pos = (np.arange(nodes) + 0.5) * STRIDE / PATCH - 0.5
    weights = np.maximum(0.0, 1.0 - np.abs(node_pos[:, None] - np.arange(patches)[None, :]))
    return weights / weights.sum(axis=1, keepdims=True)


def ring_nodes(nodes):
    span = np.arange(nodes + 2 * SWEEPS) - SWEEPS
    ring = np.concatenate([span[SWEEPS:], span, span[:SWEEPS]])
    part = np.zeros(len(ring), np.int32)
    part[nodes + SWEEPS : len(ring) - SWEEPS] = 1
    order = np.arange(len(ring)).reshape(PATCH, -1).T.reshape(-1)
    return (ring[order], part[order])


def row_nodes(nodes):
    span = np.arange(nodes + 2 * SWEEPS) - SWEEPS
    return span.reshape(8, -1).T.reshape(-1)


def target_tables(nodes, patches):
    ring, part = ring_nodes(nodes)
    spread = spread_weights(nodes, patches)

    def wide(positions):
        table = np.zeros((len(positions), 3, patches))
        for tile in range(3):
            at = positions - (tile - 1) * nodes
            hit = (at >= 0) & (at < nodes)
            table[hit, tile] = spread[at[hit]]
        return table

    shape = (3, 3, patches, patches)
    rows = wide(row_nodes(nodes))[:, None, :, :, None]
    cols = wide(ring).transpose(1, 2, 0)[:, None, None]
    left = np.broadcast_to(rows, (rows.shape[0],) + shape).reshape(rows.shape[0], -1)
    right = np.broadcast_to(cols, shape + (len(ring),)).reshape(-1, len(ring))
    return (left.astype(BF16), right.astype(np.float32), part[None])


def ring_tables(nodes):
    ring, part = ring_nodes(nodes)
    place = np.arange(3 * nodes)[:, None] - nodes
    into = (place == ring[None]).astype(BF16)
    column = np.arange(2 * nodes)[None]
    out = ((ring[:, None] == column % nodes) & (part[:, None] == column // nodes)).astype(BF16)
    return (into, out, ring.astype(np.int32)[None])


def permuted(value, table):
    result = None
    for piece in range(3):
        part = value.astype(BF16)
        moved = dot(part, table)
        result = moved if result is None else result + moved
        value = value - part.astype(F32)
    return result


def gains_kernel(place_ref, own_ref, even_ref, odd_ref, into_ref, ring_ref, gain_ref, pull_ref, rows_ref):
    strips = gain_ref.shape[0]
    at_even = place_ref[2] == 1
    before = jnp.where(at_even, odd_ref[...], even_ref[...])
    after = jnp.where(at_even, even_ref[...], odd_ref[...])
    weight = permuted(jnp.concatenate([before, own_ref[...], after], axis=1), into_ref[...])
    row_node = lax.broadcasted_iota(jnp.int32, weight.shape, 0) - SWEEPS + place_ref[0]
    col_node = ring_ref[...] + place_ref[1]
    inside = (row_node >= 0) & (row_node < place_ref[3]) & (col_node >= 0) & (col_node < place_ref[4])
    gain = jnp.where(inside, 1.0 / (4.0 + weight), 0.0)
    for value, out in ((gain, gain_ref), (gain * weight, pull_ref)):
        rows_ref[...] = value.reshape(value.shape[0], -1, PATCH).transpose(1, 0, 2)
        for strip in range(strips):
            for tile in range(rows_ref.shape[0]):
                out[strip, :, tile * PATCH : (tile + 1) * PATCH] = rows_ref[tile, pl.ds(strip, 8, strips), :]


def gains(place, own, even, odd, nodes):
    into, _, ring = ring_tables(nodes)
    shape = jax.ShapeDtypeStruct((own.shape[0] // 8, 8, ring.shape[1]), F32)
    return pl.pallas_call(
        gains_kernel,
        out_shape=(shape, shape),
        in_specs=[SMEM] + [VMEM] * 5,
        out_specs=(VMEM, VMEM),
        scratch_shapes=[pltpu.VMEM((ring.shape[1] // PATCH, own.shape[0], PATCH), F32)],
        compiler_params=PARAMS,
        cost_estimate=pl.CostEstimate(flops=10**9, bytes_accessed=2**20, transcendentals=0),
        name="gains",
    )(place, own, even, odd, jnp.asarray(into), jnp.asarray(ring))


def relax_kernel(
    place_ref, own_ref, even_ref, odd_ref, gain_ref, pull_ref, left_ref, right_ref, part_ref, out_table_ref,
    mesh_ref, landing_ref, work_ref, base_ref, rows_ref,
):
    strips, _, lanes = work_ref.shape
    nodes = mesh_ref.shape[2]
    at_even = place_ref[2] == 1
    before = jnp.where(at_even, odd_ref[...], even_ref[...])
    after = jnp.where(at_even, even_ref[...], odd_ref[...])
    sources = jnp.concatenate([before, own_ref[...], after], axis=0)
    spread = jnp.where(part_ref[...] == 1, sources[:, 1:2], sources[:, 0:1]) * right_ref[...]
    target = None
    for piece in range(3):
        part = spread.astype(BF16)
        term = dot(left_ref[...], part)
        target = term if target is None else target + term
        spread = spread - part.astype(F32)
    target = target.reshape(strips, 8, lanes)
    base_ref[...] = pull_ref[...] * target
    work_ref[...] = jnp.where(gain_ref[...] > 0.0, target, 0.0)
    tiles = lanes // PATCH

    def row(strip):
        return [work_ref[strip, :, i * PATCH : (i + 1) * PATCH] for i in range(tiles)]

    def sweep(counter, carry):
        here = row(0)
        above = [pltpu.roll(value, 1, 0) for value in row(strips - 1)]
        around = [pltpu.roll(value, 7, 0) for value in here]
        for strip in range(strips):
            below = row(strip + 1) if strip + 1 < strips else around
            ring = [pltpu.roll(here[-1], 1, 1)] + here + [pltpu.roll(here[0], PATCH - 1, 1)]
            for tile in range(tiles):
                at = (strip, slice(None), slice(tile * PATCH, (tile + 1) * PATCH))
                total = (above[tile] + below[tile]) + (ring[tile] + ring[tile + 2])
                work_ref[at] = gain_ref[at] * total + base_ref[at]
            above, here = here, below
        return carry

    lax.fori_loop(0, SWEEPS, sweep, 0)
    final = permuted(work_ref[...].reshape(strips * 8, lanes), out_table_ref[...])
    for strip in range(strips):
        for part in range(2):
            rows_ref[part, pl.ds(strip, 8, strips), :] = final[8 * strip : 8 * strip + 8, part * nodes : (part + 1) * nodes]
    down = rows_ref[0, SWEEPS : SWEEPS + nodes]
    across = rows_ref[1, SWEEPS : SWEEPS + nodes]
    mesh_ref[0, 0] = down
    mesh_ref[0, 1] = across
    share = 1.0 / nodes
    down_mean = jnp.sum(jnp.transpose(down), axis=0, keepdims=True) * share
    across_mean = jnp.sum(across, axis=0, keepdims=True) * share
    line = lax.broadcasted_iota(jnp.int32, landing_ref.shape, 0)
    ramp = lax.broadcasted_iota(jnp.int32, landing_ref.shape, 1).astype(F32)
    profile = jnp.where(line == 0, down_mean, across_mean)
    landing_ref[...] = jnp.clip(ramp + profile, 0.0, nodes - 1.0)


def relax(place, targets, weights, nodes, patches):
    left, right, part = target_tables(nodes, patches)
    _, out_table, _ = ring_tables(nodes)
    shape = weights[0].shape
    return pl.pallas_call(
        relax_kernel,
        out_shape=(
            jax.ShapeDtypeStruct((1, 2, nodes, nodes), F32),
            jax.ShapeDtypeStruct((8, nodes), F32),
        ),
        in_specs=[SMEM] + [VMEM] * 9,
        out_specs=(VMEM, VMEM),
        scratch_shapes=[pltpu.VMEM(shape, F32)] * 2 + [pltpu.VMEM((2, shape[0] * 8, nodes), F32)],
        compiler_params=PARAMS,
        cost_estimate=pl.CostEstimate(flops=4 * 10**9, bytes_accessed=3 * 2**20, transcendentals=0),
        name="relax",
    )(place, *targets, *weights, *map(jnp.asarray, (left, right, part, out_table)))


def compose_kernel(place_ref, *refs):
    *landing_refs, out_ref = refs
    count = len(landing_refs)
    section = place_ref[5]
    received = [ref[...] for ref in landing_refs]
    nodes = received[0].shape[1]
    ramp = lax.broadcasted_iota(jnp.int32, received[0].shape, 1).astype(F32)
    value = received[0]
    for other in range(count - 2, -1, -1):
        landing = received[0]
        for code in range(1, count):
            landing = jnp.where(section == other ^ code, received[code], landing)
        floor = jnp.minimum(jnp.floor(landing), nodes - 2.0)
        index = floor.astype(jnp.int32)
        share = landing - floor
        below = jnp.take_along_axis(value, index, axis=1)
        above = jnp.take_along_axis(value, index + 1, axis=1)
        value = jnp.where(section > other, (1.0 - share) * below + share * above, value)
    out_ref[0, 0, 0] = (value - ramp)[:2]


def compose(place, landings):
    nodes = landings[0].shape[1]
    return pl.pallas_call(
        compose_kernel,
        out_shape=jax.ShapeDtypeStruct((1, 1, 1, 2, nodes), F32),
        in_specs=[SMEM] + [VMEM] * len(landings),
        out_specs=VMEM,
        name="compose",
    )(place, *landings)


def swap_pairs(value, axis, first, spare):
    count, other = lax.axis_size(axis), lax.axis_size(spare)
    axes = ("gz", "ty", "tx")
    flip = axes.index(axis) > axes.index(spare)

    def place(here, beside):
        return beside * count + here if flip else here * other + beside

    moves = []
    for here in range(count):
        there = ((here + first) ^ 1) - first
        for beside in range(other):
            target = place(there, beside) if 0 <= there < count else place(here, beside ^ 1)
            moves.append((place(here, beside), target))
    return lax.ppermute(value, (spare, axis) if flip else (axis, spare), moves)


def rows_beside(value):
    count = lax.axis_size("ty")
    if count == 2:
        other = swap_pairs(value, "ty", 0, "gz")
        return (other, other)
    even = swap_pairs(value, "ty", 0, "gz")
    odd = swap_pairs(value, "ty", 1, "gz")
    at_even = lax.axis_index("ty") % 2 == 0
    return (jnp.where(at_even, odd, even), jnp.where(at_even, even, odd))


def ring_rows(value):
    up, down = rows_beside(value)
    return jnp.concatenate([up, value, down], axis=0)


def to_next(value, turn):
    count, rows = lax.axis_size("gz"), lax.axis_size("ty")
    if not turn:
        return lax.ppermute(value, "gz", [(i, (i + 1) % count) for i in range(count)])
    moves = [(i * rows + j, (i + 1) % count * rows + (j ^ 1)) for i in range(count) for j in range(rows)]
    return lax.ppermute(value, ("gz", "ty"), moves)


def local(images, boundary, anchor):
    nodes = anchor.shape[1]
    own = images[0]
    patches = own.shape[0] // PATCH
    section, ty, tx = (lax.axis_index(axis) for axis in ("gz", "ty", "tx"))
    sections, n_ty, n_tx = (lax.axis_size(axis) for axis in ("gz", "ty", "tx"))
    place = jnp.stack([ty * nodes, tx * nodes, 1 - tx % 2, n_ty * nodes, n_tx * nodes, section]).astype(jnp.int32)
    rights, lefts = map(jnp.asarray, transform_tables())
    far = swap_pairs(own, "gz", 1, "ty")
    near = swap_pairs(own, "gz", 0, "ty")
    own_spec, near_spec = spectra(own, near, rights, lefts)
    up, down = rows_beside(anchor[0])
    rows = jnp.concatenate([up[nodes - SWEEPS :], anchor[0], down[:SWEEPS]], axis=0)
    weights = gains(place, rows, swap_pairs(rows, "tx", 0, "gz"), swap_pairs(rows, "tx", 1, "gz"), nodes)
    far, weights = lax.optimization_barrier((far, weights))
    flow = flows(place, far, boundary, own_spec, near_spec, rights, lefts)
    around = ring_rows(flow)
    before = to_next(flow, 0)
    if n_ty == 2:
        beside = to_next(flow, 1)
        before = jnp.concatenate([beside, before, beside], axis=0)
    else:
        before = ring_rows(before)
    column = jnp.where(section <= 1, around[:, 0:2], 0.5 * (around[:, 0:2] + before[:, 2:4]))
    column = jnp.pad(column, ((0, 0), (0, PATCH - 2)))
    targets = (column, swap_pairs(column, "tx", 0, "gz"), swap_pairs(column, "tx", 1, "gz"))
    mesh, landing = relax(place, targets, weights, nodes, patches)
    landings = [landing]
    for code in range(1, sections):
        landings.append(lax.ppermute(landing, "gz", [(i, i ^ code) for i in range(sections)]))
    drift = compose(place, landings)
    return (mesh, drift)


def solution(mesh):
    return jax.shard_map(
        local,
        mesh=mesh,
        in_specs=(P("gz", "ty", "tx"), P("ty", "tx"), P("gz", "ty", "tx")),
        out_specs=(P("gz", None, "ty", "tx"), P("gz", "ty", "tx", None, None)),
        check_vma=False,
    )
```

```python
import math

import jax
import jax.numpy as jnp
import numpy as np
from jax import lax
from jax.experimental import pallas as pl
from jax.experimental.pallas import tpu as pltpu
from jax.sharding import PartitionSpec as P

PATCH = 128
STRIDE = 4
SWEEPS = 32
HALF = PATCH // 2
BF16 = jnp.bfloat16
F32 = jnp.float32


def split_table(table):
    high = table.astype(BF16)
    low = (table - high.astype(np.float64)).astype(BF16)
    return (high, low)


def transform_tables():
    counter = np.arange(PATCH)
    phase = (counter[:, None] * counter[None, :] % PATCH) * (2.0 * math.pi / PATCH)
    basis = np.concatenate([np.cos(phase[:HALF]), np.sin(phase[:HALF])])
    basis[HALF] = np.cos(phase[HALF])
    gains = np.full(PATCH, 2.0)
    gains[0] = gains[HALF] = 1.0
    inverse = basis.T * gains / PATCH
    forward_pair = np.zeros((2, PATCH, 2, 2, HALF))
    inverse_pair = np.zeros((2, 2, HALF, 2, PATCH))
    for side in range(2):
        forward_pair[side, :, :, side] = basis.T.reshape(PATCH, 2, HALF)
        inverse_pair[:, side, :, side] = inverse.T.reshape(2, HALF, PATCH)
    forward_pair = forward_pair.reshape(2 * PATCH, 2 * PATCH)
    inverse_pair = inverse_pair.reshape(2 * PATCH, 2 * PATCH)
    right_high, right_low = split_table(forward_pair)
    back_high, back_low = split_table(inverse_pair)
    left_high, left_low = split_table(basis)
    undo_high, undo_low = split_table(inverse / PATCH)
    rights = np.stack([right_high, right_low, back_high, back_low])
    lefts = np.stack(
        [
            np.concatenate([left_high, left_high, left_low], axis=1),
            np.concatenate([undo_high, undo_high, undo_low], axis=1),
        ]
    )
    return (rights, lefts)


def halves(value):
    high = value.astype(BF16)
    return (high, (value - high.astype(F32)).astype(BF16))


def dot(left, right):
    return jnp.dot(left, right, preferred_element_type=F32)


def left_transform(table, value):
    high, low = halves(value)
    return dot(table, jnp.concatenate([high, low, high], axis=0))


def quarters(spec):
    return (
        (spec[:HALF, :PATCH], spec[:HALF, PATCH:]),
        (spec[HALF:, :PATCH], spec[HALF:, PATCH:]),
    )


def cross_operand(spec):
    (cc, cs), (sc, ss) = quarters(spec)
    first_row = lax.broadcasted_iota(jnp.int32, (HALF, PATCH), 0) == 0
    first_lane = lax.broadcasted_iota(jnp.int32, (HALF, PATCH), 1) % HALF == 0

    def lanes(cosine, sine):
        return (cosine, jnp.where(first_lane, sine, cosine), jnp.where(first_lane, 0.0, sine))

    return (
        lanes(cc, cs),
        lanes(jnp.where(first_row, sc, cc), jnp.where(first_row, ss, cs)),
        lanes(jnp.where(first_row, 0.0, sc), jnp.where(first_row, 0.0, ss)),
    )


def cross(operand, spec):
    (row_c, row_d, row_s) = operand
    (bc, bs) = quarters(spec)

    def cosine(a, b):
        return a[0] * b[0] + a[2] * b[1]

    def sine(a, b):
        return a[1] * b[1] - a[2] * b[0]

    cc = cosine(row_c, bc) + cosine(row_s, bs)
    cs = sine(row_c, bc) + sine(row_s, bs)
    sc = cosine(row_d, bs) - cosine(row_s, bc)
    ss = sine(row_d, bs) - sine(row_s, bc)
    return jnp.concatenate(
        [jnp.concatenate([cc, cs], axis=1), jnp.concatenate([sc, ss], axis=1)], axis=0
    )


def windows(rows, cols):
    wide = 2 * PATCH
    return [(slice(r, r + PATCH), slice(c, c + wide)) for r in range(0, rows, PATCH) for c in range(0, cols, wide)]


def side_by_side(value):
    return jnp.concatenate([value[i : i + PATCH] for i in range(0, value.shape[0], PATCH)], axis=1)


def forward(pixels, rights_ref, lefts_ref):
    right = dot(pixels, rights_ref[0]) + dot(pixels, rights_ref[1])
    return left_transform(lefts_ref[0], side_by_side(right))


def spectra_kernel(own_ref, near_ref, rights_ref, lefts_ref, own_out, near_out):
    for image, out in ((own_ref, own_out), (near_ref, near_out)):
        pixels = jnp.concatenate([image[window] for window in windows(*image.shape)], axis=0)
        out[...] = forward(pixels, rights_ref, lefts_ref)


def flows_kernel(
    far_ref, edge_ref, own_spec, near_spec, rights_ref, lefts_ref, out_ref, stats_ref
):
    wide = 2 * PATCH
    spots = windows(*far_ref.shape)
    blocks = len(spots)
    patches = 2 * blocks
    at_edge = lax.axis_index("gz") == 0
    at_even = lax.axis_index("gz") % 2 == 0
    pixels = jnp.concatenate(
        [jnp.where(at_edge, edge_ref[spot].astype(F32), far_ref[spot].astype(F32)).astype(BF16) for spot in spots], axis=0
    )
    spec = forward(pixels, rights_ref, lefts_ref)
    products = []
    for block in range(blocks):
        lanes = slice(block * wide, (block + 1) * wide)
        far, near = spec[:, lanes], near_spec[:, lanes]
        operand = cross_operand(jnp.where(at_even, far, near))
        products.append(cross(operand, own_spec[:, lanes]))
        products.append(cross(operand, jnp.where(at_even, near, far)))
    high, low = halves(jnp.concatenate(products, axis=0))
    back = dot(high, rights_ref[2]) + dot(low, rights_ref[2]) + dot(high, rights_ref[3])
    scores = left_transform(lefts_ref[1], side_by_side(back))
    groups = scores.reshape(PATCH // 8, 8, 2 * blocks * wide)
    peak = jnp.max(groups, axis=0)
    total = jnp.zeros_like(peak)
    moment = jnp.zeros_like(peak)
    for group in range(PATCH // 8):
        weight = jnp.exp(groups[group] - peak)
        shift = 8 * group - (PATCH if group >= PATCH // 16 else 0)
        total = total + weight
        moment = moment + float(shift) * weight
    for block in range(blocks):
        for pair in range(2):
            for side in range(2):
                at = (2 * block + pair) * 2 + side
                lanes = slice(at * PATCH, (at + 1) * PATCH)
                slot = pair * patches + 2 * block + side
                stats_ref[0, slot] = peak[:, lanes]
                stats_ref[1, slot] = total[:, lanes]
                stats_ref[2, slot] = moment[:, lanes]
    peak = stats_ref[0]
    best = jnp.max(jnp.max(peak, axis=1, keepdims=True), axis=2, keepdims=True)
    scale = jnp.exp(peak - best)
    total = scale * stats_ref[1]
    within = lax.broadcasted_iota(jnp.int32, peak.shape, 1).astype(F32)
    moment = scale * stats_ref[2] + within * total
    total = jnp.sum(total, axis=1)
    lane = lax.broadcasted_iota(jnp.int32, total.shape, 1)
    signed = jnp.where(lane < HALF, lane, lane - PATCH).astype(F32)
    mass = jnp.sum(total, axis=1, keepdims=True) * STRIDE
    along_rows = jnp.sum(jnp.sum(moment, axis=1), axis=1, keepdims=True) / mass
    along_cols = jnp.sum(total * signed, axis=1, keepdims=True) / mass
    values = (
        along_rows[:patches],
        along_cols[:patches],
        along_rows[patches:] - along_rows[:patches],
        along_cols[patches:] - along_cols[:patches],
    )
    lane = lax.broadcasted_iota(jnp.int32, (patches, PATCH), 1)
    patch = lax.broadcasted_iota(jnp.int32, (patches, PATCH), 0)
    lines = []
    for first, second in (values[:2], values[2:]):
        line = jnp.where(lane == patch, first, jnp.where(lane == patches + patch, second, 0.0))
        lines.append(jnp.sum(line, axis=0, keepdims=True))
    line = lax.broadcasted_iota(jnp.int32, out_ref.shape, 0)
    out_ref[...] = jnp.where(line == 0, lines[0], lines[1])


VMEM = pl.BlockSpec(memory_space=pltpu.VMEM)
PARAMS = pltpu.CompilerParams(vmem_limit_bytes=40 * 2**20)


def spectra(own, near, rights, lefts):
    count = own.shape[0] // PATCH * (own.shape[1] // PATCH)
    spec = jax.ShapeDtypeStruct((PATCH, count * PATCH), F32)
    return pl.pallas_call(
        spectra_kernel,
        out_shape=(spec, spec),
        in_specs=[VMEM] * 4,
        out_specs=(VMEM, VMEM),
        compiler_params=PARAMS,
        cost_estimate=pl.CostEstimate(flops=3 * 10**9, bytes_accessed=3 * 2**20, transcendentals=0),
        name="spectra",
    )(own, near, rights, lefts)


def flows(far, edge, own_spec, near_spec, rights, lefts):
    patches = far.shape[0] // PATCH * (far.shape[1] // PATCH)
    return pl.pallas_call(
        flows_kernel,
        out_shape=jax.ShapeDtypeStruct((8, PATCH), F32),
        in_specs=[VMEM] * 6,
        out_specs=VMEM,
        scratch_shapes=[pltpu.VMEM((3, 2 * patches, 8, PATCH), F32)],
        compiler_params=PARAMS,
        cost_estimate=pl.CostEstimate(flops=4 * 10**9, bytes_accessed=3 * 2**20, transcendentals=0),
        name="flows",
    )(far, edge, own_spec, near_spec, rights, lefts)


def spread_weights(nodes, patches):
    node_pos = (np.arange(nodes) + 0.5) * STRIDE / PATCH - 0.5
    weights = np.maximum(0.0, 1.0 - np.abs(node_pos[:, None] - np.arange(patches)[None, :]))
    return weights / weights.sum(axis=1, keepdims=True)


def ring_nodes(nodes):
    span = np.arange(nodes + 2 * SWEEPS) - SWEEPS
    ring = np.concatenate([span[SWEEPS:], span, span[:SWEEPS]])
    part = np.zeros(len(ring), np.int32)
    part[nodes + SWEEPS : len(ring) - SWEEPS] = 1
    order = np.arange(len(ring)).reshape(PATCH, -1).T.reshape(-1)
    return (ring[order], part[order])


def row_nodes(nodes):
    span = np.arange(nodes + 2 * SWEEPS) - SWEEPS
    return span.reshape(8, -1).T.reshape(-1)


def target_tables(nodes, patches):
    ring, part = ring_nodes(nodes)
    spread = spread_weights(nodes, patches)

    def wide(positions):
        table = np.zeros((len(positions), 3, patches))
        for tile in range(3):
            at = positions - (tile - 1) * nodes
            hit = (at >= 0) & (at < nodes)
            table[hit, tile] = spread[at[hit]]
        return table

    shape = (3, 3, patches, patches)
    rows = wide(row_nodes(nodes))[:, None, :, :, None]
    cols = wide(ring).transpose(1, 2, 0)[:, None, None]
    left = np.broadcast_to(rows, (rows.shape[0],) + shape).reshape(rows.shape[0], -1)
    right = np.broadcast_to(cols, shape + (len(ring),)).reshape(-1, len(ring))
    return (left.astype(BF16), right.astype(np.float32), part[None])


def ring_tables(nodes):
    ring, part = ring_nodes(nodes)
    place = np.arange(3 * nodes)[:, None] - nodes
    into = (place == ring[None]).astype(BF16)
    column = np.arange(2 * nodes)[None]
    out = ((ring[:, None] == column % nodes) & (part[:, None] == column // nodes)).astype(BF16)
    return (into, out, ring.astype(np.int32)[None])


def permuted(value, table):
    result = None
    for piece in range(3):
        part = value.astype(BF16)
        moved = dot(part, table)
        result = moved if result is None else result + moved
        value = value - part.astype(F32)
    return result


def tiles_beside(even_ref, odd_ref):
    at_even = lax.axis_index("tx") % 2 == 0
    even, odd = even_ref[...], odd_ref[...]
    return (jnp.where(at_even, odd, even), jnp.where(at_even, even, odd))


def gains_kernel(own_ref, even_ref, odd_ref, into_ref, ring_ref, gain_ref, pull_ref, rows_ref):
    strips = gain_ref.shape[0]
    nodes = own_ref.shape[1]
    before, after = tiles_beside(even_ref, odd_ref)
    weight = permuted(jnp.concatenate([before, own_ref[...], after], axis=1), into_ref[...])
    row_node = lax.broadcasted_iota(jnp.int32, weight.shape, 0) - SWEEPS
    row_node = row_node + lax.axis_index("ty") * nodes
    col_node = ring_ref[...] + lax.axis_index("tx") * nodes
    inside = (row_node >= 0) & (row_node < lax.axis_size("ty") * nodes)
    inside = inside & (col_node >= 0) & (col_node < lax.axis_size("tx") * nodes)
    gain = jnp.where(inside, 1.0 / (4.0 + weight), 0.0)
    for value, out in ((gain, gain_ref), (gain * weight, pull_ref)):
        rows_ref[...] = value.reshape(value.shape[0], -1, PATCH).transpose(1, 0, 2)
        for strip in range(strips):
            for tile in range(rows_ref.shape[0]):
                out[strip, :, tile * PATCH : (tile + 1) * PATCH] = rows_ref[tile, pl.ds(strip, 8, strips), :]


def gains(own, even, odd, nodes):
    into, _, ring = ring_tables(nodes)
    shape = jax.ShapeDtypeStruct((own.shape[0] // 8, 8, ring.shape[1]), F32)
    return pl.pallas_call(
        gains_kernel,
        out_shape=(shape, shape),
        in_specs=[VMEM] * 5,
        out_specs=(VMEM, VMEM),
        scratch_shapes=[pltpu.VMEM((ring.shape[1] // PATCH, own.shape[0], PATCH), F32)],
        compiler_params=PARAMS,
        cost_estimate=pl.CostEstimate(flops=10**9, bytes_accessed=2**20, transcendentals=0),
        name="gains",
    )(own, even, odd, jnp.asarray(into), jnp.asarray(ring))


def relax_kernel(
    own_ref, even_ref, odd_ref, gain_ref, pull_ref, left_ref, right_ref, part_ref, out_table_ref,
    mesh_ref, landing_ref, work_ref, base_ref, rows_ref,
):
    strips, _, lanes = work_ref.shape
    nodes = mesh_ref.shape[2]
    patches = left_ref.shape[1] // 9
    before, after = tiles_beside(even_ref, odd_ref)
    rows = [before[:3], own_ref[:3], after[:3]]
    rows.append(jnp.zeros((PATCH - 9, PATCH), F32))
    columns = jnp.transpose(jnp.concatenate(rows, axis=0))

    def sources(part):
        lines = slice(part * patches, (part + 1) * patches)
        return jnp.concatenate([columns[lines, i : i + 1] for i in range(9)], axis=0)

    spread = jnp.where(part_ref[...] == 1, sources(1), sources(0)) * right_ref[...]
    target = None
    for piece in range(3):
        part = spread.astype(BF16)
        term = dot(left_ref[...], part)
        target = term if target is None else target + term
        spread = spread - part.astype(F32)
    target = target.reshape(strips, 8, lanes)
    base_ref[...] = pull_ref[...] * target
    work_ref[...] = jnp.where(gain_ref[...] > 0.0, target, 0.0)
    tiles = lanes // PATCH

    def row(strip):
        return [work_ref[strip, :, i * PATCH : (i + 1) * PATCH] for i in range(tiles)]

    def sweep(counter, carry):
        here = row(0)
        above = [pltpu.roll(value, 1, 0) for value in row(strips - 1)]
        around = [pltpu.roll(value, 7, 0) for value in here]
        for strip in range(strips):
            below = row(strip + 1) if strip + 1 < strips else around
            ring = [pltpu.roll(here[-1], 1, 1)] + here + [pltpu.roll(here[0], PATCH - 1, 1)]
            for tile in range(tiles):
                at = (strip, slice(None), slice(tile * PATCH, (tile + 1) * PATCH))
                total = (above[tile] + below[tile]) + (ring[tile] + ring[tile + 2])
                work_ref[at] = gain_ref[at] * total + base_ref[at]
            above, here = here, below
        return carry

    lax.fori_loop(0, SWEEPS, sweep, 0, unroll=8)
    final = permuted(work_ref[...].reshape(strips * 8, lanes), out_table_ref[...])
    for strip in range(strips):
        for part in range(2):
            rows_ref[part, pl.ds(strip, 8, strips), :] = final[8 * strip : 8 * strip + 8, part * nodes : (part + 1) * nodes]
    down = rows_ref[0, SWEEPS : SWEEPS + nodes]
    across = rows_ref[1, SWEEPS : SWEEPS + nodes]
    mesh_ref[0, 0] = down
    mesh_ref[0, 1] = across
    share = 1.0 / nodes
    down_mean = jnp.sum(jnp.transpose(down), axis=0, keepdims=True) * share
    across_mean = jnp.sum(across, axis=0, keepdims=True) * share
    line = lax.broadcasted_iota(jnp.int32, landing_ref.shape, 0)
    ramp = lax.broadcasted_iota(jnp.int32, landing_ref.shape, 1).astype(F32)
    profile = jnp.where(line == 0, down_mean, across_mean)
    landing_ref[...] = jnp.clip(ramp + profile, 0.0, nodes - 1.0)


def relax(targets, weights, nodes, patches):
    left, right, part = target_tables(nodes, patches)
    _, out_table, _ = ring_tables(nodes)
    shape = weights[0].shape
    return pl.pallas_call(
        relax_kernel,
        out_shape=(
            jax.ShapeDtypeStruct((1, 2, nodes, nodes), F32),
            jax.ShapeDtypeStruct((8, nodes), F32),
        ),
        in_specs=[VMEM] * 9,
        out_specs=(VMEM, VMEM),
        scratch_shapes=[pltpu.VMEM(shape, F32)] * 2 + [pltpu.VMEM((2, shape[0] * 8, nodes), F32)],
        compiler_params=PARAMS,
        cost_estimate=pl.CostEstimate(flops=4 * 10**9, bytes_accessed=3 * 2**20, transcendentals=0),
        name="relax",
    )(*targets, *weights, *map(jnp.asarray, (left, right, part, out_table)))


def compose_kernel(*refs):
    *landing_refs, out_ref = refs
    count = len(landing_refs)
    section = lax.axis_index("gz")
    received = [ref[...] for ref in landing_refs]
    nodes = received[0].shape[1]
    ramp = lax.broadcasted_iota(jnp.int32, received[0].shape, 1).astype(F32)
    value = received[0]
    for other in range(count - 2, -1, -1):
        landing = received[0]
        for code in range(1, count):
            landing = jnp.where(section == other ^ code, received[code], landing)
        floor = jnp.minimum(jnp.floor(landing), nodes - 2.0)
        index = floor.astype(jnp.int32)
        share = landing - floor
        below = jnp.take_along_axis(value, index, axis=1)
        above = jnp.take_along_axis(value, index + 1, axis=1)
        value = jnp.where(section > other, (1.0 - share) * below + share * above, value)
    out_ref[0, 0, 0] = (value - ramp)[:2]


def compose(landings):
    nodes = landings[0].shape[1]
    return pl.pallas_call(
        compose_kernel,
        out_shape=jax.ShapeDtypeStruct((1, 1, 1, 2, nodes), F32),
        in_specs=[VMEM] * len(landings),
        out_specs=VMEM,
        compiler_params=pltpu.CompilerParams(vmem_limit_bytes=2**20),
        name="compose",
    )(*landings)


def swap_pairs(value, axis, first, spare):
    count, other = lax.axis_size(axis), lax.axis_size(spare)
    axes = ("gz", "ty", "tx")
    flip = axes.index(axis) > axes.index(spare)

    def place(here, beside):
        return beside * count + here if flip else here * other + beside

    moves = []
    for here in range(count):
        there = ((here + first) ^ 1) - first
        for beside in range(other):
            target = place(there, beside) if 0 <= there < count else place(here, beside ^ 1)
            moves.append((place(here, beside), target))
    return lax.ppermute(value, (spare, axis) if flip else (axis, spare), moves)


def rows_beside(value):
    count = lax.axis_size("ty")
    if count == 2:
        other = swap_pairs(value, "ty", 0, "gz")
        return (other, other)
    even = swap_pairs(value, "ty", 0, "gz")
    odd = swap_pairs(value, "ty", 1, "gz")
    at_even = lax.axis_index("ty") % 2 == 0
    return (jnp.where(at_even, odd, even), jnp.where(at_even, even, odd))


def to_next(value, turn):
    count, rows = lax.axis_size("gz"), lax.axis_size("ty")
    if not turn:
        return lax.ppermute(value, "gz", [(i, (i + 1) % count) for i in range(count)])
    moves = [(i * rows + j, (i + 1) % count * rows + (j ^ 1)) for i in range(count) for j in range(rows)]
    return lax.ppermute(value, ("gz", "ty"), moves)


def patch_targets(flow):
    first = lax.axis_index("gz") <= 1
    before = to_next(flow, 0)

    def target(near, earlier):
        return jnp.where(first, near[0:1], 0.5 * (near[0:1] + earlier[1:2]))

    if lax.axis_size("ty") == 2:
        beside = target(rows_beside(flow)[0], to_next(flow, 1))
        lines = [beside, target(flow, before), beside]
    else:
        (up, down), (up_before, down_before) = rows_beside(flow), rows_beside(before)
        lines = [target(up, up_before), target(flow, before), target(down, down_before)]
    return jnp.concatenate(lines + [jnp.zeros((5, flow.shape[1]), F32)], axis=0)


def local(images, boundary, anchor):
    nodes = anchor.shape[1]
    own = images[0]
    patches = own.shape[0] // PATCH
    sections = lax.axis_size("gz")
    rights, lefts = map(jnp.asarray, transform_tables())
    far = swap_pairs(own, "gz", 1, "ty")
    near = swap_pairs(own, "gz", 0, "ty")
    up, down = rows_beside(anchor[0])
    rows = jnp.concatenate([up[nodes - SWEEPS :], anchor[0], down[:SWEEPS]], axis=0)
    near, rows = lax.optimization_barrier((near, rows))
    specs = spectra(own, near, rights, lefts)
    weights = gains(rows, swap_pairs(rows, "tx", 0, "gz"), swap_pairs(rows, "tx", 1, "gz"), nodes)
    far, weights, specs = lax.optimization_barrier((far, weights, specs))
    flow = flows(far, boundary, *specs, rights, lefts)
    line = patch_targets(flow)
    targets = (line, swap_pairs(line, "tx", 0, "gz"), swap_pairs(line, "tx", 1, "gz"))
    mesh, landing = relax(targets, weights, nodes, patches)
    landings = [landing]
    for code in range(1, sections):
        landings.append(lax.ppermute(landing, "gz", [(i, i ^ code) for i in range(sections)]))
    drift = compose(landings)
    return (mesh, drift)


def solution(mesh):
    return jax.shard_map(
        local,
        mesh=mesh,
        in_specs=(P("gz", "ty", "tx"), P("ty", "tx"), P("gz", "ty", "tx")),
        out_specs=(P("gz", None, "ty", "tx"), P("gz", "ty", "tx", None, None)),
        check_vma=False,
    )
```

```python
import math

import jax
import jax.numpy as jnp
import numpy as np
from jax import lax
from jax.experimental import pallas as pl
from jax.experimental.pallas import tpu as pltpu
from jax.sharding import PartitionSpec as P

PATCH = 128
STRIDE = 4
SWEEPS = 32
HALF = PATCH // 2
BF16 = jnp.bfloat16
F32 = jnp.float32


def split_table(table):
    high = table.astype(BF16)
    low = (table - high.astype(np.float64)).astype(BF16)
    return (high, low)


def transform_tables():
    counter = np.arange(PATCH)
    phase = (counter[:, None] * counter[None, :] % PATCH) * (2.0 * math.pi / PATCH)
    basis = np.concatenate([np.cos(phase[:HALF]), np.sin(phase[:HALF])])
    basis[HALF] = np.cos(phase[HALF])
    gains = np.full(PATCH, 2.0)
    gains[0] = gains[HALF] = 1.0
    inverse = basis.T * gains / PATCH
    tables = [part for table in (basis.T, inverse.T, basis, inverse / PATCH) for part in split_table(table)]
    return jnp.asarray(np.stack(tables))


def pair_tables(tables_ref):
    lower = lax.broadcasted_iota(jnp.int32, (PATCH, PATCH), 1) < HALF
    forwards, inverses = [], []
    for index in range(2):
        table = tables_ref[index].astype(F32)
        turned = pltpu.roll(table, HALF, 1)
        first = jnp.concatenate([jnp.where(lower, table, 0.0), jnp.where(lower, turned, 0.0)], axis=1)
        second = jnp.concatenate([jnp.where(lower, 0.0, turned), jnp.where(lower, 0.0, table)], axis=1)
        forwards.append(jnp.concatenate([first, second], axis=0).astype(BF16))
        table = tables_ref[2 + index]
        empty = jnp.zeros((HALF, PATCH), BF16)
        rows = []
        for part in (table[:HALF], table[HALF:]):
            rows += [jnp.concatenate([part, empty], axis=1), jnp.concatenate([empty, part], axis=1)]
        inverses.append(jnp.concatenate(rows, axis=0))
    return forwards + inverses


def halves(value):
    high = value.astype(BF16)
    return (high, (value - high.astype(F32)).astype(BF16))


def dot(left, right):
    return jnp.dot(left, right, preferred_element_type=F32)


def left_transform(table_high, table_low, value):
    high, low = halves(value)
    table = jnp.concatenate([table_high, table_high, table_low], axis=1)
    return dot(table, jnp.concatenate([high, low, high], axis=0))


def quarters(spec):
    return (
        (spec[:HALF, :PATCH], spec[:HALF, PATCH:]),
        (spec[HALF:, :PATCH], spec[HALF:, PATCH:]),
    )


def cross_operand(spec):
    (cc, cs), (sc, ss) = quarters(spec)
    first_row = lax.broadcasted_iota(jnp.int32, (HALF, PATCH), 0) == 0
    first_lane = lax.broadcasted_iota(jnp.int32, (HALF, PATCH), 1) % HALF == 0

    def lanes(cosine, sine):
        return (cosine, jnp.where(first_lane, sine, cosine), jnp.where(first_lane, 0.0, sine))

    return (
        lanes(cc, cs),
        lanes(jnp.where(first_row, sc, cc), jnp.where(first_row, ss, cs)),
        lanes(jnp.where(first_row, 0.0, sc), jnp.where(first_row, 0.0, ss)),
    )


def cross(operand, spec):
    (row_c, row_d, row_s) = operand
    (bc, bs) = quarters(spec)

    def cosine(a, b):
        return a[0] * b[0] + a[2] * b[1]

    def sine(a, b):
        return a[1] * b[1] - a[2] * b[0]

    cc = cosine(row_c, bc) + cosine(row_s, bs)
    cs = sine(row_c, bc) + sine(row_s, bs)
    sc = cosine(row_d, bs) - cosine(row_s, bc)
    ss = sine(row_d, bs) - sine(row_s, bc)
    return jnp.concatenate(
        [jnp.concatenate([cc, cs], axis=1), jnp.concatenate([sc, ss], axis=1)], axis=0
    )


def windows(rows, cols):
    wide = 2 * PATCH
    return [(slice(r, r + PATCH), slice(c, c + wide)) for r in range(0, rows, PATCH) for c in range(0, cols, wide)]


def side_by_side(value):
    return jnp.concatenate([value[i : i + PATCH] for i in range(0, value.shape[0], PATCH)], axis=1)


def forward(pixels, pairs, tables_ref):
    right = dot(pixels, pairs[0]) + dot(pixels, pairs[1])
    return left_transform(tables_ref[4], tables_ref[5], side_by_side(right))


def image_spectra(image_ref, pairs, tables_ref):
    pixels = jnp.concatenate([image_ref[window] for window in windows(*image_ref.shape)], axis=0)
    return forward(pixels, pairs, tables_ref)


def near_kernel(image_ref, tables_ref, spec_out, pairs_out):
    pairs = pair_tables(tables_ref)
    for index, pair in enumerate(pairs):
        pairs_out[index] = pair
    spec_out[...] = image_spectra(image_ref, pairs, tables_ref)


def own_kernel(image_ref, pairs_ref, tables_ref, spec_out):
    spec_out[...] = image_spectra(image_ref, pairs_ref, tables_ref)


def rows_kernel(up_ref, own_ref, down_ref, out_ref):
    nodes = own_ref.shape[0]
    out_ref[:SWEEPS] = up_ref[nodes - SWEEPS :]
    out_ref[SWEEPS : SWEEPS + nodes] = own_ref[...]
    out_ref[SWEEPS + nodes :] = down_ref[:SWEEPS]


def flows_kernel(
    far_ref, edge_ref, own_spec, near_spec, rights_ref, tables_ref, out_ref, stats_ref
):
    wide = 2 * PATCH
    spots = windows(*far_ref.shape)
    blocks = len(spots)
    patches = 2 * blocks
    at_edge = lax.axis_index("gz") == 0
    at_even = lax.axis_index("gz") % 2 == 0
    pixels = jnp.concatenate(
        [jnp.where(at_edge, edge_ref[spot].astype(F32), far_ref[spot].astype(F32)).astype(BF16) for spot in spots], axis=0
    )
    spec = forward(pixels, rights_ref, tables_ref)
    products = []
    for block in range(blocks):
        lanes = slice(block * wide, (block + 1) * wide)
        far, near = spec[:, lanes], near_spec[:, lanes]
        operand = cross_operand(jnp.where(at_even, far, near))
        products.append(cross(operand, own_spec[:, lanes]))
        products.append(cross(operand, jnp.where(at_even, near, far)))
    high, low = halves(jnp.concatenate(products, axis=0))
    back = dot(high, rights_ref[2]) + dot(low, rights_ref[2]) + dot(high, rights_ref[3])
    scores = left_transform(tables_ref[6], tables_ref[7], side_by_side(back))
    groups = scores.reshape(PATCH // 8, 8, 2 * blocks * wide)
    peak = jnp.max(groups, axis=0)
    total = jnp.zeros_like(peak)
    moment = jnp.zeros_like(peak)
    for group in range(PATCH // 8):
        weight = jnp.exp(groups[group] - peak)
        shift = 8 * group - (PATCH if group >= PATCH // 16 else 0)
        total = total + weight
        moment = moment + float(shift) * weight
    for block in range(blocks):
        for pair in range(2):
            for side in range(2):
                at = (2 * block + pair) * 2 + side
                lanes = slice(at * PATCH, (at + 1) * PATCH)
                slot = pair * patches + 2 * block + side
                stats_ref[0, slot] = peak[:, lanes]
                stats_ref[1, slot] = total[:, lanes]
                stats_ref[2, slot] = moment[:, lanes]
    peak = stats_ref[0]
    best = jnp.max(jnp.max(peak, axis=1, keepdims=True), axis=2, keepdims=True)
    scale = jnp.exp(peak - best)
    total = scale * stats_ref[1]
    within = lax.broadcasted_iota(jnp.int32, peak.shape, 1).astype(F32)
    moment = scale * stats_ref[2] + within * total
    total = jnp.sum(total, axis=1)
    lane = lax.broadcasted_iota(jnp.int32, total.shape, 1)
    signed = jnp.where(lane < HALF, lane, lane - PATCH).astype(F32)
    mass = jnp.sum(total, axis=1, keepdims=True) * STRIDE
    along_rows = jnp.sum(jnp.sum(moment, axis=1), axis=1, keepdims=True) / mass
    along_cols = jnp.sum(total * signed, axis=1, keepdims=True) / mass
    values = (
        along_rows[:patches],
        along_cols[:patches],
        along_rows[patches:] - along_rows[:patches],
        along_cols[patches:] - along_cols[:patches],
    )
    lane = lax.broadcasted_iota(jnp.int32, (patches, PATCH), 1)
    patch = lax.broadcasted_iota(jnp.int32, (patches, PATCH), 0)
    lines = []
    for first, second in (values[:2], values[2:]):
        line = jnp.where(lane == patch, first, jnp.where(lane == patches + patch, second, 0.0))
        lines.append(jnp.sum(line, axis=0, keepdims=True))
    line = lax.broadcasted_iota(jnp.int32, out_ref.shape, 0)
    out_ref[...] = jnp.where(line == 0, lines[0], lines[1])


VMEM = pl.BlockSpec(memory_space=pltpu.VMEM)
PARAMS = pltpu.CompilerParams(vmem_limit_bytes=40 * 2**20)


def spec_shape(image):
    return jax.ShapeDtypeStruct((PATCH, image.shape[0] // PATCH * image.shape[1]), F32)


def near_spectra(near, tables):
    pairs = jax.ShapeDtypeStruct((4, 2 * PATCH, 2 * PATCH), BF16)
    return pl.pallas_call(
        near_kernel,
        out_shape=(spec_shape(near), pairs),
        in_specs=[VMEM] * 2,
        out_specs=(VMEM, VMEM),
        compiler_params=PARAMS,
        cost_estimate=pl.CostEstimate(flops=2 * 10**9, bytes_accessed=2 * 2**20, transcendentals=0),
        name="near_spectra",
    )(near, tables)


def own_spectra(own, pairs, tables):
    return pl.pallas_call(
        own_kernel,
        out_shape=spec_shape(own),
        in_specs=[VMEM] * 3,
        out_specs=VMEM,
        compiler_params=PARAMS,
        cost_estimate=pl.CostEstimate(flops=10**9, bytes_accessed=2 * 2**20, transcendentals=0),
        name="own_spectra",
    )(own, pairs, tables)


def anchor_rows(up, own, down):
    nodes = own.shape[0]
    return pl.pallas_call(
        rows_kernel,
        out_shape=jax.ShapeDtypeStruct((nodes + 2 * SWEEPS, nodes), F32),
        in_specs=[VMEM] * 3,
        out_specs=VMEM,
        compiler_params=pltpu.CompilerParams(vmem_limit_bytes=2**20),
        name="anchor_rows",
    )(up, own, down)


def flows(far, edge, own_spec, near_spec, pairs, tables):
    patches = far.shape[0] // PATCH * (far.shape[1] // PATCH)
    return pl.pallas_call(
        flows_kernel,
        out_shape=jax.ShapeDtypeStruct((8, PATCH), F32),
        in_specs=[VMEM] * 6,
        out_specs=VMEM,
        scratch_shapes=[pltpu.VMEM((3, 2 * patches, 8, PATCH), F32)],
        compiler_params=PARAMS,
        cost_estimate=pl.CostEstimate(flops=4 * 10**9, bytes_accessed=3 * 2**20, transcendentals=0),
        name="flows",
    )(far, edge, own_spec, near_spec, pairs, tables)


def spread_weights(nodes, patches):
    node_pos = (np.arange(nodes) + 0.5) * STRIDE / PATCH - 0.5
    weights = np.maximum(0.0, 1.0 - np.abs(node_pos[:, None] - np.arange(patches)[None, :]))
    return weights / weights.sum(axis=1, keepdims=True)


def ring_nodes(nodes):
    span = np.arange(nodes + 2 * SWEEPS) - SWEEPS
    ring = np.concatenate([span[SWEEPS:], span, span[:SWEEPS]])
    part = np.zeros(len(ring), np.int32)
    part[nodes + SWEEPS : len(ring) - SWEEPS] = 1
    order = np.arange(len(ring)).reshape(PATCH, -1).T.reshape(-1)
    return (ring[order], part[order])


def row_nodes(nodes):
    span = np.arange(nodes + 2 * SWEEPS) - SWEEPS
    return span.reshape(8, -1).T.reshape(-1)


def target_tables(nodes, patches):
    ring, part = ring_nodes(nodes)
    spread = spread_weights(nodes, patches)

    def wide(positions):
        table = np.zeros((len(positions), 3, patches))
        for tile in range(3):
            at = positions - (tile - 1) * nodes
            hit = (at >= 0) & (at < nodes)
            table[hit, tile] = spread[at[hit]]
        return table

    shape = (3, 3, patches, patches)
    rows = wide(row_nodes(nodes))[:, None, :, :, None]
    cols = wide(ring).transpose(1, 2, 0)[:, None, None]
    left = np.broadcast_to(rows, (rows.shape[0],) + shape).reshape(rows.shape[0], -1)
    right = np.broadcast_to(cols, shape + (len(ring),)).reshape(-1, len(ring))
    return (left.astype(BF16), right.astype(np.float32), part[None])


def ring_tables(nodes):
    ring, part = ring_nodes(nodes)
    place = np.arange(3 * nodes)[:, None] - nodes
    into = (place == ring[None]).astype(BF16)
    column = np.arange(2 * nodes)[None]
    out = ((ring[:, None] == column % nodes) & (part[:, None] == column // nodes)).astype(BF16)
    return (into, out, ring.astype(np.int32)[None])


def permuted(value, table):
    result = None
    for piece in range(3):
        part = value.astype(BF16)
        moved = dot(part, table)
        result = moved if result is None else result + moved
        value = value - part.astype(F32)
    return result


def tiles_beside(even_ref, odd_ref):
    at_even = lax.axis_index("tx") % 2 == 0
    even, odd = even_ref[...], odd_ref[...]
    return (jnp.where(at_even, odd, even), jnp.where(at_even, even, odd))


def gains_kernel(own_ref, even_ref, odd_ref, into_ref, ring_ref, gain_ref, pull_ref, rows_ref):
    strips = gain_ref.shape[0]
    nodes = own_ref.shape[1]
    before, after = tiles_beside(even_ref, odd_ref)
    weight = permuted(jnp.concatenate([before, own_ref[...], after], axis=1), into_ref[...])
    row_node = lax.broadcasted_iota(jnp.int32, weight.shape, 0) - SWEEPS
    row_node = row_node + lax.axis_index("ty") * nodes
    col_node = ring_ref[...] + lax.axis_index("tx") * nodes
    inside = (row_node >= 0) & (row_node < lax.axis_size("ty") * nodes)
    inside = inside & (col_node >= 0) & (col_node < lax.axis_size("tx") * nodes)
    gain = jnp.where(inside, 1.0 / (4.0 + weight), 0.0)
    for value, out in ((gain, gain_ref), (gain * weight, pull_ref)):
        rows_ref[...] = value.reshape(value.shape[0], -1, PATCH).transpose(1, 0, 2)
        for strip in range(strips):
            for tile in range(rows_ref.shape[0]):
                out[strip, :, tile * PATCH : (tile + 1) * PATCH] = rows_ref[tile, pl.ds(strip, 8, strips), :]


def gains(own, even, odd, nodes):
    into, _, ring = ring_tables(nodes)
    shape = jax.ShapeDtypeStruct((own.shape[0] // 8, 8, ring.shape[1]), F32)
    return pl.pallas_call(
        gains_kernel,
        out_shape=(shape, shape),
        in_specs=[VMEM] * 5,
        out_specs=(VMEM, VMEM),
        scratch_shapes=[pltpu.VMEM((ring.shape[1] // PATCH, own.shape[0], PATCH), F32)],
        compiler_params=PARAMS,
        cost_estimate=pl.CostEstimate(flops=10**9, bytes_accessed=2**20, transcendentals=0),
        name="gains",
    )(own, even, odd, jnp.asarray(into), jnp.asarray(ring))


def relax_kernel(
    own_ref, even_ref, odd_ref, gain_ref, pull_ref, left_ref, right_ref, part_ref, ones_ref, cols_table_ref, rows_table_ref,
    work_ref, landing_ref, base_ref,
):
    strips, _, lanes = work_ref.shape
    nodes = landing_ref.shape[1]
    patches = left_ref.shape[1] // 9
    before, after = tiles_beside(even_ref, odd_ref)
    rows = [before[:3], own_ref[:3], after[:3]]
    rows.append(jnp.zeros((PATCH - 9, PATCH), F32))
    columns = jnp.transpose(jnp.concatenate(rows, axis=0))

    def sources(part):
        lines = slice(part * patches, (part + 1) * patches)
        return jnp.concatenate([columns[lines, i : i + 1] for i in range(9)], axis=0)

    spread = jnp.where(part_ref[...] == 1, sources(1), sources(0)) * right_ref[...]
    target = None
    for piece in range(3):
        part = spread.astype(BF16)
        term = dot(left_ref[...], part)
        target = term if target is None else target + term
        spread = spread - part.astype(F32)
    target = target.reshape(strips, 8, lanes)
    base_ref[...] = pull_ref[...] * target
    work_ref[...] = jnp.where(gain_ref[...] > 0.0, target, 0.0)
    tiles = lanes // PATCH

    def row(strip):
        return [work_ref[strip, :, i * PATCH : (i + 1) * PATCH] for i in range(tiles)]

    def sweep(counter, carry):
        here = row(0)
        above = [pltpu.roll(value, 1, 0) for value in row(strips - 1)]
        around = [pltpu.roll(value, 7, 0) for value in here]
        for strip in range(strips):
            below = row(strip + 1) if strip + 1 < strips else around
            ring = [pltpu.roll(here[-1], 1, 1)] + here + [pltpu.roll(here[0], PATCH - 1, 1)]
            for tile in range(tiles):
                at = (strip, slice(None), slice(tile * PATCH, (tile + 1) * PATCH))
                total = (above[tile] + below[tile]) + (ring[tile] + ring[tile + 2])
                work_ref[at] = gain_ref[at] * total + base_ref[at]
            above, here = here, below
        return carry

    lax.fori_loop(0, SWEEPS, sweep, 0, unroll=8)
    mesh = work_ref[...].reshape(strips * 8, lanes)
    ones = ones_ref[...]
    sums = None
    for piece in range(3):
        part = mesh.astype(BF16)
        term = lax.dot_general(ones, part, (((1,), (1,)), ((), ())), preferred_element_type=F32)
        sums = term if sums is None else sums + term
        mesh = mesh - part.astype(F32)
    down_mean = permuted(sums, rows_table_ref[...])[:1] / nodes
    strip = lax.broadcasted_iota(jnp.int32, (strips, 8, lanes), 0)
    row = lax.broadcasted_iota(jnp.int32, (strips, 8, lanes), 1) * strips + strip
    kept = jnp.where((row >= SWEEPS) & (row < SWEEPS + nodes), work_ref[...], 0.0)
    across = permuted(jnp.sum(kept, axis=0), cols_table_ref[...])
    across_mean = jnp.sum(across, axis=0, keepdims=True) / nodes
    line = lax.broadcasted_iota(jnp.int32, landing_ref.shape, 0)
    ramp = lax.broadcasted_iota(jnp.int32, landing_ref.shape, 1).astype(F32)
    profile = jnp.where(line == 0, down_mean, across_mean)
    landing_ref[...] = jnp.clip(ramp + profile, 0.0, nodes - 1.0)


def relax(targets, weights, nodes, patches):
    left, right, part = target_tables(nodes, patches)
    ring, ring_part = ring_nodes(nodes)
    own = (ring >= 0) & (ring < nodes)
    ones = np.broadcast_to(own & (ring_part == 0), (16, len(ring))).astype(BF16)
    node = np.arange(nodes)[None]
    cols_table = ((ring[:, None] == node) & (ring_part[:, None] == 1)).astype(BF16)
    rows_table = (row_nodes(nodes)[:, None] == node).astype(BF16)
    tables = map(jnp.asarray, (left, right, part, ones, cols_table, rows_table))
    shape = weights[0].shape
    return pl.pallas_call(
        relax_kernel,
        out_shape=(jax.ShapeDtypeStruct(shape, F32), jax.ShapeDtypeStruct((8, nodes), F32)),
        in_specs=[VMEM] * 11,
        out_specs=(VMEM, VMEM),
        scratch_shapes=[pltpu.VMEM(shape, F32)],
        compiler_params=PARAMS,
        cost_estimate=pl.CostEstimate(flops=4 * 10**9, bytes_accessed=3 * 2**20, transcendentals=0),
        name="relax",
    )(*targets, *weights, *tables)


def mesh_kernel(ring_ref, table_ref, mesh_ref, rows_ref):
    strips, _, lanes = ring_ref.shape
    nodes = mesh_ref.shape[2]
    final = permuted(ring_ref[...].reshape(strips * 8, lanes), table_ref[...])
    for strip in range(strips):
        for part in range(2):
            columns = slice(part * nodes, (part + 1) * nodes)
            rows_ref[part, pl.ds(strip, 8, strips), :] = final[8 * strip : 8 * strip + 8, columns]
    mesh_ref[0] = rows_ref[:, SWEEPS : SWEEPS + nodes]


def natural_mesh(ring, nodes):
    _, table, _ = ring_tables(nodes)
    return pl.pallas_call(
        mesh_kernel,
        out_shape=jax.ShapeDtypeStruct((1, 2, nodes, nodes), F32),
        in_specs=[VMEM] * 2,
        out_specs=VMEM,
        scratch_shapes=[pltpu.VMEM((2, ring.shape[0] * 8, nodes), F32)],
        compiler_params=PARAMS,
        cost_estimate=pl.CostEstimate(flops=10**9, bytes_accessed=2**20, transcendentals=0),
        name="natural_mesh",
    )(ring, jnp.asarray(table))


def compose_kernel(*refs):
    *landing_refs, out_ref = refs
    count = len(landing_refs)
    section = lax.axis_index("gz")
    received = [ref[...] for ref in landing_refs]
    nodes = received[0].shape[1]
    ramp = lax.broadcasted_iota(jnp.int32, received[0].shape, 1).astype(F32)
    value = received[0]
    for other in range(count - 2, -1, -1):
        landing = received[0]
        for code in range(1, count):
            landing = jnp.where(section == other ^ code, received[code], landing)
        floor = jnp.minimum(jnp.floor(landing), nodes - 2.0)
        index = floor.astype(jnp.int32)
        share = landing - floor
        below = jnp.take_along_axis(value, index, axis=1)
        above = jnp.take_along_axis(value, index + 1, axis=1)
        value = jnp.where(section > other, (1.0 - share) * below + share * above, value)
    out_ref[0, 0, 0] = (value - ramp)[:2]


def compose(landings):
    nodes = landings[0].shape[1]
    return pl.pallas_call(
        compose_kernel,
        out_shape=jax.ShapeDtypeStruct((1, 1, 1, 2, nodes), F32),
        in_specs=[VMEM] * len(landings),
        out_specs=VMEM,
        compiler_params=pltpu.CompilerParams(vmem_limit_bytes=2**20),
        name="compose",
    )(*landings)


def swap_pairs(value, axis, first, spare):
    count, other = lax.axis_size(axis), lax.axis_size(spare)
    axes = ("gz", "ty", "tx")
    flip = axes.index(axis) > axes.index(spare)

    def place(here, beside):
        return beside * count + here if flip else here * other + beside

    moves = []
    for here in range(count):
        there = ((here + first) ^ 1) - first
        for beside in range(other):
            target = place(there, beside) if 0 <= there < count else place(here, beside ^ 1)
            moves.append((place(here, beside), target))
    return lax.ppermute(value, (spare, axis) if flip else (axis, spare), moves)


def rows_beside(value):
    count = lax.axis_size("ty")
    if count == 2:
        other = swap_pairs(value, "ty", 0, "gz")
        return (other, other)
    even = swap_pairs(value, "ty", 0, "gz")
    odd = swap_pairs(value, "ty", 1, "gz")
    at_even = lax.axis_index("ty") % 2 == 0
    return (jnp.where(at_even, odd, even), jnp.where(at_even, even, odd))


def to_next(value, turn):
    count, rows = lax.axis_size("gz"), lax.axis_size("ty")
    if not turn:
        return lax.ppermute(value, "gz", [(i, (i + 1) % count) for i in range(count)])
    moves = [(i * rows + j, (i + 1) % count * rows + (j ^ 1)) for i in range(count) for j in range(rows)]
    return lax.ppermute(value, ("gz", "ty"), moves)


def patch_targets(flow):
    first = lax.axis_index("gz") <= 1
    before = to_next(flow, 0)

    def target(near, earlier):
        return jnp.where(first, near[0:1], 0.5 * (near[0:1] + earlier[1:2]))

    if lax.axis_size("ty") == 2:
        beside = target(rows_beside(flow)[0], to_next(flow, 1))
        lines = [beside, target(flow, before), beside]
    else:
        (up, down), (up_before, down_before) = rows_beside(flow), rows_beside(before)
        lines = [target(up, up_before), target(flow, before), target(down, down_before)]
    return jnp.concatenate(lines + [jnp.zeros((5, flow.shape[1]), F32)], axis=0)


def local(images, boundary, anchor):
    nodes = anchor.shape[1]
    own = images[0]
    patches = own.shape[0] // PATCH
    sections = lax.axis_size("gz")
    tables = transform_tables()
    far = swap_pairs(own, "gz", 1, "ty")
    near = swap_pairs(own, "gz", 0, "ty")
    up, down = rows_beside(anchor[0])
    near_spec, pairs = near_spectra(near, tables)
    own_spec = own_spectra(own, pairs, tables)
    up, down, own_spec = lax.optimization_barrier((up, down, own_spec))
    rows = anchor_rows(up, anchor[0], down)
    weights = gains(rows, swap_pairs(rows, "tx", 0, "gz"), swap_pairs(rows, "tx", 1, "gz"), nodes)
    far, own_spec, near_spec = lax.optimization_barrier((far, own_spec, near_spec))
    flow = flows(far, boundary, own_spec, near_spec, pairs, tables)
    line = patch_targets(flow)
    targets = (line, swap_pairs(line, "tx", 0, "gz"), swap_pairs(line, "tx", 1, "gz"))
    ring, landing = relax(targets, weights, nodes, patches)
    landings = [landing]
    for code in range(1, sections):
        landings.append(lax.ppermute(landing, "gz", [(i, i ^ code) for i in range(sections)]))
    mesh = natural_mesh(ring, nodes)
    mesh, landings = lax.optimization_barrier((mesh, landings))
    drift = compose(landings)
    return (mesh, drift)


def solution(mesh):
    return jax.shard_map(
        local,
        mesh=mesh,
        in_specs=(P("gz", "ty", "tx"), P("ty", "tx"), P("gz", "ty", "tx")),
        out_specs=(P("gz", None, "ty", "tx"), P("gz", "ty", "tx", None, None)),
        check_vma=False,
    )
```

```python
import math

import jax
import jax.numpy as jnp
import numpy as np
from jax import lax
from jax.experimental import pallas as pl
from jax.experimental.pallas import tpu as pltpu
from jax.sharding import PartitionSpec as P

PATCH = 128
STRIDE = 4
SWEEPS = 32
HALF = PATCH // 2
BF16 = jnp.bfloat16
F32 = jnp.float32


def split_table(table):
    high = table.astype(BF16)
    low = (table - high.astype(np.float64)).astype(BF16)
    return (high, low)


def transform_tables():
    counter = np.arange(PATCH)
    phase = (counter[:, None] * counter[None, :] % PATCH) * (2.0 * math.pi / PATCH)
    basis = np.concatenate([np.cos(phase[:HALF]), np.sin(phase[:HALF])])
    basis[HALF] = np.cos(phase[HALF])
    gains = np.full(PATCH, 2.0)
    gains[0] = gains[HALF] = 1.0
    inverse = basis.T * gains / PATCH
    tables = [part for table in (basis.T, inverse.T, basis, inverse / PATCH) for part in split_table(table)]
    return jnp.asarray(np.stack(tables))


def pair_tables(tables_ref):
    lower = lax.broadcasted_iota(jnp.int32, (PATCH, PATCH), 1) < HALF
    forwards, inverses = [], []
    for index in range(2):
        table = tables_ref[index].astype(F32)
        turned = pltpu.roll(table, HALF, 1)
        first = jnp.concatenate([jnp.where(lower, table, 0.0), jnp.where(lower, turned, 0.0)], axis=1)
        second = jnp.concatenate([jnp.where(lower, 0.0, turned), jnp.where(lower, 0.0, table)], axis=1)
        forwards.append(jnp.concatenate([first, second], axis=0).astype(BF16))
        table = tables_ref[2 + index]
        empty = jnp.zeros((HALF, PATCH), BF16)
        rows = []
        for part in (table[:HALF], table[HALF:]):
            rows += [jnp.concatenate([part, empty], axis=1), jnp.concatenate([empty, part], axis=1)]
        inverses.append(jnp.concatenate(rows, axis=0))
    return forwards + inverses


def halves(value):
    high = value.astype(BF16)
    return (high, (value - high.astype(F32)).astype(BF16))


def dot(left, right):
    return jnp.dot(left, right, preferred_element_type=F32)


def left_transform(table_high, table_low, value):
    high, low = halves(value)
    table = jnp.concatenate([table_high, table_high, table_low], axis=1)
    return dot(table, jnp.concatenate([high, low, high], axis=0))


def quarters(spec):
    return (
        (spec[:HALF, :PATCH], spec[:HALF, PATCH:]),
        (spec[HALF:, :PATCH], spec[HALF:, PATCH:]),
    )


def cross_operand(spec):
    (cc, cs), (sc, ss) = quarters(spec)
    first_row = lax.broadcasted_iota(jnp.int32, (HALF, PATCH), 0) == 0
    first_lane = lax.broadcasted_iota(jnp.int32, (HALF, PATCH), 1) % HALF == 0

    def lanes(cosine, sine):
        return (cosine, jnp.where(first_lane, sine, cosine), jnp.where(first_lane, 0.0, sine))

    return (
        lanes(cc, cs),
        lanes(jnp.where(first_row, sc, cc), jnp.where(first_row, ss, cs)),
        lanes(jnp.where(first_row, 0.0, sc), jnp.where(first_row, 0.0, ss)),
    )


def cross(operand, spec):
    (row_c, row_d, row_s) = operand
    (bc, bs) = quarters(spec)

    def cosine(a, b):
        return a[0] * b[0] + a[2] * b[1]

    def sine(a, b):
        return a[1] * b[1] - a[2] * b[0]

    cc = cosine(row_c, bc) + cosine(row_s, bs)
    cs = sine(row_c, bc) + sine(row_s, bs)
    sc = cosine(row_d, bs) - cosine(row_s, bc)
    ss = sine(row_d, bs) - sine(row_s, bc)
    return jnp.concatenate(
        [jnp.concatenate([cc, cs], axis=1), jnp.concatenate([sc, ss], axis=1)], axis=0
    )


def windows(rows, cols):
    wide = 2 * PATCH
    return [(slice(r, r + PATCH), slice(c, c + wide)) for r in range(0, rows, PATCH) for c in range(0, cols, wide)]


def side_by_side(value):
    return jnp.concatenate([value[i : i + PATCH] for i in range(0, value.shape[0], PATCH)], axis=1)


def forward(pixels, pairs, tables_ref):
    right = dot(pixels, pairs[0]) + dot(pixels, pairs[1])
    return left_transform(tables_ref[4], tables_ref[5], side_by_side(right))


def image_spectra(image_ref, pairs, tables_ref):
    pixels = jnp.concatenate([image_ref[window] for window in windows(*image_ref.shape)], axis=0)
    return forward(pixels, pairs, tables_ref)


def near_kernel(image_ref, tables_ref, spec_out, pairs_out):
    pairs = pair_tables(tables_ref)
    for index, pair in enumerate(pairs):
        pairs_out[index] = pair
    spec_out[...] = image_spectra(image_ref, pairs, tables_ref)


def own_kernel(image_ref, pairs_ref, tables_ref, spec_out):
    spec_out[...] = image_spectra(image_ref, pairs_ref, tables_ref)


def rows_kernel(up_ref, own_ref, down_ref, out_ref):
    nodes = own_ref.shape[0]
    out_ref[:SWEEPS] = up_ref[nodes - SWEEPS :]
    out_ref[SWEEPS : SWEEPS + nodes] = own_ref[...]
    out_ref[SWEEPS + nodes :] = down_ref[:SWEEPS]


def flows_kernel(
    far_ref, edge_ref, own_spec, near_spec, rights_ref, tables_ref, out_ref, stats_ref
):
    wide = 2 * PATCH
    spots = windows(*far_ref.shape)
    blocks = len(spots)
    patches = 2 * blocks
    at_edge = lax.axis_index("gz") == 0
    at_even = lax.axis_index("gz") % 2 == 0
    pixels = jnp.concatenate(
        [jnp.where(at_edge, edge_ref[spot].astype(F32), far_ref[spot].astype(F32)).astype(BF16) for spot in spots], axis=0
    )
    spec = forward(pixels, rights_ref, tables_ref)
    products = []
    for block in range(blocks):
        lanes = slice(block * wide, (block + 1) * wide)
        far, near = spec[:, lanes], near_spec[:, lanes]
        operand = cross_operand(jnp.where(at_even, far, near))
        products.append(cross(operand, own_spec[:, lanes]))
        products.append(cross(operand, jnp.where(at_even, near, far)))
    high, low = halves(jnp.concatenate(products, axis=0))
    back = dot(high, rights_ref[2]) + dot(low, rights_ref[2]) + dot(high, rights_ref[3])
    scores = left_transform(tables_ref[6], tables_ref[7], side_by_side(back))
    groups = scores.reshape(PATCH // 8, 8, 2 * blocks * wide)
    peak = jnp.max(groups, axis=0)
    total = jnp.zeros_like(peak)
    moment = jnp.zeros_like(peak)
    for group in range(PATCH // 8):
        weight = jnp.exp(groups[group] - peak)
        shift = 8 * group - (PATCH if group >= PATCH // 16 else 0)
        total = total + weight
        moment = moment + float(shift) * weight
    for block in range(blocks):
        for pair in range(2):
            for side in range(2):
                at = (2 * block + pair) * 2 + side
                lanes = slice(at * PATCH, (at + 1) * PATCH)
                slot = pair * patches + 2 * block + side
                stats_ref[0, slot] = peak[:, lanes]
                stats_ref[1, slot] = total[:, lanes]
                stats_ref[2, slot] = moment[:, lanes]
    peak = stats_ref[0]
    best = jnp.max(jnp.max(peak, axis=1, keepdims=True), axis=2, keepdims=True)
    scale = jnp.exp(peak - best)
    total = scale * stats_ref[1]
    within = lax.broadcasted_iota(jnp.int32, peak.shape, 1).astype(F32)
    moment = scale * stats_ref[2] + within * total
    total = jnp.sum(total, axis=1)
    lane = lax.broadcasted_iota(jnp.int32, total.shape, 1)
    signed = jnp.where(lane < HALF, lane, lane - PATCH).astype(F32)
    mass = jnp.sum(total, axis=1, keepdims=True) * STRIDE
    along_rows = jnp.sum(jnp.sum(moment, axis=1), axis=1, keepdims=True) / mass
    along_cols = jnp.sum(total * signed, axis=1, keepdims=True) / mass
    values = (
        along_rows[:patches],
        along_cols[:patches],
        along_rows[patches:] - along_rows[:patches],
        along_cols[patches:] - along_cols[:patches],
    )
    lane = lax.broadcasted_iota(jnp.int32, (patches, PATCH), 1)
    patch = lax.broadcasted_iota(jnp.int32, (patches, PATCH), 0)
    lines = []
    for first, second in (values[:2], values[2:]):
        line = jnp.where(lane == patch, first, jnp.where(lane == patches + patch, second, 0.0))
        lines.append(jnp.sum(line, axis=0, keepdims=True))
    line = lax.broadcasted_iota(jnp.int32, out_ref.shape, 0)
    out_ref[...] = jnp.where(line == 0, lines[0], lines[1])


VMEM = pl.BlockSpec(memory_space=pltpu.VMEM)
PARAMS = pltpu.CompilerParams(vmem_limit_bytes=40 * 2**20)


def spec_shape(image):
    return jax.ShapeDtypeStruct((PATCH, image.shape[0] // PATCH * image.shape[1]), F32)


def near_spectra(near, tables):
    pairs = jax.ShapeDtypeStruct((4, 2 * PATCH, 2 * PATCH), BF16)
    return pl.pallas_call(
        near_kernel,
        out_shape=(spec_shape(near), pairs),
        in_specs=[VMEM] * 2,
        out_specs=(VMEM, VMEM),
        compiler_params=PARAMS,
        cost_estimate=pl.CostEstimate(flops=2 * 10**9, bytes_accessed=2 * 2**20, transcendentals=0),
        name="near_spectra",
    )(near, tables)


def own_spectra(own, pairs, tables):
    return pl.pallas_call(
        own_kernel,
        out_shape=spec_shape(own),
        in_specs=[VMEM] * 3,
        out_specs=VMEM,
        compiler_params=PARAMS,
        cost_estimate=pl.CostEstimate(flops=10**9, bytes_accessed=2 * 2**20, transcendentals=0),
        name="own_spectra",
    )(own, pairs, tables)


def anchor_rows(up, own, down):
    nodes = own.shape[0]
    return pl.pallas_call(
        rows_kernel,
        out_shape=jax.ShapeDtypeStruct((nodes + 2 * SWEEPS, nodes), F32),
        in_specs=[VMEM] * 3,
        out_specs=VMEM,
        compiler_params=pltpu.CompilerParams(vmem_limit_bytes=2**20),
        name="anchor_rows",
    )(up, own, down)


def flows(far, edge, own_spec, near_spec, pairs, tables):
    patches = far.shape[0] // PATCH * (far.shape[1] // PATCH)
    return pl.pallas_call(
        flows_kernel,
        out_shape=jax.ShapeDtypeStruct((8, PATCH), F32),
        in_specs=[VMEM] * 6,
        out_specs=VMEM,
        scratch_shapes=[pltpu.VMEM((3, 2 * patches, 8, PATCH), F32)],
        compiler_params=PARAMS,
        cost_estimate=pl.CostEstimate(flops=4 * 10**9, bytes_accessed=3 * 2**20, transcendentals=0),
        name="flows",
    )(far, edge, own_spec, near_spec, pairs, tables)


def spread_weights(nodes, patches):
    node_pos = (np.arange(nodes) + 0.5) * STRIDE / PATCH - 0.5
    weights = np.maximum(0.0, 1.0 - np.abs(node_pos[:, None] - np.arange(patches)[None, :]))
    return weights / weights.sum(axis=1, keepdims=True)


def ring_nodes(nodes):
    span = np.arange(nodes + 2 * SWEEPS) - SWEEPS
    ring = np.concatenate([span[SWEEPS:], span, span[:SWEEPS]])
    part = np.zeros(len(ring), np.int32)
    part[nodes + SWEEPS : len(ring) - SWEEPS] = 1
    order = np.arange(len(ring)).reshape(PATCH, -1).T.reshape(-1)
    return (ring[order], part[order])


def row_nodes(nodes):
    span = np.arange(nodes + 2 * SWEEPS) - SWEEPS
    return span.reshape(8, -1).T.reshape(-1)


def target_tables(nodes, patches):
    ring, _ = ring_nodes(nodes)
    spread = spread_weights(nodes, patches)

    def wide(positions):
        table = np.zeros((len(positions), 3, patches))
        for tile in range(3):
            at = positions - (tile - 1) * nodes
            hit = (at >= 0) & (at < nodes)
            table[hit, tile] = spread[at[hit]]
        return table

    shape = (3, 3, patches, patches)
    rows = wide(row_nodes(nodes))[:, None, :, :, None]
    cols = wide(ring).transpose(1, 2, 0)[:, None, None]
    left = np.broadcast_to(rows, (rows.shape[0],) + shape).reshape(rows.shape[0], -1)
    right = np.broadcast_to(cols, shape + (len(ring),)).reshape(-1, len(ring))
    return (left.astype(BF16), right.astype(BF16))


def ring_tables(nodes):
    ring, part = ring_nodes(nodes)
    place = np.arange(3 * nodes)[:, None] - nodes
    into = (place == ring[None]).astype(BF16)
    column = np.arange(2 * nodes)[None]
    out = ((ring[:, None] == column % nodes) & (part[:, None] == column // nodes)).astype(BF16)
    return (into, out)


def permuted(value, table):
    result = None
    for piece in range(3):
        part = value.astype(BF16)
        moved = dot(part, table)
        result = moved if result is None else result + moved
        value = value - part.astype(F32)
    return result


def ring_place(rows, lanes):
    lane = lax.broadcasted_iota(jnp.int32, (rows, lanes), 1)
    return lane % PATCH * (lanes // PATCH) + lane // PATCH


def tiles_beside(even_ref, odd_ref):
    at_even = lax.axis_index("tx") % 2 == 0
    even, odd = even_ref[...], odd_ref[...]
    return (jnp.where(at_even, odd, even), jnp.where(at_even, even, odd))


def gains_kernel(own_ref, even_ref, odd_ref, into_ref, gain_ref, pull_ref, rows_ref):
    strips = gain_ref.shape[0]
    nodes = own_ref.shape[1]
    before, after = tiles_beside(even_ref, odd_ref)
    weight = permuted(jnp.concatenate([before, own_ref[...], after], axis=1), into_ref[...])
    row_node = lax.broadcasted_iota(jnp.int32, weight.shape, 0) - SWEEPS
    row_node = row_node + lax.axis_index("ty") * nodes
    lanes = into_ref.shape[1]
    place = ring_place(1, lanes)
    shift = jnp.where(place < nodes + SWEEPS, 0, jnp.where(place < lanes - SWEEPS, nodes + 2 * SWEEPS, lanes))
    col_node = place - shift + lax.axis_index("tx") * nodes
    inside = (row_node >= 0) & (row_node < lax.axis_size("ty") * nodes)
    inside = inside & (col_node >= 0) & (col_node < lax.axis_size("tx") * nodes)
    gain = jnp.where(inside, 1.0 / (4.0 + weight), 0.0)
    for value, out in ((gain, gain_ref), (gain * weight, pull_ref)):
        rows_ref[...] = value.reshape(value.shape[0], -1, PATCH).transpose(1, 0, 2)
        for strip in range(strips):
            for tile in range(rows_ref.shape[0]):
                out[strip, :, tile * PATCH : (tile + 1) * PATCH] = rows_ref[tile, pl.ds(strip, 8, strips), :]


def gains(own, even, odd, nodes):
    into, _ = ring_tables(nodes)
    shape = jax.ShapeDtypeStruct((own.shape[0] // 8, 8, into.shape[1]), F32)
    return pl.pallas_call(
        gains_kernel,
        out_shape=(shape, shape),
        in_specs=[VMEM] * 4,
        out_specs=(VMEM, VMEM),
        scratch_shapes=[pltpu.VMEM((into.shape[1] // PATCH, own.shape[0], PATCH), F32)],
        compiler_params=PARAMS,
        cost_estimate=pl.CostEstimate(flops=10**9, bytes_accessed=2**20, transcendentals=0),
        name="gains",
    )(own, even, odd, jnp.asarray(into))


def relax_kernel(
    own_ref, even_ref, odd_ref, gain_ref, pull_ref, left_ref, right_ref, cols_table_ref, rows_table_ref,
    work_ref, landing_ref, base_ref,
):
    strips, _, lanes = work_ref.shape
    nodes = landing_ref.shape[1]
    patches = left_ref.shape[1] // 9
    before, after = tiles_beside(even_ref, odd_ref)
    rows = [before[:3], own_ref[:3], after[:3]]
    rows.append(jnp.zeros((PATCH - 9, PATCH), F32))
    columns = jnp.transpose(jnp.concatenate(rows, axis=0))

    def sources(part):
        lines = slice(part * patches, (part + 1) * patches)
        return jnp.concatenate([columns[lines, i : i + 1] for i in range(9)], axis=0)

    place = ring_place(1, lanes)
    second = (place >= nodes + SWEEPS) & (place < lanes - SWEEPS)
    spread = jnp.where(second, sources(1), sources(0)) * right_ref[...].astype(F32)
    target = None
    for piece in range(3):
        part = spread.astype(BF16)
        term = dot(left_ref[...], part)
        target = term if target is None else target + term
        spread = spread - part.astype(F32)
    target = target.reshape(strips, 8, lanes)
    base_ref[...] = pull_ref[...] * target
    work_ref[...] = jnp.where(gain_ref[...] > 0.0, target, 0.0)
    tiles = lanes // PATCH

    def row(strip):
        return [work_ref[strip, :, i * PATCH : (i + 1) * PATCH] for i in range(tiles)]

    def sweep(counter, carry):
        here = row(0)
        above = [pltpu.roll(value, 1, 0) for value in row(strips - 1)]
        around = [pltpu.roll(value, 7, 0) for value in here]
        for strip in range(strips):
            below = row(strip + 1) if strip + 1 < strips else around
            ring = [pltpu.roll(here[-1], 1, 1)] + here + [pltpu.roll(here[0], PATCH - 1, 1)]
            for tile in range(tiles):
                at = (strip, slice(None), slice(tile * PATCH, (tile + 1) * PATCH))
                total = (above[tile] + below[tile]) + (ring[tile] + ring[tile + 2])
                work_ref[at] = gain_ref[at] * total + base_ref[at]
            above, here = here, below
        return carry

    lax.fori_loop(0, SWEEPS, sweep, 0, unroll=16)
    mesh = work_ref[...].reshape(strips * 8, lanes)
    ones = jnp.where(ring_place(16, lanes) < nodes, 1.0, 0.0).astype(BF16)
    sums = None
    for piece in range(3):
        part = mesh.astype(BF16)
        term = lax.dot_general(ones, part, (((1,), (1,)), ((), ())), preferred_element_type=F32)
        sums = term if sums is None else sums + term
        mesh = mesh - part.astype(F32)
    down_mean = permuted(sums, rows_table_ref[...])[:1] / nodes
    strip = lax.broadcasted_iota(jnp.int32, (strips, 8, lanes), 0)
    row = lax.broadcasted_iota(jnp.int32, (strips, 8, lanes), 1) * strips + strip
    kept = jnp.where((row >= SWEEPS) & (row < SWEEPS + nodes), work_ref[...], 0.0)
    across = permuted(jnp.sum(kept, axis=0), cols_table_ref[...])
    across_mean = jnp.sum(across, axis=0, keepdims=True) / nodes
    line = lax.broadcasted_iota(jnp.int32, landing_ref.shape, 0)
    ramp = lax.broadcasted_iota(jnp.int32, landing_ref.shape, 1).astype(F32)
    profile = jnp.where(line == 0, down_mean, across_mean)
    landing_ref[...] = jnp.clip(ramp + profile, 0.0, nodes - 1.0)


def relax(targets, weights, nodes, patches):
    left, right = target_tables(nodes, patches)
    ring, ring_part = ring_nodes(nodes)
    node = np.arange(nodes)[None]
    cols_table = ((ring[:, None] == node) & (ring_part[:, None] == 1)).astype(BF16)
    rows_table = (row_nodes(nodes)[:, None] == node).astype(BF16)
    tables = map(jnp.asarray, (left, right, cols_table, rows_table))
    shape = weights[0].shape
    return pl.pallas_call(
        relax_kernel,
        out_shape=(jax.ShapeDtypeStruct(shape, F32), jax.ShapeDtypeStruct((8, nodes), F32)),
        in_specs=[VMEM] * 9,
        out_specs=(VMEM, VMEM),
        scratch_shapes=[pltpu.VMEM(shape, F32)],
        compiler_params=PARAMS,
        cost_estimate=pl.CostEstimate(flops=4 * 10**9, bytes_accessed=3 * 2**20, transcendentals=0),
        name="relax",
    )(*targets, *weights, *tables)


def mesh_kernel(ring_ref, table_ref, mesh_ref, rows_ref):
    strips, _, lanes = ring_ref.shape
    nodes = mesh_ref.shape[2]
    final = permuted(ring_ref[...].reshape(strips * 8, lanes), table_ref[...])
    for strip in range(strips):
        for part in range(2):
            columns = slice(part * nodes, (part + 1) * nodes)
            rows_ref[part, pl.ds(strip, 8, strips), :] = final[8 * strip : 8 * strip + 8, columns]
    mesh_ref[0] = rows_ref[:, SWEEPS : SWEEPS + nodes]


def natural_mesh(ring, nodes):
    _, table = ring_tables(nodes)
    return pl.pallas_call(
        mesh_kernel,
        out_shape=jax.ShapeDtypeStruct((1, 2, nodes, nodes), F32),
        in_specs=[VMEM] * 2,
        out_specs=VMEM,
        scratch_shapes=[pltpu.VMEM((2, ring.shape[0] * 8, nodes), F32)],
        compiler_params=PARAMS,
        cost_estimate=pl.CostEstimate(flops=10**9, bytes_accessed=2**20, transcendentals=0),
        name="natural_mesh",
    )(ring, jnp.asarray(table))


def compose_kernel(*refs):
    *landing_refs, out_ref = refs
    count = len(landing_refs)
    section = lax.axis_index("gz")
    received = [ref[...] for ref in landing_refs]
    nodes = received[0].shape[1]
    ramp = lax.broadcasted_iota(jnp.int32, received[0].shape, 1).astype(F32)
    value = received[0]
    for other in range(count - 2, -1, -1):
        landing = received[0]
        for code in range(1, count):
            landing = jnp.where(section == other ^ code, received[code], landing)
        floor = jnp.minimum(jnp.floor(landing), nodes - 2.0)
        index = floor.astype(jnp.int32)
        share = landing - floor
        below = jnp.take_along_axis(value, index, axis=1)
        above = jnp.take_along_axis(value, index + 1, axis=1)
        value = jnp.where(section > other, (1.0 - share) * below + share * above, value)
    out_ref[0, 0, 0] = (value - ramp)[:2]


def compose(landings):
    nodes = landings[0].shape[1]
    return pl.pallas_call(
        compose_kernel,
        out_shape=jax.ShapeDtypeStruct((1, 1, 1, 2, nodes), F32),
        in_specs=[VMEM] * len(landings),
        out_specs=VMEM,
        compiler_params=pltpu.CompilerParams(vmem_limit_bytes=2**20),
        name="compose",
    )(*landings)


def swap_pairs(value, axis, first, spare):
    count, other = lax.axis_size(axis), lax.axis_size(spare)
    axes = ("gz", "ty", "tx")
    flip = axes.index(axis) > axes.index(spare)

    def place(here, beside):
        return beside * count + here if flip else here * other + beside

    moves = []
    for here in range(count):
        there = ((here + first) ^ 1) - first
        for beside in range(other):
            target = place(there, beside) if 0 <= there < count else place(here, beside ^ 1)
            moves.append((place(here, beside), target))
    return lax.ppermute(value, (spare, axis) if flip else (axis, spare), moves)


def rows_beside(value):
    count = lax.axis_size("ty")
    if count == 2:
        other = swap_pairs(value, "ty", 0, "gz")
        return (other, other)
    even = swap_pairs(value, "ty", 0, "gz")
    odd = swap_pairs(value, "ty", 1, "gz")
    at_even = lax.axis_index("ty") % 2 == 0
    return (jnp.where(at_even, odd, even), jnp.where(at_even, even, odd))


def to_next(value, turn):
    count, rows = lax.axis_size("gz"), lax.axis_size("ty")
    if not turn:
        return lax.ppermute(value, "gz", [(i, (i + 1) % count) for i in range(count)])
    moves = [(i * rows + j, (i + 1) % count * rows + (j ^ 1)) for i in range(count) for j in range(rows)]
    return lax.ppermute(value, ("gz", "ty"), moves)


def patch_targets(flow):
    first = lax.axis_index("gz") <= 1
    before = to_next(flow, 0)

    def target(near, earlier):
        return jnp.where(first, near[0:1], 0.5 * (near[0:1] + earlier[1:2]))

    if lax.axis_size("ty") == 2:
        beside = target(rows_beside(flow)[0], to_next(flow, 1))
        lines = [beside, target(flow, before), beside]
    else:
        (up, down), (up_before, down_before) = rows_beside(flow), rows_beside(before)
        lines = [target(up, up_before), target(flow, before), target(down, down_before)]
    return jnp.concatenate(lines + [jnp.zeros((5, flow.shape[1]), F32)], axis=0)


def local(images, boundary, anchor):
    nodes = anchor.shape[1]
    own = images[0]
    patches = own.shape[0] // PATCH
    sections = lax.axis_size("gz")
    tables = transform_tables()
    far = swap_pairs(own, "gz", 1, "ty")
    near = swap_pairs(own, "gz", 0, "ty")
    up, down = rows_beside(anchor[0])
    near_spec, pairs = near_spectra(near, tables)
    own_spec = own_spectra(own, pairs, tables)
    far, own_spec, near_spec = lax.optimization_barrier((far, own_spec, near_spec))
    flow = flows(far, boundary, own_spec, near_spec, pairs, tables)
    flow, up, down = lax.optimization_barrier((flow, up, down))
    rows = anchor_rows(up, anchor[0], down)
    weights = gains(rows, swap_pairs(rows, "tx", 0, "gz"), swap_pairs(rows, "tx", 1, "gz"), nodes)
    line = patch_targets(flow)
    targets = (line, swap_pairs(line, "tx", 0, "gz"), swap_pairs(line, "tx", 1, "gz"))
    ring, landing = relax(targets, weights, nodes, patches)
    landings = [landing]
    for code in range(1, sections):
        landings.append(lax.ppermute(landing, "gz", [(i, i ^ code) for i in range(sections)]))
    mesh = natural_mesh(ring, nodes)
    mesh, landings = lax.optimization_barrier((mesh, landings))
    drift = compose(landings)
    return (mesh, drift)


def solution(mesh):
    return jax.shard_map(
        local,
        mesh=mesh,
        in_specs=(P("gz", "ty", "tx"), P("ty", "tx"), P("gz", "ty", "tx")),
        out_specs=(P("gz", None, "ty", "tx"), P("gz", "ty", "tx", None, None)),
        check_vma=False,
    )
```

```python
import math

import jax
import jax.numpy as jnp
import numpy as np
from jax import lax
from jax.experimental import pallas as pl
from jax.experimental.pallas import tpu as pltpu
from jax.sharding import PartitionSpec as P

PATCH = 128
STRIDE = 4
SWEEPS = 32
HALF = PATCH // 2
BF16 = jnp.bfloat16
F32 = jnp.float32


def split_table(table):
    high = table.astype(BF16)
    low = (table - high.astype(np.float64)).astype(BF16)
    return (high, low)


def transform_tables():
    counter = np.arange(PATCH)
    phase = (counter[:, None] * counter[None, :] % PATCH) * (2.0 * math.pi / PATCH)
    basis = np.concatenate([np.cos(phase[:HALF]), np.sin(phase[:HALF])])
    basis[HALF] = np.cos(phase[HALF])
    gains = np.full(PATCH, 2.0)
    gains[0] = gains[HALF] = 1.0
    inverse = basis.T * gains / PATCH
    tables = [part for table in (basis.T, inverse.T, basis, inverse / PATCH) for part in split_table(table)]
    return jnp.asarray(np.stack(tables))


def pair_tables(tables_ref):
    lower = lax.broadcasted_iota(jnp.int32, (PATCH, PATCH), 1) < HALF
    pairs = []
    for index in range(2):
        table = tables_ref[index].astype(F32)
        turned = pltpu.roll(table, HALF, 1)
        first = jnp.concatenate([jnp.where(lower, table, 0.0), jnp.where(lower, turned, 0.0)], axis=1)
        second = jnp.concatenate([jnp.where(lower, 0.0, turned), jnp.where(lower, 0.0, table)], axis=1)
        pairs.append(jnp.concatenate([first, second], axis=0).astype(BF16))
    inverse = jnp.concatenate([tables_ref[2], tables_ref[3]], axis=1)
    return pairs + [jnp.concatenate([inverse, inverse], axis=0)]


def single_patches(product):
    lower = lax.broadcasted_iota(jnp.int32, (PATCH, PATCH), 1) < HALF
    cosine, sine = product[:, :PATCH], product[:, PATCH:]
    first = jnp.where(lower, cosine, pltpu.roll(sine, HALF, 1))
    second = jnp.where(lower, pltpu.roll(cosine, HALF, 1), sine)
    return [first, second]


def halves(value):
    high = value.astype(BF16)
    return (high, (value - high.astype(F32)).astype(BF16))


def dot(left, right):
    return jnp.dot(left, right, preferred_element_type=F32)


def left_transform(table_high, table_low, value):
    high, low = halves(value)
    table = jnp.concatenate([table_high, table_high, table_low], axis=1)
    return dot(table, jnp.concatenate([high, low, high], axis=0))


def quarters(spec):
    return (
        (spec[:HALF, :PATCH], spec[:HALF, PATCH:]),
        (spec[HALF:, :PATCH], spec[HALF:, PATCH:]),
    )


def cross_operand(spec):
    (cc, cs), (sc, ss) = quarters(spec)
    first_row = lax.broadcasted_iota(jnp.int32, (HALF, PATCH), 0) == 0
    first_lane = lax.broadcasted_iota(jnp.int32, (HALF, PATCH), 1) % HALF == 0

    def lanes(cosine, sine):
        return (cosine, jnp.where(first_lane, sine, cosine), jnp.where(first_lane, 0.0, sine))

    return (
        lanes(cc, cs),
        lanes(jnp.where(first_row, sc, cc), jnp.where(first_row, ss, cs)),
        lanes(jnp.where(first_row, 0.0, sc), jnp.where(first_row, 0.0, ss)),
    )


def cross(operand, spec):
    (row_c, row_d, row_s) = operand
    (bc, bs) = quarters(spec)

    def cosine(a, b):
        return a[0] * b[0] + a[2] * b[1]

    def sine(a, b):
        return a[1] * b[1] - a[2] * b[0]

    cc = cosine(row_c, bc) + cosine(row_s, bs)
    cs = sine(row_c, bc) + sine(row_s, bs)
    sc = cosine(row_d, bs) - cosine(row_s, bc)
    ss = sine(row_d, bs) - sine(row_s, bc)
    return jnp.concatenate(
        [jnp.concatenate([cc, cs], axis=1), jnp.concatenate([sc, ss], axis=1)], axis=0
    )


def windows(rows, cols):
    wide = 2 * PATCH
    return [(slice(r, r + PATCH), slice(c, c + wide)) for r in range(0, rows, PATCH) for c in range(0, cols, wide)]


def side_by_side(value):
    return jnp.concatenate([value[i : i + PATCH] for i in range(0, value.shape[0], PATCH)], axis=1)


def forward(pixels, pairs, tables_ref):
    right = dot(pixels, pairs[0]) + dot(pixels, pairs[1])
    return left_transform(tables_ref[4], tables_ref[5], side_by_side(right))


def image_spectra(image_ref, pairs, tables_ref):
    pixels = jnp.concatenate([image_ref[window] for window in windows(*image_ref.shape)], axis=0)
    return forward(pixels, pairs, tables_ref)


def near_kernel(image_ref, tables_ref, spec_out, pairs_out):
    pairs = pair_tables(tables_ref)
    for index, pair in enumerate(pairs):
        pairs_out[index] = pair
    spec_out[...] = image_spectra(image_ref, pairs, tables_ref)


def own_kernel(image_ref, pairs_ref, tables_ref, spec_out):
    spec_out[...] = image_spectra(image_ref, pairs_ref, tables_ref)


def rows_kernel(up_ref, own_ref, down_ref, out_ref):
    nodes = own_ref.shape[0]
    out_ref[:SWEEPS] = up_ref[nodes - SWEEPS :]
    out_ref[SWEEPS : SWEEPS + nodes] = own_ref[...]
    out_ref[SWEEPS + nodes :] = down_ref[:SWEEPS]


def flows_kernel(
    far_ref, edge_ref, own_spec, near_spec, rights_ref, tables_ref, out_ref, stats_ref
):
    wide = 2 * PATCH
    spots = windows(*far_ref.shape)
    blocks = len(spots)
    patches = 2 * blocks
    at_edge = lax.axis_index("gz") == 0
    at_even = lax.axis_index("gz") % 2 == 0
    pixels = jnp.concatenate(
        [jnp.where(at_edge, edge_ref[spot].astype(F32), far_ref[spot].astype(F32)).astype(BF16) for spot in spots], axis=0
    )
    spec = forward(pixels, rights_ref, tables_ref)
    products = []
    for block in range(blocks):
        lanes = slice(block * wide, (block + 1) * wide)
        far, near = spec[:, lanes], near_spec[:, lanes]
        operand = cross_operand(jnp.where(at_even, far, near))
        products.append(cross(operand, own_spec[:, lanes]))
        products.append(cross(operand, jnp.where(at_even, near, far)))
    singles = [single for product in products for single in single_patches(product)]
    both = dot(jnp.concatenate(halves(jnp.concatenate(singles, axis=0)), axis=1), rights_ref[2])
    back = both[:, :PATCH] + both[:, PATCH:]
    scores = left_transform(tables_ref[6], tables_ref[7], side_by_side(back))
    groups = scores.reshape(PATCH // 8, 8, 2 * blocks * wide)
    peak = jnp.max(groups, axis=0)
    total = jnp.zeros_like(peak)
    moment = jnp.zeros_like(peak)
    for group in range(PATCH // 8):
        weight = jnp.exp(groups[group] - peak)
        shift = 8 * group - (PATCH if group >= PATCH // 16 else 0)
        total = total + weight
        moment = moment + float(shift) * weight
    for block in range(blocks):
        for pair in range(2):
            for side in range(2):
                at = (2 * block + pair) * 2 + side
                lanes = slice(at * PATCH, (at + 1) * PATCH)
                slot = pair * patches + 2 * block + side
                stats_ref[0, slot] = peak[:, lanes]
                stats_ref[1, slot] = total[:, lanes]
                stats_ref[2, slot] = moment[:, lanes]
    peak = stats_ref[0]
    best = jnp.max(jnp.max(peak, axis=1, keepdims=True), axis=2, keepdims=True)
    scale = jnp.exp(peak - best)
    total = scale * stats_ref[1]
    within = lax.broadcasted_iota(jnp.int32, peak.shape, 1).astype(F32)
    moment = scale * stats_ref[2] + within * total
    total = jnp.sum(total, axis=1)
    lane = lax.broadcasted_iota(jnp.int32, total.shape, 1)
    signed = jnp.where(lane < HALF, lane, lane - PATCH).astype(F32)
    mass = jnp.sum(total, axis=1, keepdims=True) * STRIDE
    along_rows = jnp.sum(jnp.sum(moment, axis=1), axis=1, keepdims=True) / mass
    along_cols = jnp.sum(total * signed, axis=1, keepdims=True) / mass
    values = (
        along_rows[:patches],
        along_cols[:patches],
        along_rows[patches:] - along_rows[:patches],
        along_cols[patches:] - along_cols[:patches],
    )
    lane = lax.broadcasted_iota(jnp.int32, (patches, PATCH), 1)
    patch = lax.broadcasted_iota(jnp.int32, (patches, PATCH), 0)
    lines = []
    for first, second in (values[:2], values[2:]):
        line = jnp.where(lane == patch, first, jnp.where(lane == patches + patch, second, 0.0))
        lines.append(jnp.sum(line, axis=0, keepdims=True))
    line = lax.broadcasted_iota(jnp.int32, out_ref.shape, 0)
    out_ref[...] = jnp.where(line == 0, lines[0], lines[1])


VMEM = pl.BlockSpec(memory_space=pltpu.VMEM)
PARAMS = pltpu.CompilerParams(vmem_limit_bytes=40 * 2**20)


def spec_shape(image):
    return jax.ShapeDtypeStruct((PATCH, image.shape[0] // PATCH * image.shape[1]), F32)


def near_spectra(near, tables):
    pairs = jax.ShapeDtypeStruct((3, 2 * PATCH, 2 * PATCH), BF16)
    return pl.pallas_call(
        near_kernel,
        out_shape=(spec_shape(near), pairs),
        in_specs=[VMEM] * 2,
        out_specs=(VMEM, VMEM),
        compiler_params=PARAMS,
        cost_estimate=pl.CostEstimate(flops=2 * 10**9, bytes_accessed=2 * 2**20, transcendentals=0),
        name="near_spectra",
    )(near, tables)


def own_spectra(own, pairs, tables):
    return pl.pallas_call(
        own_kernel,
        out_shape=spec_shape(own),
        in_specs=[VMEM] * 3,
        out_specs=VMEM,
        compiler_params=PARAMS,
        cost_estimate=pl.CostEstimate(flops=10**9, bytes_accessed=2 * 2**20, transcendentals=0),
        name="own_spectra",
    )(own, pairs, tables)


def anchor_rows(up, own, down):
    nodes = own.shape[0]
    return pl.pallas_call(
        rows_kernel,
        out_shape=jax.ShapeDtypeStruct((nodes + 2 * SWEEPS, nodes), F32),
        in_specs=[VMEM] * 3,
        out_specs=VMEM,
        compiler_params=pltpu.CompilerParams(vmem_limit_bytes=2**20),
        name="anchor_rows",
    )(up, own, down)


def flows(far, edge, own_spec, near_spec, pairs, tables):
    patches = far.shape[0] // PATCH * (far.shape[1] // PATCH)
    return pl.pallas_call(
        flows_kernel,
        out_shape=jax.ShapeDtypeStruct((8, PATCH), F32),
        in_specs=[VMEM] * 6,
        out_specs=VMEM,
        scratch_shapes=[pltpu.VMEM((3, 2 * patches, 8, PATCH), F32)],
        compiler_params=PARAMS,
        cost_estimate=pl.CostEstimate(flops=4 * 10**9, bytes_accessed=3 * 2**20, transcendentals=0),
        name="flows",
    )(far, edge, own_spec, near_spec, pairs, tables)


def spread_weights(nodes, patches):
    node_pos = (np.arange(nodes) + 0.5) * STRIDE / PATCH - 0.5
    weights = np.maximum(0.0, 1.0 - np.abs(node_pos[:, None] - np.arange(patches)[None, :]))
    return weights / weights.sum(axis=1, keepdims=True)


def ring_nodes(nodes):
    span = np.arange(nodes + 2 * SWEEPS) - SWEEPS
    ring = np.concatenate([span[SWEEPS:], span, span[:SWEEPS]])
    part = np.zeros(len(ring), np.int32)
    part[nodes + SWEEPS : len(ring) - SWEEPS] = 1
    order = np.arange(len(ring)).reshape(PATCH, -1).T.reshape(-1)
    return (ring[order], part[order])


def row_nodes(nodes):
    span = np.arange(nodes + 2 * SWEEPS) - SWEEPS
    return span.reshape(8, -1).T.reshape(-1)


def target_tables(nodes, patches):
    ring, _ = ring_nodes(nodes)
    spread = spread_weights(nodes, patches)

    def wide(positions):
        table = np.zeros((len(positions), 3, patches))
        for tile in range(3):
            at = positions - (tile - 1) * nodes
            hit = (at >= 0) & (at < nodes)
            table[hit, tile] = spread[at[hit]]
        return table

    shape = (3, 3, patches, patches)
    rows = wide(row_nodes(nodes))[:, None, :, :, None]
    cols = wide(ring).transpose(1, 2, 0)[:, None, None]
    left = np.broadcast_to(rows, (rows.shape[0],) + shape).reshape(rows.shape[0], -1)
    right = np.broadcast_to(cols, shape + (len(ring),)).reshape(-1, len(ring))
    return (left.astype(BF16), right.astype(BF16))


def ring_tables(nodes):
    ring, part = ring_nodes(nodes)
    place = np.arange(3 * nodes)[:, None] - nodes
    into = (place == ring[None]).astype(BF16)
    column = np.arange(2 * nodes)[None]
    out = ((ring[:, None] == column % nodes) & (part[:, None] == column // nodes)).astype(BF16)
    return (into, out)


def permuted(value, table):
    result = None
    for piece in range(3):
        part = value.astype(BF16)
        moved = dot(part, table)
        result = moved if result is None else result + moved
        value = value - part.astype(F32)
    return result


def ring_place(rows, lanes):
    lane = lax.broadcasted_iota(jnp.int32, (rows, lanes), 1)
    return lane % PATCH * (lanes // PATCH) + lane // PATCH


def tiles_beside(even_ref, odd_ref):
    at_even = lax.axis_index("tx") % 2 == 0
    even, odd = even_ref[...], odd_ref[...]
    return (jnp.where(at_even, odd, even), jnp.where(at_even, even, odd))


def gains_kernel(own_ref, even_ref, odd_ref, into_ref, gain_ref, pull_ref, rows_ref):
    strips = gain_ref.shape[0]
    nodes = own_ref.shape[1]
    before, after = tiles_beside(even_ref, odd_ref)
    weight = permuted(jnp.concatenate([before, own_ref[...], after], axis=1), into_ref[...])
    row_node = lax.broadcasted_iota(jnp.int32, weight.shape, 0) - SWEEPS
    row_node = row_node + lax.axis_index("ty") * nodes
    lanes = into_ref.shape[1]
    place = ring_place(1, lanes)
    shift = jnp.where(place < nodes + SWEEPS, 0, jnp.where(place < lanes - SWEEPS, nodes + 2 * SWEEPS, lanes))
    col_node = place - shift + lax.axis_index("tx") * nodes
    inside = (row_node >= 0) & (row_node < lax.axis_size("ty") * nodes)
    inside = inside & (col_node >= 0) & (col_node < lax.axis_size("tx") * nodes)
    gain = jnp.where(inside, 1.0 / (4.0 + weight), 0.0)
    for value, out in ((gain, gain_ref), (gain * weight, pull_ref)):
        rows_ref[...] = value.reshape(value.shape[0], -1, PATCH).transpose(1, 0, 2)
        for strip in range(strips):
            for tile in range(rows_ref.shape[0]):
                out[strip, :, tile * PATCH : (tile + 1) * PATCH] = rows_ref[tile, pl.ds(strip, 8, strips), :]


def gains(own, even, odd, nodes):
    into, _ = ring_tables(nodes)
    shape = jax.ShapeDtypeStruct((own.shape[0] // 8, 8, into.shape[1]), F32)
    return pl.pallas_call(
        gains_kernel,
        out_shape=(shape, shape),
        in_specs=[VMEM] * 4,
        out_specs=(VMEM, VMEM),
        scratch_shapes=[pltpu.VMEM((into.shape[1] // PATCH, own.shape[0], PATCH), F32)],
        compiler_params=PARAMS,
        cost_estimate=pl.CostEstimate(flops=10**9, bytes_accessed=2**20, transcendentals=0),
        name="gains",
    )(own, even, odd, jnp.asarray(into))


def relax_kernel(
    own_ref, even_ref, odd_ref, gain_ref, pull_ref, left_ref, right_ref, cols_table_ref, rows_table_ref,
    work_ref, landing_ref, base_ref,
):
    strips, _, lanes = work_ref.shape
    nodes = landing_ref.shape[1]
    patches = left_ref.shape[1] // 9
    before, after = tiles_beside(even_ref, odd_ref)
    rows = [before[:3], own_ref[:3], after[:3]]
    rows.append(jnp.zeros((PATCH - 9, PATCH), F32))
    columns = jnp.transpose(jnp.concatenate(rows, axis=0))

    def sources(part):
        lines = slice(part * patches, (part + 1) * patches)
        return jnp.concatenate([columns[lines, i : i + 1] for i in range(9)], axis=0)

    place = ring_place(1, lanes)
    second = (place >= nodes + SWEEPS) & (place < lanes - SWEEPS)
    spread = jnp.where(second, sources(1), sources(0)) * right_ref[...].astype(F32)
    target = None
    for piece in range(3):
        part = spread.astype(BF16)
        term = dot(left_ref[...], part)
        target = term if target is None else target + term
        spread = spread - part.astype(F32)
    target = target.reshape(strips, 8, lanes)
    base_ref[...] = pull_ref[...] * target
    work_ref[...] = jnp.where(gain_ref[...] > 0.0, target, 0.0)
    tiles = lanes // PATCH

    def row(strip):
        return [work_ref[strip, :, i * PATCH : (i + 1) * PATCH] for i in range(tiles)]

    def sweep(counter, carry):
        here = row(0)
        above = [pltpu.roll(value, 1, 0) for value in row(strips - 1)]
        around = [pltpu.roll(value, 7, 0) for value in here]
        for strip in range(strips):
            below = row(strip + 1) if strip + 1 < strips else around
            ring = [pltpu.roll(here[-1], 1, 1)] + here + [pltpu.roll(here[0], PATCH - 1, 1)]
            for tile in range(tiles):
                at = (strip, slice(None), slice(tile * PATCH, (tile + 1) * PATCH))
                total = (above[tile] + below[tile]) + (ring[tile] + ring[tile + 2])
                work_ref[at] = gain_ref[at] * total + base_ref[at]
            above, here = here, below
        return carry

    lax.fori_loop(0, SWEEPS, sweep, 0, unroll=16)
    mesh = work_ref[...].reshape(strips * 8, lanes)
    ones = jnp.where(ring_place(16, lanes) < nodes, 1.0, 0.0).astype(BF16)
    sums = None
    for piece in range(3):
        part = mesh.astype(BF16)
        term = lax.dot_general(ones, part, (((1,), (1,)), ((), ())), preferred_element_type=F32)
        sums = term if sums is None else sums + term
        mesh = mesh - part.astype(F32)
    down_mean = permuted(sums, rows_table_ref[...])[:1] / nodes
    strip = lax.broadcasted_iota(jnp.int32, (strips, 8, lanes), 0)
    row = lax.broadcasted_iota(jnp.int32, (strips, 8, lanes), 1) * strips + strip
    kept = jnp.where((row >= SWEEPS) & (row < SWEEPS + nodes), work_ref[...], 0.0)
    across = permuted(jnp.sum(kept, axis=0), cols_table_ref[...])
    across_mean = jnp.sum(across, axis=0, keepdims=True) / nodes
    line = lax.broadcasted_iota(jnp.int32, landing_ref.shape, 0)
    ramp = lax.broadcasted_iota(jnp.int32, landing_ref.shape, 1).astype(F32)
    profile = jnp.where(line == 0, down_mean, across_mean)
    landing_ref[...] = jnp.clip(ramp + profile, 0.0, nodes - 1.0)


def relax(targets, weights, nodes, patches):
    left, right = target_tables(nodes, patches)
    ring, ring_part = ring_nodes(nodes)
    node = np.arange(nodes)[None]
    cols_table = ((ring[:, None] == node) & (ring_part[:, None] == 1)).astype(BF16)
    rows_table = (row_nodes(nodes)[:, None] == node).astype(BF16)
    tables = map(jnp.asarray, (left, right, cols_table, rows_table))
    shape = weights[0].shape
    return pl.pallas_call(
        relax_kernel,
        out_shape=(jax.ShapeDtypeStruct(shape, F32), jax.ShapeDtypeStruct((8, nodes), F32)),
        in_specs=[VMEM] * 9,
        out_specs=(VMEM, VMEM),
        scratch_shapes=[pltpu.VMEM(shape, F32)],
        compiler_params=PARAMS,
        cost_estimate=pl.CostEstimate(flops=4 * 10**9, bytes_accessed=3 * 2**20, transcendentals=0),
        name="relax",
    )(*targets, *weights, *tables)


def mesh_kernel(ring_ref, table_ref, mesh_ref, rows_ref):
    strips, _, lanes = ring_ref.shape
    nodes = mesh_ref.shape[2]
    final = permuted(ring_ref[...].reshape(strips * 8, lanes), table_ref[...])
    for strip in range(strips):
        for part in range(2):
            columns = slice(part * nodes, (part + 1) * nodes)
            rows_ref[part, pl.ds(strip, 8, strips), :] = final[8 * strip : 8 * strip + 8, columns]
    mesh_ref[0] = rows_ref[:, SWEEPS : SWEEPS + nodes]


def natural_mesh(ring, nodes):
    _, table = ring_tables(nodes)
    return pl.pallas_call(
        mesh_kernel,
        out_shape=jax.ShapeDtypeStruct((1, 2, nodes, nodes), F32),
        in_specs=[VMEM] * 2,
        out_specs=VMEM,
        scratch_shapes=[pltpu.VMEM((2, ring.shape[0] * 8, nodes), F32)],
        compiler_params=PARAMS,
        cost_estimate=pl.CostEstimate(flops=10**9, bytes_accessed=2**20, transcendentals=0),
        name="natural_mesh",
    )(ring, jnp.asarray(table))


def compose_kernel(*refs):
    *landing_refs, out_ref = refs
    count = len(landing_refs)
    section = lax.axis_index("gz")
    received = [ref[...] for ref in landing_refs]
    nodes = received[0].shape[1]
    ramp = lax.broadcasted_iota(jnp.int32, received[0].shape, 1).astype(F32)
    value = received[0]
    for other in range(count - 2, -1, -1):
        landing = received[0]
        for code in range(1, count):
            landing = jnp.where(section == other ^ code, received[code], landing)
        floor = jnp.minimum(jnp.floor(landing), nodes - 2.0)
        index = floor.astype(jnp.int32)
        share = landing - floor
        below = jnp.take_along_axis(value, index, axis=1)
        above = jnp.take_along_axis(value, index + 1, axis=1)
        value = jnp.where(section > other, (1.0 - share) * below + share * above, value)
    out_ref[0, 0, 0] = (value - ramp)[:2]


def compose(landings):
    nodes = landings[0].shape[1]
    return pl.pallas_call(
        compose_kernel,
        out_shape=jax.ShapeDtypeStruct((1, 1, 1, 2, nodes), F32),
        in_specs=[VMEM] * len(landings),
        out_specs=VMEM,
        compiler_params=pltpu.CompilerParams(vmem_limit_bytes=2**20),
        name="compose",
    )(*landings)


def swap_pairs(value, axis, first, spare):
    count, other = lax.axis_size(axis), lax.axis_size(spare)
    axes = ("gz", "ty", "tx")
    flip = axes.index(axis) > axes.index(spare)

    def place(here, beside):
        return beside * count + here if flip else here * other + beside

    moves = []
    for here in range(count):
        there = ((here + first) ^ 1) - first
        for beside in range(other):
            target = place(there, beside) if 0 <= there < count else place(here, beside ^ 1)
            moves.append((place(here, beside), target))
    return lax.ppermute(value, (spare, axis) if flip else (axis, spare), moves)


def rows_beside(value):
    count = lax.axis_size("ty")
    if count == 2:
        other = swap_pairs(value, "ty", 0, "gz")
        return (other, other)
    even = swap_pairs(value, "ty", 0, "gz")
    odd = swap_pairs(value, "ty", 1, "gz")
    at_even = lax.axis_index("ty") % 2 == 0
    return (jnp.where(at_even, odd, even), jnp.where(at_even, even, odd))


def to_next(value, turn):
    count, rows = lax.axis_size("gz"), lax.axis_size("ty")
    if not turn:
        return lax.ppermute(value, "gz", [(i, (i + 1) % count) for i in range(count)])
    moves = [(i * rows + j, (i + 1) % count * rows + (j ^ 1)) for i in range(count) for j in range(rows)]
    return lax.ppermute(value, ("gz", "ty"), moves)


def patch_targets(flow):
    first = lax.axis_index("gz") <= 1
    before = to_next(flow, 0)

    def target(near, earlier):
        return jnp.where(first, near[0:1], 0.5 * (near[0:1] + earlier[1:2]))

    if lax.axis_size("ty") == 2:
        beside = target(rows_beside(flow)[0], to_next(flow, 1))
        lines = [beside, target(flow, before), beside]
    else:
        (up, down), (up_before, down_before) = rows_beside(flow), rows_beside(before)
        lines = [target(up, up_before), target(flow, before), target(down, down_before)]
    return jnp.concatenate(lines + [jnp.zeros((5, flow.shape[1]), F32)], axis=0)


def local(images, boundary, anchor):
    nodes = anchor.shape[1]
    own = images[0]
    patches = own.shape[0] // PATCH
    sections = lax.axis_size("gz")
    tables = transform_tables()
    far = swap_pairs(own, "gz", 1, "ty")
    near = swap_pairs(own, "gz", 0, "ty")
    up, down = rows_beside(anchor[0])
    near_spec, pairs = near_spectra(near, tables)
    own_spec = own_spectra(own, pairs, tables)
    far, own_spec, near_spec = lax.optimization_barrier((far, own_spec, near_spec))
    flow = flows(far, boundary, own_spec, near_spec, pairs, tables)
    flow, up, down = lax.optimization_barrier((flow, up, down))
    rows = anchor_rows(up, anchor[0], down)
    weights = gains(rows, swap_pairs(rows, "tx", 0, "gz"), swap_pairs(rows, "tx", 1, "gz"), nodes)
    line = patch_targets(flow)
    targets = (line, swap_pairs(line, "tx", 0, "gz"), swap_pairs(line, "tx", 1, "gz"))
    ring, landing = relax(targets, weights, nodes, patches)
    landings = [landing]
    for code in range(1, sections):
        landings.append(lax.ppermute(landing, "gz", [(i, i ^ code) for i in range(sections)]))
    mesh = natural_mesh(ring, nodes)
    mesh, landings = lax.optimization_barrier((mesh, landings))
    drift = compose(landings)
    return (mesh, drift)


def solution(mesh):
    return jax.shard_map(
        local,
        mesh=mesh,
        in_specs=(P("gz", "ty", "tx"), P("ty", "tx"), P("gz", "ty", "tx")),
        out_specs=(P("gz", None, "ty", "tx"), P("gz", "ty", "tx", None, None)),
        check_vma=False,
    )
```

```python
import math

import jax
import jax.numpy as jnp
import numpy as np
from jax import lax
from jax.experimental import pallas as pl
from jax.experimental.pallas import tpu as pltpu
from jax.sharding import PartitionSpec as P

PATCH = 128
STRIDE = 4
SWEEPS = 32
HALF = PATCH // 2
BF16 = jnp.bfloat16
F32 = jnp.float32


def split_table(table):
    high = table.astype(BF16)
    low = (table - high.astype(np.float64)).astype(BF16)
    return (high, low)


def transform_tables():
    counter = np.arange(PATCH)
    phase = (counter[:, None] * counter[None, :] % PATCH) * (2.0 * math.pi / PATCH)
    basis = np.concatenate([np.cos(phase[:HALF]), np.sin(phase[:HALF])])
    basis[HALF] = np.cos(phase[HALF])
    gains = np.full(PATCH, 2.0)
    gains[0] = gains[HALF] = 1.0
    inverse = basis.T * gains / PATCH
    tables = [part for table in (basis.T, inverse.T, basis, inverse / PATCH) for part in split_table(table)]
    return jnp.asarray(np.stack(tables))


def product_tables(tables_ref):
    forward_table = jnp.concatenate([tables_ref[0], tables_ref[1]], axis=1)
    inverse = jnp.concatenate([tables_ref[2], tables_ref[3]], axis=1)
    return [forward_table, jnp.concatenate([inverse, inverse], axis=0)]


def paired_patches(first, second):
    lower = lax.broadcasted_iota(jnp.int32, (PATCH, PATCH), 1) < HALF
    cosine = jnp.where(lower, first, pltpu.roll(second, HALF, 1))
    sine = jnp.where(lower, pltpu.roll(first, HALF, 1), second)
    return [cosine, sine]


def single_patches(product):
    lower = lax.broadcasted_iota(jnp.int32, (PATCH, PATCH), 1) < HALF
    cosine, sine = product[:, :PATCH], product[:, PATCH:]
    first = jnp.where(lower, cosine, pltpu.roll(sine, HALF, 1))
    second = jnp.where(lower, pltpu.roll(cosine, HALF, 1), sine)
    return [first, second]


def halves(value):
    high = value.astype(BF16)
    return (high, (value - high.astype(F32)).astype(BF16))


def dot(left, right):
    return jnp.dot(left, right, preferred_element_type=F32)


def left_transform(table_high, table_low, value):
    high, low = halves(value)
    table = jnp.concatenate([table_high, table_high, table_low], axis=1)
    return dot(table, jnp.concatenate([high, low, high], axis=0))


def quarters(spec):
    return (
        (spec[:HALF, :PATCH], spec[:HALF, PATCH:]),
        (spec[HALF:, :PATCH], spec[HALF:, PATCH:]),
    )


def cross_operand(spec):
    (cc, cs), (sc, ss) = quarters(spec)
    first_row = lax.broadcasted_iota(jnp.int32, (HALF, PATCH), 0) == 0
    first_lane = lax.broadcasted_iota(jnp.int32, (HALF, PATCH), 1) % HALF == 0

    def lanes(cosine, sine):
        return (cosine, jnp.where(first_lane, sine, cosine), jnp.where(first_lane, 0.0, sine))

    return (
        lanes(cc, cs),
        lanes(jnp.where(first_row, sc, cc), jnp.where(first_row, ss, cs)),
        lanes(jnp.where(first_row, 0.0, sc), jnp.where(first_row, 0.0, ss)),
    )


def cross(operand, spec):
    (row_c, row_d, row_s) = operand
    (bc, bs) = quarters(spec)

    def cosine(a, b):
        return a[0] * b[0] + a[2] * b[1]

    def sine(a, b):
        return a[1] * b[1] - a[2] * b[0]

    cc = cosine(row_c, bc) + cosine(row_s, bs)
    cs = sine(row_c, bc) + sine(row_s, bs)
    sc = cosine(row_d, bs) - cosine(row_s, bc)
    ss = sine(row_d, bs) - sine(row_s, bc)
    return jnp.concatenate(
        [jnp.concatenate([cc, cs], axis=1), jnp.concatenate([sc, ss], axis=1)], axis=0
    )


def windows(rows, cols):
    return [(slice(r, r + PATCH), slice(c, c + PATCH)) for r in range(0, rows, PATCH) for c in range(0, cols, PATCH)]


def side_by_side(value):
    return jnp.concatenate([value[i : i + PATCH] for i in range(0, value.shape[0], PATCH)], axis=1)


def forward(pixels, table, tables_ref):
    both = dot(pixels, table)
    right = both[:, :PATCH] + both[:, PATCH:]
    singles = [right[i : i + PATCH] for i in range(0, right.shape[0], PATCH)]
    tiles = [tile for i in range(0, len(singles), 2) for tile in paired_patches(*singles[i : i + 2])]
    return left_transform(tables_ref[4], tables_ref[5], jnp.concatenate(tiles, axis=1))


def image_spectra(image_ref, table, tables_ref):
    pixels = jnp.concatenate([image_ref[window] for window in windows(*image_ref.shape)], axis=0)
    return forward(pixels, table, tables_ref)


def near_kernel(image_ref, tables_ref, spec_out, forward_out, inverse_out):
    table, inverse = product_tables(tables_ref)
    forward_out[...] = table
    inverse_out[...] = inverse
    spec_out[...] = image_spectra(image_ref, table, tables_ref)


def own_kernel(image_ref, forward_ref, tables_ref, spec_out):
    spec_out[...] = image_spectra(image_ref, forward_ref[...], tables_ref)


def rows_kernel(up_ref, own_ref, down_ref, out_ref):
    nodes = own_ref.shape[0]
    out_ref[:SWEEPS] = up_ref[nodes - SWEEPS :]
    out_ref[SWEEPS : SWEEPS + nodes] = own_ref[...]
    out_ref[SWEEPS + nodes :] = down_ref[:SWEEPS]


def flows_kernel(
    far_ref, edge_ref, own_spec, near_spec, forward_ref, inverse_ref, tables_ref, out_ref, stats_ref
):
    wide = 2 * PATCH
    spots = windows(*far_ref.shape)
    patches = len(spots)
    blocks = patches // 2
    at_edge = lax.axis_index("gz") == 0
    at_even = lax.axis_index("gz") % 2 == 0
    pixels = jnp.concatenate(
        [jnp.where(at_edge, edge_ref[spot].astype(F32), far_ref[spot].astype(F32)).astype(BF16) for spot in spots], axis=0
    )
    spec = forward(pixels, forward_ref[...], tables_ref)
    products = []
    for block in range(blocks):
        lanes = slice(block * wide, (block + 1) * wide)
        far, near = spec[:, lanes], near_spec[:, lanes]
        operand = cross_operand(jnp.where(at_even, far, near))
        products.append(cross(operand, own_spec[:, lanes]))
        products.append(cross(operand, jnp.where(at_even, near, far)))
    singles = [single for product in products for single in single_patches(product)]
    both = dot(jnp.concatenate(halves(jnp.concatenate(singles, axis=0)), axis=1), inverse_ref[...])
    back = both[:, :PATCH] + both[:, PATCH:]
    scores = left_transform(tables_ref[6], tables_ref[7], side_by_side(back))
    groups = scores.reshape(PATCH // 8, 8, 2 * blocks * wide)
    peak = jnp.max(groups, axis=0)
    total = jnp.zeros_like(peak)
    moment = jnp.zeros_like(peak)
    for group in range(PATCH // 8):
        weight = jnp.exp(groups[group] - peak)
        shift = 8 * group - (PATCH if group >= PATCH // 16 else 0)
        total = total + weight
        moment = moment + float(shift) * weight
    for block in range(blocks):
        for pair in range(2):
            for side in range(2):
                at = (2 * block + pair) * 2 + side
                lanes = slice(at * PATCH, (at + 1) * PATCH)
                slot = pair * patches + 2 * block + side
                stats_ref[0, slot] = peak[:, lanes]
                stats_ref[1, slot] = total[:, lanes]
                stats_ref[2, slot] = moment[:, lanes]
    peak = stats_ref[0]
    best = jnp.max(jnp.max(peak, axis=1, keepdims=True), axis=2, keepdims=True)
    scale = jnp.exp(peak - best)
    total = scale * stats_ref[1]
    within = lax.broadcasted_iota(jnp.int32, peak.shape, 1).astype(F32)
    moment = scale * stats_ref[2] + within * total
    total = jnp.sum(total, axis=1)
    lane = lax.broadcasted_iota(jnp.int32, total.shape, 1)
    signed = jnp.where(lane < HALF, lane, lane - PATCH).astype(F32)
    mass = jnp.sum(total, axis=1, keepdims=True) * STRIDE
    along_rows = jnp.sum(jnp.sum(moment, axis=1), axis=1, keepdims=True) / mass
    along_cols = jnp.sum(total * signed, axis=1, keepdims=True) / mass
    values = (
        along_rows[:patches],
        along_cols[:patches],
        along_rows[patches:] - along_rows[:patches],
        along_cols[patches:] - along_cols[:patches],
    )
    lane = lax.broadcasted_iota(jnp.int32, (patches, PATCH), 1)
    patch = lax.broadcasted_iota(jnp.int32, (patches, PATCH), 0)
    lines = []
    for first, second in (values[:2], values[2:]):
        line = jnp.where(lane == patch, first, jnp.where(lane == patches + patch, second, 0.0))
        lines.append(jnp.sum(line, axis=0, keepdims=True))
    line = lax.broadcasted_iota(jnp.int32, out_ref.shape, 0)
    out_ref[...] = jnp.where(line == 0, lines[0], lines[1])


VMEM = pl.BlockSpec(memory_space=pltpu.VMEM)
PARAMS = pltpu.CompilerParams(vmem_limit_bytes=40 * 2**20)


def spec_shape(image):
    return jax.ShapeDtypeStruct((PATCH, image.shape[0] // PATCH * image.shape[1]), F32)


def near_spectra(near, tables):
    forward_table = jax.ShapeDtypeStruct((PATCH, 2 * PATCH), BF16)
    inverse_table = jax.ShapeDtypeStruct((2 * PATCH, 2 * PATCH), BF16)
    return pl.pallas_call(
        near_kernel,
        out_shape=(spec_shape(near), forward_table, inverse_table),
        in_specs=[VMEM] * 2,
        out_specs=(VMEM,) * 3,
        compiler_params=PARAMS,
        cost_estimate=pl.CostEstimate(flops=2 * 10**9, bytes_accessed=2 * 2**20, transcendentals=0),
        name="near_spectra",
    )(near, tables)


def own_spectra(own, forward_table, tables):
    return pl.pallas_call(
        own_kernel,
        out_shape=spec_shape(own),
        in_specs=[VMEM] * 3,
        out_specs=VMEM,
        compiler_params=PARAMS,
        cost_estimate=pl.CostEstimate(flops=10**9, bytes_accessed=2 * 2**20, transcendentals=0),
        name="own_spectra",
    )(own, forward_table, tables)


def anchor_rows(up, own, down):
    nodes = own.shape[0]
    return pl.pallas_call(
        rows_kernel,
        out_shape=jax.ShapeDtypeStruct((nodes + 2 * SWEEPS, nodes), F32),
        in_specs=[VMEM] * 3,
        out_specs=VMEM,
        compiler_params=pltpu.CompilerParams(vmem_limit_bytes=2**20),
        name="anchor_rows",
    )(up, own, down)


def flows(far, edge, own_spec, near_spec, pairs, tables):
    forward_table, inverse_table = pairs
    patches = far.shape[0] // PATCH * (far.shape[1] // PATCH)
    return pl.pallas_call(
        flows_kernel,
        out_shape=jax.ShapeDtypeStruct((8, PATCH), F32),
        in_specs=[VMEM] * 7,
        out_specs=VMEM,
        scratch_shapes=[pltpu.VMEM((3, 2 * patches, 8, PATCH), F32)],
        compiler_params=PARAMS,
        cost_estimate=pl.CostEstimate(flops=4 * 10**9, bytes_accessed=3 * 2**20, transcendentals=0),
        name="flows",
    )(far, edge, own_spec, near_spec, forward_table, inverse_table, tables)


def spread_weights(nodes, patches):
    node_pos = (np.arange(nodes) + 0.5) * STRIDE / PATCH - 0.5
    weights = np.maximum(0.0, 1.0 - np.abs(node_pos[:, None] - np.arange(patches)[None, :]))
    return weights / weights.sum(axis=1, keepdims=True)


def ring_nodes(nodes):
    span = np.arange(nodes + 2 * SWEEPS) - SWEEPS
    ring = np.concatenate([span[SWEEPS:], span, span[:SWEEPS]])
    part = np.zeros(len(ring), np.int32)
    part[nodes + SWEEPS : len(ring) - SWEEPS] = 1
    order = np.arange(len(ring)).reshape(PATCH, -1).T.reshape(-1)
    return (ring[order], part[order])


def row_nodes(nodes):
    span = np.arange(nodes + 2 * SWEEPS) - SWEEPS
    return span.reshape(8, -1).T.reshape(-1)


def target_tables(nodes, patches):
    ring, _ = ring_nodes(nodes)
    spread = spread_weights(nodes, patches)

    def wide(positions):
        table = np.zeros((len(positions), 3, patches))
        for tile in range(3):
            at = positions - (tile - 1) * nodes
            hit = (at >= 0) & (at < nodes)
            table[hit, tile] = spread[at[hit]]
        return table

    shape = (3, 3, patches, patches)
    rows = wide(row_nodes(nodes))[:, None, :, :, None]
    cols = wide(ring).transpose(1, 2, 0)[:, None, None]
    left = np.broadcast_to(rows, (rows.shape[0],) + shape).reshape(rows.shape[0], -1)
    right = np.broadcast_to(cols, shape + (len(ring),)).reshape(-1, len(ring))
    return (left.astype(BF16), right.astype(BF16))


def ring_tables(nodes):
    ring, part = ring_nodes(nodes)
    place = np.arange(3 * nodes)[:, None] - nodes
    into = (place == ring[None]).astype(BF16)
    column = np.arange(2 * nodes)[None]
    out = ((ring[:, None] == column % nodes) & (part[:, None] == column // nodes)).astype(BF16)
    return (into, out)


def permuted(value, table):
    result = None
    for piece in range(3):
        part = value.astype(BF16)
        moved = dot(part, table)
        result = moved if result is None else result + moved
        value = value - part.astype(F32)
    return result


def ring_place(rows, lanes):
    lane = lax.broadcasted_iota(jnp.int32, (rows, lanes), 1)
    return lane % PATCH * (lanes // PATCH) + lane // PATCH


def tiles_beside(even_ref, odd_ref):
    at_even = lax.axis_index("tx") % 2 == 0
    even, odd = even_ref[...], odd_ref[...]
    return (jnp.where(at_even, odd, even), jnp.where(at_even, even, odd))


def gains_kernel(own_ref, even_ref, odd_ref, into_ref, gain_ref, pull_ref, rows_ref):
    strips = gain_ref.shape[0]
    nodes = own_ref.shape[1]
    before, after = tiles_beside(even_ref, odd_ref)
    weight = permuted(jnp.concatenate([before, own_ref[...], after], axis=1), into_ref[...])
    row_node = lax.broadcasted_iota(jnp.int32, weight.shape, 0) - SWEEPS
    row_node = row_node + lax.axis_index("ty") * nodes
    lanes = into_ref.shape[1]
    place = ring_place(1, lanes)
    shift = jnp.where(place < nodes + SWEEPS, 0, jnp.where(place < lanes - SWEEPS, nodes + 2 * SWEEPS, lanes))
    col_node = place - shift + lax.axis_index("tx") * nodes
    inside = (row_node >= 0) & (row_node < lax.axis_size("ty") * nodes)
    inside = inside & (col_node >= 0) & (col_node < lax.axis_size("tx") * nodes)
    gain = jnp.where(inside, 1.0 / (4.0 + weight), 0.0)
    for value, out in ((gain, gain_ref), (gain * weight, pull_ref)):
        rows_ref[...] = value.reshape(value.shape[0], -1, PATCH).transpose(1, 0, 2)
        for strip in range(strips):
            for tile in range(rows_ref.shape[0]):
                out[strip, :, tile * PATCH : (tile + 1) * PATCH] = rows_ref[tile, pl.ds(strip, 8, strips), :]


def gains(own, even, odd, nodes):
    into, _ = ring_tables(nodes)
    shape = jax.ShapeDtypeStruct((own.shape[0] // 8, 8, into.shape[1]), F32)
    return pl.pallas_call(
        gains_kernel,
        out_shape=(shape, shape),
        in_specs=[VMEM] * 4,
        out_specs=(VMEM, VMEM),
        scratch_shapes=[pltpu.VMEM((into.shape[1] // PATCH, own.shape[0], PATCH), F32)],
        compiler_params=PARAMS,
        cost_estimate=pl.CostEstimate(flops=10**9, bytes_accessed=2**20, transcendentals=0),
        name="gains",
    )(own, even, odd, jnp.asarray(into))


def relax_kernel(
    own_ref, even_ref, odd_ref, gain_ref, pull_ref, left_ref, right_ref, cols_table_ref, rows_table_ref,
    work_ref, landing_ref, base_ref,
):
    strips, _, lanes = work_ref.shape
    nodes = landing_ref.shape[1]
    patches = left_ref.shape[1] // 9
    before, after = tiles_beside(even_ref, odd_ref)
    rows = [before[:3], own_ref[:3], after[:3]]
    rows.append(jnp.zeros((PATCH - 9, PATCH), F32))
    columns = jnp.transpose(jnp.concatenate(rows, axis=0))

    def sources(part):
        lines = slice(part * patches, (part + 1) * patches)
        return jnp.concatenate([columns[lines, i : i + 1] for i in range(9)], axis=0)

    place = ring_place(1, lanes)
    second = (place >= nodes + SWEEPS) & (place < lanes - SWEEPS)
    spread = jnp.where(second, sources(1), sources(0)) * right_ref[...].astype(F32)
    target = None
    for piece in range(3):
        part = spread.astype(BF16)
        term = dot(left_ref[...], part)
        target = term if target is None else target + term
        spread = spread - part.astype(F32)
    target = target.reshape(strips, 8, lanes)
    base_ref[...] = pull_ref[...] * target
    work_ref[...] = jnp.where(gain_ref[...] > 0.0, target, 0.0)
    tiles = lanes // PATCH

    def row(strip):
        return [work_ref[strip, :, i * PATCH : (i + 1) * PATCH] for i in range(tiles)]

    def sweep(counter, carry):
        here = row(0)
        above = [pltpu.roll(value, 1, 0) for value in row(strips - 1)]
        around = [pltpu.roll(value, 7, 0) for value in here]
        for strip in range(strips):
            below = row(strip + 1) if strip + 1 < strips else around
            ring = [pltpu.roll(here[-1], 1, 1)] + here + [pltpu.roll(here[0], PATCH - 1, 1)]
            for tile in range(tiles):
                at = (strip, slice(None), slice(tile * PATCH, (tile + 1) * PATCH))
                total = (above[tile] + below[tile]) + (ring[tile] + ring[tile + 2])
                work_ref[at] = gain_ref[at] * total + base_ref[at]
            above, here = here, below
        return carry

    lax.fori_loop(0, SWEEPS, sweep, 0, unroll=32)
    mesh = work_ref[...].reshape(strips * 8, lanes)
    ones = jnp.where(ring_place(16, lanes) < nodes, 1.0, 0.0).astype(BF16)
    sums = None
    for piece in range(3):
        part = mesh.astype(BF16)
        term = lax.dot_general(ones, part, (((1,), (1,)), ((), ())), preferred_element_type=F32)
        sums = term if sums is None else sums + term
        mesh = mesh - part.astype(F32)
    down_mean = permuted(sums, rows_table_ref[...])[:1] / nodes
    strip = lax.broadcasted_iota(jnp.int32, (strips, 8, lanes), 0)
    row = lax.broadcasted_iota(jnp.int32, (strips, 8, lanes), 1) * strips + strip
    kept = jnp.where((row >= SWEEPS) & (row < SWEEPS + nodes), work_ref[...], 0.0)
    across = permuted(jnp.sum(kept, axis=0), cols_table_ref[...])
    across_mean = jnp.sum(across, axis=0, keepdims=True) / nodes
    line = lax.broadcasted_iota(jnp.int32, landing_ref.shape, 0)
    ramp = lax.broadcasted_iota(jnp.int32, landing_ref.shape, 1).astype(F32)
    profile = jnp.where(line == 0, down_mean, across_mean)
    landing_ref[...] = jnp.clip(ramp + profile, 0.0, nodes - 1.0)


def relax(targets, weights, nodes, patches):
    left, right = target_tables(nodes, patches)
    ring, ring_part = ring_nodes(nodes)
    node = np.arange(nodes)[None]
    cols_table = ((ring[:, None] == node) & (ring_part[:, None] == 1)).astype(BF16)
    rows_table = (row_nodes(nodes)[:, None] == node).astype(BF16)
    tables = map(jnp.asarray, (left, right, cols_table, rows_table))
    shape = weights[0].shape
    return pl.pallas_call(
        relax_kernel,
        out_shape=(jax.ShapeDtypeStruct(shape, F32), jax.ShapeDtypeStruct((8, nodes), F32)),
        in_specs=[VMEM] * 9,
        out_specs=(VMEM, VMEM),
        scratch_shapes=[pltpu.VMEM(shape, F32)],
        compiler_params=PARAMS,
        cost_estimate=pl.CostEstimate(flops=4 * 10**9, bytes_accessed=3 * 2**20, transcendentals=0),
        name="relax",
    )(*targets, *weights, *tables)


def mesh_kernel(ring_ref, table_ref, mesh_ref, rows_ref):
    strips, _, lanes = ring_ref.shape
    nodes = mesh_ref.shape[2]
    final = permuted(ring_ref[...].reshape(strips * 8, lanes), table_ref[...])
    for strip in range(strips):
        for part in range(2):
            columns = slice(part * nodes, (part + 1) * nodes)
            rows_ref[part, pl.ds(strip, 8, strips), :] = final[8 * strip : 8 * strip + 8, columns]
    mesh_ref[0] = rows_ref[:, SWEEPS : SWEEPS + nodes]


def natural_mesh(ring, nodes):
    _, table = ring_tables(nodes)
    return pl.pallas_call(
        mesh_kernel,
        out_shape=jax.ShapeDtypeStruct((1, 2, nodes, nodes), F32),
        in_specs=[VMEM] * 2,
        out_specs=VMEM,
        scratch_shapes=[pltpu.VMEM((2, ring.shape[0] * 8, nodes), F32)],
        compiler_params=PARAMS,
        cost_estimate=pl.CostEstimate(flops=10**9, bytes_accessed=2**20, transcendentals=0),
        name="natural_mesh",
    )(ring, jnp.asarray(table))


def compose_kernel(*refs):
    *landing_refs, out_ref = refs
    count = len(landing_refs)
    section = lax.axis_index("gz")
    received = [ref[...] for ref in landing_refs]
    nodes = received[0].shape[1]
    ramp = lax.broadcasted_iota(jnp.int32, received[0].shape, 1).astype(F32)
    value = received[0]
    for other in range(count - 2, -1, -1):
        landing = received[0]
        for code in range(1, count):
            landing = jnp.where(section == other ^ code, received[code], landing)
        floor = jnp.minimum(jnp.floor(landing), nodes - 2.0)
        index = floor.astype(jnp.int32)
        share = landing - floor
        below = jnp.take_along_axis(value, index, axis=1)
        above = jnp.take_along_axis(value, index + 1, axis=1)
        value = jnp.where(section > other, (1.0 - share) * below + share * above, value)
    out_ref[0, 0, 0] = (value - ramp)[:2]


def compose(landings):
    nodes = landings[0].shape[1]
    return pl.pallas_call(
        compose_kernel,
        out_shape=jax.ShapeDtypeStruct((1, 1, 1, 2, nodes), F32),
        in_specs=[VMEM] * len(landings),
        out_specs=VMEM,
        compiler_params=pltpu.CompilerParams(vmem_limit_bytes=2**20),
        name="compose",
    )(*landings)


def swap_pairs(value, axis, first, spare):
    count, other = lax.axis_size(axis), lax.axis_size(spare)
    axes = ("gz", "ty", "tx")
    flip = axes.index(axis) > axes.index(spare)

    def place(here, beside):
        return beside * count + here if flip else here * other + beside

    moves = []
    for here in range(count):
        there = ((here + first) ^ 1) - first
        for beside in range(other):
            target = place(there, beside) if 0 <= there < count else place(here, beside ^ 1)
            moves.append((place(here, beside), target))
    return lax.ppermute(value, (spare, axis) if flip else (axis, spare), moves)


def rows_beside(value):
    count = lax.axis_size("ty")
    if count == 2:
        other = swap_pairs(value, "ty", 0, "gz")
        return (other, other)
    even = swap_pairs(value, "ty", 0, "gz")
    odd = swap_pairs(value, "ty", 1, "gz")
    at_even = lax.axis_index("ty") % 2 == 0
    return (jnp.where(at_even, odd, even), jnp.where(at_even, even, odd))


def to_next(value, turn):
    count, rows = lax.axis_size("gz"), lax.axis_size("ty")
    if not turn:
        return lax.ppermute(value, "gz", [(i, (i + 1) % count) for i in range(count)])
    moves = [(i * rows + j, (i + 1) % count * rows + (j ^ 1)) for i in range(count) for j in range(rows)]
    return lax.ppermute(value, ("gz", "ty"), moves)


def patch_targets(flow):
    first = lax.axis_index("gz") <= 1
    before = to_next(flow, 0)

    def target(near, earlier):
        return jnp.where(first, near[0:1], 0.5 * (near[0:1] + earlier[1:2]))

    if lax.axis_size("ty") == 2:
        beside = target(rows_beside(flow)[0], to_next(flow, 1))
        lines = [beside, target(flow, before), beside]
    else:
        (up, down), (up_before, down_before) = rows_beside(flow), rows_beside(before)
        lines = [target(up, up_before), target(flow, before), target(down, down_before)]
    return jnp.concatenate(lines + [jnp.zeros((5, flow.shape[1]), F32)], axis=0)


def local(images, boundary, anchor):
    nodes = anchor.shape[1]
    own = images[0]
    patches = own.shape[0] // PATCH
    sections = lax.axis_size("gz")
    tables = transform_tables()
    far = swap_pairs(own, "gz", 1, "ty")
    near = swap_pairs(own, "gz", 0, "ty")
    up, down = rows_beside(anchor[0])
    near_spec, *pairs = near_spectra(near, tables)
    own_spec = own_spectra(own, pairs[0], tables)
    far, own_spec, near_spec = lax.optimization_barrier((far, own_spec, near_spec))
    flow = flows(far, boundary, own_spec, near_spec, pairs, tables)
    flow, up, down = lax.optimization_barrier((flow, up, down))
    rows = anchor_rows(up, anchor[0], down)
    weights = gains(rows, swap_pairs(rows, "tx", 0, "gz"), swap_pairs(rows, "tx", 1, "gz"), nodes)
    line = patch_targets(flow)
    targets = (line, swap_pairs(line, "tx", 0, "gz"), swap_pairs(line, "tx", 1, "gz"))
    ring, landing = relax(targets, weights, nodes, patches)
    landings = [landing]
    for code in range(1, sections):
        landings.append(lax.ppermute(landing, "gz", [(i, i ^ code) for i in range(sections)]))
    mesh = natural_mesh(ring, nodes)
    mesh, landings = lax.optimization_barrier((mesh, landings))
    drift = compose(landings)
    return (mesh, drift)


def solution(mesh):
    return jax.shard_map(
        local,
        mesh=mesh,
        in_specs=(P("gz", "ty", "tx"), P("ty", "tx"), P("gz", "ty", "tx")),
        out_specs=(P("gz", None, "ty", "tx"), P("gz", "ty", "tx", None, None)),
        check_vma=False,
    )
```

```python
import math

import jax
import jax.numpy as jnp
import numpy as np
from jax import lax
from jax.experimental import pallas as pl
from jax.experimental.pallas import tpu as pltpu
from jax.sharding import PartitionSpec as P

PATCH = 128
STRIDE = 4
SWEEPS = 32
HALF = PATCH // 2
BF16 = jnp.bfloat16
F32 = jnp.float32


def split_table(table):
    high = table.astype(BF16)
    low = (table - high.astype(np.float64)).astype(BF16)
    return (high, low)


def transform_tables():
    counter = np.arange(PATCH)
    phase = (counter[:, None] * counter[None, :] % PATCH) * (2.0 * math.pi / PATCH)
    basis = np.concatenate([np.cos(phase[:HALF]), np.sin(phase[:HALF])])
    basis[HALF] = np.cos(phase[HALF])
    gains = np.full(PATCH, 2.0)
    gains[0] = gains[HALF] = 1.0
    inverse = basis.T * gains / PATCH
    tables = [part for table in (basis.T, inverse.T, basis, inverse / PATCH) for part in split_table(table)]
    return jnp.asarray(np.stack(tables))


def product_tables(tables_ref):
    forward_table = jnp.concatenate([tables_ref[0], tables_ref[1]], axis=1)
    inverse = jnp.concatenate([tables_ref[2], tables_ref[3]], axis=1)
    return [forward_table, jnp.concatenate([inverse, inverse], axis=0)]


def paired_patches(first, second):
    lower = lax.broadcasted_iota(jnp.int32, (PATCH, PATCH), 1) < HALF
    cosine = jnp.where(lower, first, pltpu.roll(second, HALF, 1))
    sine = jnp.where(lower, pltpu.roll(first, HALF, 1), second)
    return [cosine, sine]


def single_patches(product):
    lower = lax.broadcasted_iota(jnp.int32, (PATCH, PATCH), 1) < HALF
    cosine, sine = product[:, :PATCH], product[:, PATCH:]
    first = jnp.where(lower, cosine, pltpu.roll(sine, HALF, 1))
    second = jnp.where(lower, pltpu.roll(cosine, HALF, 1), sine)
    return [first, second]


def halves(value):
    high = value.astype(BF16)
    return (high, (value - high.astype(F32)).astype(BF16))


def dot(left, right):
    return jnp.dot(left, right, preferred_element_type=F32)


def left_transform(table_high, table_low, value):
    high, low = halves(value)
    table = jnp.concatenate([table_high, table_high, table_low], axis=1)
    return dot(table, jnp.concatenate([high, low, high], axis=0))


def quarters(spec):
    return (
        (spec[:HALF, :PATCH], spec[:HALF, PATCH:]),
        (spec[HALF:, :PATCH], spec[HALF:, PATCH:]),
    )


def cross_operand(spec):
    (cc, cs), (sc, ss) = quarters(spec)
    first_row = lax.broadcasted_iota(jnp.int32, (HALF, PATCH), 0) == 0
    first_lane = lax.broadcasted_iota(jnp.int32, (HALF, PATCH), 1) % HALF == 0

    def lanes(cosine, sine):
        return (cosine, jnp.where(first_lane, sine, cosine), jnp.where(first_lane, 0.0, sine))

    return (
        lanes(cc, cs),
        lanes(jnp.where(first_row, sc, cc), jnp.where(first_row, ss, cs)),
        lanes(jnp.where(first_row, 0.0, sc), jnp.where(first_row, 0.0, ss)),
    )


def cross(operand, spec):
    (row_c, row_d, row_s) = operand
    (bc, bs) = quarters(spec)

    def cosine(a, b):
        return a[0] * b[0] + a[2] * b[1]

    def sine(a, b):
        return a[1] * b[1] - a[2] * b[0]

    cc = cosine(row_c, bc) + cosine(row_s, bs)
    cs = sine(row_c, bc) + sine(row_s, bs)
    sc = cosine(row_d, bs) - cosine(row_s, bc)
    ss = sine(row_d, bs) - sine(row_s, bc)
    return jnp.concatenate(
        [jnp.concatenate([cc, cs], axis=1), jnp.concatenate([sc, ss], axis=1)], axis=0
    )


def windows(rows, cols):
    return [(slice(r, r + PATCH), slice(c, c + PATCH)) for r in range(0, rows, PATCH) for c in range(0, cols, PATCH)]


def side_by_side(value):
    return jnp.concatenate([value[i : i + PATCH] for i in range(0, value.shape[0], PATCH)], axis=1)


def forward(pixels, table, tables_ref):
    both = dot(pixels, table)
    right = both[:, :PATCH] + both[:, PATCH:]
    singles = [right[i : i + PATCH] for i in range(0, right.shape[0], PATCH)]
    tiles = [tile for i in range(0, len(singles), 2) for tile in paired_patches(*singles[i : i + 2])]
    return left_transform(tables_ref[4], tables_ref[5], jnp.concatenate(tiles, axis=1))


def image_spectra(image_ref, table, tables_ref):
    pixels = jnp.concatenate([image_ref[window] for window in windows(*image_ref.shape)], axis=0)
    return forward(pixels, table, tables_ref)


def near_kernel(image_ref, tables_ref, spec_out, forward_out, inverse_out):
    table, inverse = product_tables(tables_ref)
    forward_out[...] = table
    inverse_out[...] = inverse
    spec_out[...] = image_spectra(image_ref, table, tables_ref)


def own_kernel(image_ref, forward_ref, tables_ref, spec_out):
    spec_out[...] = image_spectra(image_ref, forward_ref[...], tables_ref)


def rows_kernel(up_ref, own_ref, down_ref, out_ref):
    nodes = own_ref.shape[0]
    out_ref[:SWEEPS] = up_ref[nodes - SWEEPS :]
    out_ref[SWEEPS : SWEEPS + nodes] = own_ref[...]
    out_ref[SWEEPS + nodes :] = down_ref[:SWEEPS]


def flows_kernel(
    far_ref, edge_ref, own_spec, near_spec, forward_ref, inverse_ref, tables_ref, out_ref, stats_ref
):
    wide = 2 * PATCH
    spots = windows(*far_ref.shape)
    patches = len(spots)
    blocks = patches // 2
    at_edge = lax.axis_index("gz") == 0
    at_even = lax.axis_index("gz") % 2 == 0
    pixels = jnp.concatenate(
        [jnp.where(at_edge, edge_ref[spot].astype(F32), far_ref[spot].astype(F32)).astype(BF16) for spot in spots], axis=0
    )
    spec = forward(pixels, forward_ref[...], tables_ref)
    products = []
    for block in range(blocks):
        lanes = slice(block * wide, (block + 1) * wide)
        far, near = spec[:, lanes], near_spec[:, lanes]
        operand = cross_operand(jnp.where(at_even, far, near))
        products.append(cross(operand, own_spec[:, lanes]))
        products.append(cross(operand, jnp.where(at_even, near, far)))
    singles = [single for product in products for single in single_patches(product)]
    both = dot(jnp.concatenate(halves(jnp.concatenate(singles, axis=0)), axis=1), inverse_ref[...])
    back = both[:, :PATCH] + both[:, PATCH:]
    scores = left_transform(tables_ref[6], tables_ref[7], side_by_side(back))
    groups = scores.reshape(PATCH // 8, 8, 2 * blocks * wide)
    peak = jnp.max(groups, axis=0)
    total = jnp.zeros_like(peak)
    moment = jnp.zeros_like(peak)
    for group in range(PATCH // 8):
        weight = jnp.exp(groups[group] - peak)
        shift = 8 * group - (PATCH if group >= PATCH // 16 else 0)
        total = total + weight
        moment = moment + float(shift) * weight
    for block in range(blocks):
        for pair in range(2):
            for side in range(2):
                at = (2 * block + pair) * 2 + side
                lanes = slice(at * PATCH, (at + 1) * PATCH)
                slot = pair * patches + 2 * block + side
                stats_ref[0, slot] = peak[:, lanes]
                stats_ref[1, slot] = total[:, lanes]
                stats_ref[2, slot] = moment[:, lanes]
    peak = stats_ref[0]
    best = jnp.max(jnp.max(peak, axis=1, keepdims=True), axis=2, keepdims=True)
    scale = jnp.exp(peak - best)
    total = scale * stats_ref[1]
    within = lax.broadcasted_iota(jnp.int32, peak.shape, 1).astype(F32)
    moment = scale * stats_ref[2] + within * total
    total = jnp.sum(total, axis=1)
    lane = lax.broadcasted_iota(jnp.int32, total.shape, 1)
    signed = jnp.where(lane < HALF, lane, lane - PATCH).astype(F32)
    mass = jnp.sum(total, axis=1, keepdims=True) * STRIDE
    along_rows = jnp.sum(jnp.sum(moment, axis=1), axis=1, keepdims=True) / mass
    along_cols = jnp.sum(total * signed, axis=1, keepdims=True) / mass
    values = (
        along_rows[:patches],
        along_cols[:patches],
        along_rows[patches:] - along_rows[:patches],
        along_cols[patches:] - along_cols[:patches],
    )
    lane = lax.broadcasted_iota(jnp.int32, (patches, PATCH), 1)
    patch = lax.broadcasted_iota(jnp.int32, (patches, PATCH), 0)
    lines = []
    for first, second in (values[:2], values[2:]):
        line = jnp.where(lane == patch, first, jnp.where(lane == patches + patch, second, 0.0))
        lines.append(jnp.sum(line, axis=0, keepdims=True))
    line = lax.broadcasted_iota(jnp.int32, out_ref.shape, 0)
    out_ref[...] = jnp.where(line == 0, lines[0], lines[1])


VMEM = pl.BlockSpec(memory_space=pltpu.VMEM)
PARAMS = pltpu.CompilerParams(vmem_limit_bytes=40 * 2**20)


def spec_shape(image):
    return jax.ShapeDtypeStruct((PATCH, image.shape[0] // PATCH * image.shape[1]), F32)


def near_spectra(near, tables):
    forward_table = jax.ShapeDtypeStruct((PATCH, 2 * PATCH), BF16)
    inverse_table = jax.ShapeDtypeStruct((2 * PATCH, 2 * PATCH), BF16)
    return pl.pallas_call(
        near_kernel,
        out_shape=(spec_shape(near), forward_table, inverse_table),
        in_specs=[VMEM] * 2,
        out_specs=(VMEM,) * 3,
        compiler_params=PARAMS,
        cost_estimate=pl.CostEstimate(flops=2 * 10**9, bytes_accessed=2 * 2**20, transcendentals=0),
        name="near_spectra",
    )(near, tables)


def own_spectra(own, forward_table, tables):
    return pl.pallas_call(
        own_kernel,
        out_shape=spec_shape(own),
        in_specs=[VMEM] * 3,
        out_specs=VMEM,
        compiler_params=PARAMS,
        cost_estimate=pl.CostEstimate(flops=10**9, bytes_accessed=2 * 2**20, transcendentals=0),
        name="own_spectra",
    )(own, forward_table, tables)


def anchor_rows(up, own, down):
    nodes = own.shape[0]
    return pl.pallas_call(
        rows_kernel,
        out_shape=jax.ShapeDtypeStruct((nodes + 2 * SWEEPS, nodes), F32),
        in_specs=[VMEM] * 3,
        out_specs=VMEM,
        compiler_params=pltpu.CompilerParams(vmem_limit_bytes=2**20),
        name="anchor_rows",
    )(up, own, down)


def flows(far, edge, own_spec, near_spec, pairs, tables):
    forward_table, inverse_table = pairs
    patches = far.shape[0] // PATCH * (far.shape[1] // PATCH)
    return pl.pallas_call(
        flows_kernel,
        out_shape=jax.ShapeDtypeStruct((8, PATCH), F32),
        in_specs=[VMEM] * 7,
        out_specs=VMEM,
        scratch_shapes=[pltpu.VMEM((3, 2 * patches, 8, PATCH), F32)],
        compiler_params=PARAMS,
        cost_estimate=pl.CostEstimate(flops=4 * 10**9, bytes_accessed=3 * 2**20, transcendentals=0),
        name="flows",
    )(far, edge, own_spec, near_spec, forward_table, inverse_table, tables)


def spread_weights(nodes, patches):
    node_pos = (np.arange(nodes) + 0.5) * STRIDE / PATCH - 0.5
    weights = np.maximum(0.0, 1.0 - np.abs(node_pos[:, None] - np.arange(patches)[None, :]))
    return weights / weights.sum(axis=1, keepdims=True)


def ring_nodes(nodes):
    span = np.arange(nodes + 2 * SWEEPS) - SWEEPS
    ring = np.concatenate([span[SWEEPS:], span, span[:SWEEPS]])
    part = np.zeros(len(ring), np.int32)
    part[nodes + SWEEPS : len(ring) - SWEEPS] = 1
    order = np.arange(len(ring)).reshape(PATCH, -1).T.reshape(-1)
    return (ring[order], part[order])


def row_nodes(nodes):
    span = np.arange(nodes + 2 * SWEEPS) - SWEEPS
    return span.reshape(8, -1).T.reshape(-1)


def target_tables(nodes, patches):
    ring, _ = ring_nodes(nodes)
    spread = spread_weights(nodes, patches)

    def wide(positions):
        table = np.zeros((len(positions), 3, patches))
        for tile in range(3):
            at = positions - (tile - 1) * nodes
            hit = (at >= 0) & (at < nodes)
            table[hit, tile] = spread[at[hit]]
        return table

    shape = (3, 3, patches, patches)
    rows = wide(row_nodes(nodes))[:, None, :, :, None]
    cols = wide(ring).transpose(1, 2, 0)[:, None, None]
    left = np.broadcast_to(rows, (rows.shape[0],) + shape).reshape(rows.shape[0], -1)
    right = np.broadcast_to(cols, shape + (len(ring),)).reshape(-1, len(ring))
    return (left.astype(BF16), right.astype(BF16))


def ring_tables(nodes):
    ring, part = ring_nodes(nodes)
    place = np.arange(3 * nodes)[:, None] - nodes
    into = (place == ring[None]).astype(BF16)
    column = np.arange(2 * nodes)[None]
    out = ((ring[:, None] == column % nodes) & (part[:, None] == column // nodes)).astype(BF16)
    return (into, out)


def permuted(value, table):
    result = None
    for piece in range(3):
        part = value.astype(BF16)
        moved = dot(part, table)
        result = moved if result is None else result + moved
        value = value - part.astype(F32)
    return result


def ring_place(rows, lanes):
    lane = lax.broadcasted_iota(jnp.int32, (rows, lanes), 1)
    return lane % PATCH * (lanes // PATCH) + lane // PATCH


def tiles_beside(even_ref, odd_ref):
    at_even = lax.axis_index("tx") % 2 == 0
    even, odd = even_ref[...], odd_ref[...]
    return (jnp.where(at_even, odd, even), jnp.where(at_even, even, odd))


def gains_kernel(own_ref, even_ref, odd_ref, into_ref, gain_ref, pull_ref, rows_ref):
    strips = gain_ref.shape[0]
    nodes = own_ref.shape[1]
    before, after = tiles_beside(even_ref, odd_ref)
    weight = permuted(jnp.concatenate([before, own_ref[...], after], axis=1), into_ref[...])
    row_node = lax.broadcasted_iota(jnp.int32, weight.shape, 0) - SWEEPS
    row_node = row_node + lax.axis_index("ty") * nodes
    lanes = into_ref.shape[1]
    place = ring_place(1, lanes)
    shift = jnp.where(place < nodes + SWEEPS, 0, jnp.where(place < lanes - SWEEPS, nodes + 2 * SWEEPS, lanes))
    col_node = place - shift + lax.axis_index("tx") * nodes
    inside = (row_node >= 0) & (row_node < lax.axis_size("ty") * nodes)
    inside = inside & (col_node >= 0) & (col_node < lax.axis_size("tx") * nodes)
    gain = jnp.where(inside, 1.0 / (4.0 + weight), 0.0)
    for value, out in ((gain, gain_ref), (gain * weight, pull_ref)):
        rows_ref[...] = value.reshape(value.shape[0], -1, PATCH).transpose(1, 0, 2)
        for strip in range(strips):
            for tile in range(rows_ref.shape[0]):
                out[strip, :, tile * PATCH : (tile + 1) * PATCH] = rows_ref[tile, pl.ds(strip, 8, strips), :]


def gains(own, even, odd, nodes):
    into, _ = ring_tables(nodes)
    shape = jax.ShapeDtypeStruct((own.shape[0] // 8, 8, into.shape[1]), F32)
    return pl.pallas_call(
        gains_kernel,
        out_shape=(shape, shape),
        in_specs=[VMEM] * 4,
        out_specs=(VMEM, VMEM),
        scratch_shapes=[pltpu.VMEM((into.shape[1] // PATCH, own.shape[0], PATCH), F32)],
        compiler_params=PARAMS,
        cost_estimate=pl.CostEstimate(flops=10**9, bytes_accessed=2**20, transcendentals=0),
        name="gains",
    )(own, even, odd, jnp.asarray(into))


def relax_kernel(
    up_ref, own_ref, down_ref, up_earlier_ref, earlier_ref, down_earlier_ref, gain_ref, pull_ref, left_ref, right_ref, cols_table_ref, rows_table_ref,
    work_ref, landing_ref, base_ref,
):
    strips, _, lanes = work_ref.shape
    nodes = landing_ref.shape[1]
    patches = left_ref.shape[1] // 9
    first = lax.axis_index("gz") <= 1
    lines = []
    for near, past in ((up_ref, up_earlier_ref), (own_ref, earlier_ref), (down_ref, down_earlier_ref)):
        lines.append(jnp.where(first, near[:3], 0.5 * (near[:3] + past[3:6])))
    rows = [line[tile : tile + 1] for tile in range(3) for line in lines]
    rows.append(jnp.zeros((PATCH - 9, PATCH), F32))
    columns = jnp.transpose(jnp.concatenate(rows, axis=0))

    def sources(part):
        lines = slice(part * patches, (part + 1) * patches)
        return jnp.concatenate([columns[lines, i : i + 1] for i in range(9)], axis=0)

    place = ring_place(1, lanes)
    second = (place >= nodes + SWEEPS) & (place < lanes - SWEEPS)
    spread = jnp.where(second, sources(1), sources(0)) * right_ref[...].astype(F32)
    target = None
    for piece in range(3):
        part = spread.astype(BF16)
        term = dot(left_ref[...], part)
        target = term if target is None else target + term
        spread = spread - part.astype(F32)
    target = target.reshape(strips, 8, lanes)
    base_ref[...] = pull_ref[...] * target
    work_ref[...] = jnp.where(gain_ref[...] > 0.0, target, 0.0)
    tiles = lanes // PATCH

    def row(strip):
        return [work_ref[strip, :, i * PATCH : (i + 1) * PATCH] for i in range(tiles)]

    def sweep(counter, carry):
        here = row(0)
        above = [pltpu.roll(value, 1, 0) for value in row(strips - 1)]
        around = [pltpu.roll(value, 7, 0) for value in here]
        for strip in range(strips):
            below = row(strip + 1) if strip + 1 < strips else around
            ring = [pltpu.roll(here[-1], 1, 1)] + here + [pltpu.roll(here[0], PATCH - 1, 1)]
            for tile in range(tiles):
                at = (strip, slice(None), slice(tile * PATCH, (tile + 1) * PATCH))
                total = (above[tile] + below[tile]) + (ring[tile] + ring[tile + 2])
                work_ref[at] = gain_ref[at] * total + base_ref[at]
            above, here = here, below
        return carry

    lax.fori_loop(0, SWEEPS, sweep, 0, unroll=32)
    mesh = work_ref[...].reshape(strips * 8, lanes)
    ones = jnp.where(ring_place(16, lanes) < nodes, 1.0, 0.0).astype(BF16)
    sums = None
    for piece in range(3):
        part = mesh.astype(BF16)
        term = lax.dot_general(ones, part, (((1,), (1,)), ((), ())), preferred_element_type=F32)
        sums = term if sums is None else sums + term
        mesh = mesh - part.astype(F32)
    down_mean = permuted(sums, rows_table_ref[...])[:1] / nodes
    strip = lax.broadcasted_iota(jnp.int32, (strips, 8, lanes), 0)
    row = lax.broadcasted_iota(jnp.int32, (strips, 8, lanes), 1) * strips + strip
    kept = jnp.where((row >= SWEEPS) & (row < SWEEPS + nodes), work_ref[...], 0.0)
    across = permuted(jnp.sum(kept, axis=0), cols_table_ref[...])
    across_mean = jnp.sum(across, axis=0, keepdims=True) / nodes
    line = lax.broadcasted_iota(jnp.int32, landing_ref.shape, 0)
    ramp = lax.broadcasted_iota(jnp.int32, landing_ref.shape, 1).astype(F32)
    profile = jnp.where(line == 0, down_mean, across_mean)
    landing_ref[...] = jnp.clip(ramp + profile, 0.0, nodes - 1.0)


def relax(targets, weights, nodes, patches):
    left, right = target_tables(nodes, patches)
    ring, ring_part = ring_nodes(nodes)
    node = np.arange(nodes)[None]
    cols_table = ((ring[:, None] == node) & (ring_part[:, None] == 1)).astype(BF16)
    rows_table = (row_nodes(nodes)[:, None] == node).astype(BF16)
    tables = map(jnp.asarray, (left, right, cols_table, rows_table))
    shape = weights[0].shape
    return pl.pallas_call(
        relax_kernel,
        out_shape=(jax.ShapeDtypeStruct(shape, F32), jax.ShapeDtypeStruct((8, nodes), F32)),
        in_specs=[VMEM] * 12,
        out_specs=(VMEM, VMEM),
        scratch_shapes=[pltpu.VMEM(shape, F32)],
        compiler_params=PARAMS,
        cost_estimate=pl.CostEstimate(flops=4 * 10**9, bytes_accessed=3 * 2**20, transcendentals=0),
        name="relax",
    )(*targets, *weights, *tables)


def mesh_kernel(ring_ref, table_ref, mesh_ref, rows_ref):
    strips, _, lanes = ring_ref.shape
    nodes = mesh_ref.shape[2]
    final = permuted(ring_ref[...].reshape(strips * 8, lanes), table_ref[...])
    for strip in range(strips):
        for part in range(2):
            columns = slice(part * nodes, (part + 1) * nodes)
            rows_ref[part, pl.ds(strip, 8, strips), :] = final[8 * strip : 8 * strip + 8, columns]
    mesh_ref[0] = rows_ref[:, SWEEPS : SWEEPS + nodes]


def natural_mesh(ring, nodes):
    _, table = ring_tables(nodes)
    return pl.pallas_call(
        mesh_kernel,
        out_shape=jax.ShapeDtypeStruct((1, 2, nodes, nodes), F32),
        in_specs=[VMEM] * 2,
        out_specs=VMEM,
        scratch_shapes=[pltpu.VMEM((2, ring.shape[0] * 8, nodes), F32)],
        compiler_params=PARAMS,
        cost_estimate=pl.CostEstimate(flops=10**9, bytes_accessed=2**20, transcendentals=0),
        name="natural_mesh",
    )(ring, jnp.asarray(table))


def compose_kernel(*refs):
    *landing_refs, out_ref = refs
    count = len(landing_refs)
    section = lax.axis_index("gz")
    received = [ref[...] for ref in landing_refs]
    nodes = received[0].shape[1]
    ramp = lax.broadcasted_iota(jnp.int32, received[0].shape, 1).astype(F32)
    value = received[0]
    for other in range(count - 2, -1, -1):
        landing = received[0]
        for code in range(1, count):
            landing = jnp.where(section == other ^ code, received[code], landing)
        floor = jnp.minimum(jnp.floor(landing), nodes - 2.0)
        index = floor.astype(jnp.int32)
        share = landing - floor
        below = jnp.take_along_axis(value, index, axis=1)
        above = jnp.take_along_axis(value, index + 1, axis=1)
        value = jnp.where(section > other, (1.0 - share) * below + share * above, value)
    out_ref[0, 0, 0] = (value - ramp)[:2]


def compose(landings):
    nodes = landings[0].shape[1]
    return pl.pallas_call(
        compose_kernel,
        out_shape=jax.ShapeDtypeStruct((1, 1, 1, 2, nodes), F32),
        in_specs=[VMEM] * len(landings),
        out_specs=VMEM,
        compiler_params=pltpu.CompilerParams(vmem_limit_bytes=2**20),
        name="compose",
    )(*landings)


def swap_pairs(value, axis, first, spare):
    count, other = lax.axis_size(axis), lax.axis_size(spare)
    axes = ("gz", "ty", "tx")
    flip = axes.index(axis) > axes.index(spare)

    def place(here, beside):
        return beside * count + here if flip else here * other + beside

    moves = []
    for here in range(count):
        there = ((here + first) ^ 1) - first
        for beside in range(other):
            target = place(there, beside) if 0 <= there < count else place(here, beside ^ 1)
            moves.append((place(here, beside), target))
    return lax.ppermute(value, (spare, axis) if flip else (axis, spare), moves)


def rows_beside(value):
    count = lax.axis_size("ty")
    if count == 2:
        other = swap_pairs(value, "ty", 0, "gz")
        return (other, other)
    even = swap_pairs(value, "ty", 0, "gz")
    odd = swap_pairs(value, "ty", 1, "gz")
    at_even = lax.axis_index("ty") % 2 == 0
    return (jnp.where(at_even, odd, even), jnp.where(at_even, even, odd))


def to_next(value, turn):
    count, rows = lax.axis_size("gz"), lax.axis_size("ty")
    if not turn:
        return lax.ppermute(value, "gz", [(i, (i + 1) % count) for i in range(count)])
    moves = [(i * rows + j, (i + 1) % count * rows + (j ^ 1)) for i in range(count) for j in range(rows)]
    return lax.ppermute(value, ("gz", "ty"), moves)


def flow_lines(flow):
    even, odd = swap_pairs(flow, "tx", 0, "gz"), swap_pairs(flow, "tx", 1, "gz")
    at_even = lax.axis_index("tx") % 2 == 0
    before, after = jnp.where(at_even, odd, even), jnp.where(at_even, even, odd)
    tiles = (before, flow, after)
    lines = [tile[row : row + 1] for row in range(2) for tile in tiles]
    lines = jnp.concatenate(lines + [flow[:2]], axis=0)
    earlier = to_next(lines, 0)
    if lax.axis_size("ty") == 2:
        beside, beside_earlier = rows_beside(lines)[0], to_next(lines, 1)
        return (beside, lines, beside, beside_earlier, earlier, beside_earlier)
    (up, down), (up_earlier, down_earlier) = rows_beside(lines), rows_beside(earlier)
    return (up, lines, down, up_earlier, earlier, down_earlier)


def local(images, boundary, anchor):
    nodes = anchor.shape[1]
    own = images[0]
    patches = own.shape[0] // PATCH
    sections = lax.axis_size("gz")
    tables = transform_tables()
    far = swap_pairs(own, "gz", 1, "ty")
    near = swap_pairs(own, "gz", 0, "ty")
    up, down = rows_beside(anchor[0])
    near_spec, *pairs = near_spectra(near, tables)
    own_spec = own_spectra(own, pairs[0], tables)
    far, own_spec, near_spec = lax.optimization_barrier((far, own_spec, near_spec))
    flow = flows(far, boundary, own_spec, near_spec, pairs, tables)
    flow, up, down = lax.optimization_barrier((flow, up, down))
    rows = anchor_rows(up, anchor[0], down)
    weights = gains(rows, swap_pairs(rows, "tx", 0, "gz"), swap_pairs(rows, "tx", 1, "gz"), nodes)
    targets = flow_lines(flow)
    ring, landing = relax(targets, weights, nodes, patches)
    landings = [landing]
    for code in range(1, sections):
        landings.append(lax.ppermute(landing, "gz", [(i, i ^ code) for i in range(sections)]))
    mesh = natural_mesh(ring, nodes)
    mesh, landings = lax.optimization_barrier((mesh, landings))
    drift = compose(landings)
    return (mesh, drift)


def solution(mesh):
    return jax.shard_map(
        local,
        mesh=mesh,
        in_specs=(P("gz", "ty", "tx"), P("ty", "tx"), P("gz", "ty", "tx")),
        out_specs=(P("gz", None, "ty", "tx"), P("gz", "ty", "tx", None, None)),
        check_vma=False,
    )
```

```python
import math

import jax
import jax.numpy as jnp
import numpy as np
from jax import lax
from jax.experimental import pallas as pl
from jax.experimental.pallas import tpu as pltpu
from jax.sharding import PartitionSpec as P

PATCH = 128
STRIDE = 4
SWEEPS = 32
HALF = PATCH // 2
BF16 = jnp.bfloat16
F32 = jnp.float32


def split_table(table):
    high = table.astype(BF16)
    low = (table - high.astype(np.float64)).astype(BF16)
    return (high, low)


def transform_tables():
    counter = np.arange(PATCH)
    phase = (counter[:, None] * counter[None, :] % PATCH) * (2.0 * math.pi / PATCH)
    basis = np.concatenate([np.cos(phase[:HALF]), np.sin(phase[:HALF])])
    basis[HALF] = np.cos(phase[HALF])
    gains = np.full(PATCH, 2.0)
    gains[0] = gains[HALF] = 1.0
    inverse = basis.T * gains / PATCH
    tables = [part for table in (basis.T, inverse.T, basis, inverse / PATCH) for part in split_table(table)]
    return jnp.asarray(np.stack(tables))


def product_tables(tables_ref):
    forward_table = jnp.concatenate([tables_ref[0], tables_ref[1]], axis=1)
    inverse = jnp.concatenate([tables_ref[2], tables_ref[3]], axis=1)
    return [forward_table, jnp.concatenate([inverse, inverse], axis=0)]


def paired_patches(first, second):
    lower = lax.broadcasted_iota(jnp.int32, (PATCH, PATCH), 1) < HALF
    cosine = jnp.where(lower, first, pltpu.roll(second, HALF, 1))
    sine = jnp.where(lower, pltpu.roll(first, HALF, 1), second)
    return [cosine, sine]


def single_patches(product):
    lower = lax.broadcasted_iota(jnp.int32, (PATCH, PATCH), 1) < HALF
    cosine, sine = product[:, :PATCH], product[:, PATCH:]
    first = jnp.where(lower, cosine, pltpu.roll(sine, HALF, 1))
    second = jnp.where(lower, pltpu.roll(cosine, HALF, 1), sine)
    return [first, second]


def halves(value):
    high = value.astype(BF16)
    return (high, (value - high.astype(F32)).astype(BF16))


def dot(left, right):
    return jnp.dot(left, right, preferred_element_type=F32)


def left_transform(table_high, table_low, value):
    high, low = halves(value)
    table = jnp.concatenate([table_high, table_high, table_low], axis=1)
    return dot(table, jnp.concatenate([high, low, high], axis=0))


def quarters(spec):
    return (
        (spec[:HALF, :PATCH], spec[:HALF, PATCH:]),
        (spec[HALF:, :PATCH], spec[HALF:, PATCH:]),
    )


def cross_operand(spec):
    (cc, cs), (sc, ss) = quarters(spec)
    first_row = lax.broadcasted_iota(jnp.int32, (HALF, PATCH), 0) == 0
    first_lane = lax.broadcasted_iota(jnp.int32, (HALF, PATCH), 1) % HALF == 0

    def lanes(cosine, sine):
        return (cosine, jnp.where(first_lane, sine, cosine), jnp.where(first_lane, 0.0, sine))

    return (
        lanes(cc, cs),
        lanes(jnp.where(first_row, sc, cc), jnp.where(first_row, ss, cs)),
        lanes(jnp.where(first_row, 0.0, sc), jnp.where(first_row, 0.0, ss)),
    )


def cross(operand, spec):
    (row_c, row_d, row_s) = operand
    (bc, bs) = quarters(spec)

    def cosine(a, b):
        return a[0] * b[0] + a[2] * b[1]

    def sine(a, b):
        return a[1] * b[1] - a[2] * b[0]

    cc = cosine(row_c, bc) + cosine(row_s, bs)
    cs = sine(row_c, bc) + sine(row_s, bs)
    sc = cosine(row_d, bs) - cosine(row_s, bc)
    ss = sine(row_d, bs) - sine(row_s, bc)
    return jnp.concatenate(
        [jnp.concatenate([cc, cs], axis=1), jnp.concatenate([sc, ss], axis=1)], axis=0
    )


def windows(rows, cols):
    return [(slice(r, r + PATCH), slice(c, c + PATCH)) for r in range(0, rows, PATCH) for c in range(0, cols, PATCH)]


def side_by_side(value):
    return jnp.concatenate([value[i : i + PATCH] for i in range(0, value.shape[0], PATCH)], axis=1)


def forward(pixels, table, tables_ref):
    both = dot(pixels, table)
    right = both[:, :PATCH] + both[:, PATCH:]
    singles = [right[i : i + PATCH] for i in range(0, right.shape[0], PATCH)]
    tiles = [tile for i in range(0, len(singles), 2) for tile in paired_patches(*singles[i : i + 2])]
    return left_transform(tables_ref[4], tables_ref[5], jnp.concatenate(tiles, axis=1))


def image_spectra(image_ref, table, tables_ref):
    pixels = jnp.concatenate([image_ref[window] for window in windows(*image_ref.shape)], axis=0)
    return forward(pixels, table, tables_ref)


def near_kernel(image_ref, tables_ref, spec_out, forward_out, inverse_out):
    table, inverse = product_tables(tables_ref)
    forward_out[...] = table
    inverse_out[...] = inverse
    spec_out[...] = image_spectra(image_ref, table, tables_ref)


def own_kernel(image_ref, forward_ref, tables_ref, spec_out):
    spec_out[...] = image_spectra(image_ref, forward_ref[...], tables_ref)


def rows_kernel(up_ref, own_ref, down_ref, out_ref):
    nodes = own_ref.shape[0]
    out_ref[:SWEEPS] = up_ref[nodes - SWEEPS :]
    out_ref[SWEEPS : SWEEPS + nodes] = own_ref[...]
    out_ref[SWEEPS + nodes :] = down_ref[:SWEEPS]


def flows_kernel(
    far_ref, edge_ref, own_spec, near_spec, forward_ref, inverse_ref, tables_ref, out_ref, stats_ref
):
    wide = 2 * PATCH
    spots = windows(*far_ref.shape)
    patches = len(spots)
    blocks = patches // 2
    at_edge = lax.axis_index("gz") == 0
    at_even = lax.axis_index("gz") % 2 == 0
    pixels = jnp.concatenate(
        [jnp.where(at_edge, edge_ref[spot].astype(F32), far_ref[spot].astype(F32)).astype(BF16) for spot in spots], axis=0
    )
    spec = forward(pixels, forward_ref[...], tables_ref)
    products = []
    for block in range(blocks):
        lanes = slice(block * wide, (block + 1) * wide)
        far, near = spec[:, lanes], near_spec[:, lanes]
        operand = cross_operand(jnp.where(at_even, far, near))
        products.append(cross(operand, own_spec[:, lanes]))
        products.append(cross(operand, jnp.where(at_even, near, far)))
    singles = [single for product in products for single in single_patches(product)]
    both = dot(jnp.concatenate(halves(jnp.concatenate(singles, axis=0)), axis=1), inverse_ref[...])
    back = both[:, :PATCH] + both[:, PATCH:]
    scores = left_transform(tables_ref[6], tables_ref[7], side_by_side(back))
    groups = scores.reshape(PATCH // 8, 8, 2 * blocks * wide)
    peak = jnp.max(groups, axis=0)
    total = jnp.zeros_like(peak)
    moment = jnp.zeros_like(peak)
    for group in reversed(range(PATCH // 8)):
        total = total + jnp.exp(groups[group] - peak)
        if group:
            moment = moment + total
        if group == PATCH // 16:
            wrapped = total
    moment = 8.0 * moment - float(PATCH) * wrapped
    for block in range(blocks):
        for pair in range(2):
            for side in range(2):
                at = (2 * block + pair) * 2 + side
                lanes = slice(at * PATCH, (at + 1) * PATCH)
                slot = pair * patches + 2 * block + side
                stats_ref[0, slot] = peak[:, lanes]
                stats_ref[1, slot] = total[:, lanes]
                stats_ref[2, slot] = moment[:, lanes]
    peak = stats_ref[0]
    best = jnp.max(jnp.max(peak, axis=1, keepdims=True), axis=2, keepdims=True)
    scale = jnp.exp(peak - best)
    total = scale * stats_ref[1]
    within = lax.broadcasted_iota(jnp.int32, peak.shape, 1).astype(F32)
    moment = scale * stats_ref[2] + within * total
    total = jnp.sum(total, axis=1)
    lane = lax.broadcasted_iota(jnp.int32, total.shape, 1)
    signed = jnp.where(lane < HALF, lane, lane - PATCH).astype(F32)
    mass = jnp.sum(total, axis=1, keepdims=True) * STRIDE
    along_rows = jnp.sum(jnp.sum(moment, axis=1), axis=1, keepdims=True) / mass
    along_cols = jnp.sum(total * signed, axis=1, keepdims=True) / mass
    values = (
        along_rows[:patches],
        along_cols[:patches],
        along_rows[patches:] - along_rows[:patches],
        along_cols[patches:] - along_cols[:patches],
    )
    lane = lax.broadcasted_iota(jnp.int32, (patches, PATCH), 1)
    patch = lax.broadcasted_iota(jnp.int32, (patches, PATCH), 0)
    lines = []
    for first, second in (values[:2], values[2:]):
        line = jnp.where(lane == patch, first, jnp.where(lane == patches + patch, second, 0.0))
        lines.append(jnp.sum(line, axis=0, keepdims=True))
    line = lax.broadcasted_iota(jnp.int32, out_ref.shape, 0)
    out_ref[...] = jnp.where(line == 0, lines[0], lines[1])


VMEM = pl.BlockSpec(memory_space=pltpu.VMEM)
PARAMS = pltpu.CompilerParams(vmem_limit_bytes=40 * 2**20)


def spec_shape(image):
    return jax.ShapeDtypeStruct((PATCH, image.shape[0] // PATCH * image.shape[1]), F32)


def near_spectra(near, tables):
    forward_table = jax.ShapeDtypeStruct((PATCH, 2 * PATCH), BF16)
    inverse_table = jax.ShapeDtypeStruct((2 * PATCH, 2 * PATCH), BF16)
    return pl.pallas_call(
        near_kernel,
        out_shape=(spec_shape(near), forward_table, inverse_table),
        in_specs=[VMEM] * 2,
        out_specs=(VMEM,) * 3,
        compiler_params=PARAMS,
        cost_estimate=pl.CostEstimate(flops=2 * 10**9, bytes_accessed=2 * 2**20, transcendentals=0),
        name="near_spectra",
    )(near, tables)


def own_spectra(own, forward_table, tables):
    return pl.pallas_call(
        own_kernel,
        out_shape=spec_shape(own),
        in_specs=[VMEM] * 3,
        out_specs=VMEM,
        compiler_params=PARAMS,
        cost_estimate=pl.CostEstimate(flops=10**9, bytes_accessed=2 * 2**20, transcendentals=0),
        name="own_spectra",
    )(own, forward_table, tables)


def anchor_rows(up, own, down):
    nodes = own.shape[0]
    return pl.pallas_call(
        rows_kernel,
        out_shape=jax.ShapeDtypeStruct((nodes + 2 * SWEEPS, nodes), F32),
        in_specs=[VMEM] * 3,
        out_specs=VMEM,
        compiler_params=pltpu.CompilerParams(vmem_limit_bytes=2**20),
        name="anchor_rows",
    )(up, own, down)


def flows(far, edge, own_spec, near_spec, pairs, tables):
    forward_table, inverse_table = pairs
    patches = far.shape[0] // PATCH * (far.shape[1] // PATCH)
    return pl.pallas_call(
        flows_kernel,
        out_shape=jax.ShapeDtypeStruct((8, PATCH), F32),
        in_specs=[VMEM] * 7,
        out_specs=VMEM,
        scratch_shapes=[pltpu.VMEM((3, 2 * patches, 8, PATCH), F32)],
        compiler_params=PARAMS,
        cost_estimate=pl.CostEstimate(flops=4 * 10**9, bytes_accessed=3 * 2**20, transcendentals=0),
        name="flows",
    )(far, edge, own_spec, near_spec, forward_table, inverse_table, tables)


def spread_weights(nodes, patches):
    node_pos = (np.arange(nodes) + 0.5) * STRIDE / PATCH - 0.5
    weights = np.maximum(0.0, 1.0 - np.abs(node_pos[:, None] - np.arange(patches)[None, :]))
    return weights / weights.sum(axis=1, keepdims=True)


def ring_nodes(nodes):
    span = np.arange(nodes + 2 * SWEEPS) - SWEEPS
    ring = np.concatenate([span[SWEEPS:], span, span[:SWEEPS]])
    part = np.zeros(len(ring), np.int32)
    part[nodes + SWEEPS : len(ring) - SWEEPS] = 1
    order = np.arange(len(ring)).reshape(PATCH, -1).T.reshape(-1)
    return (ring[order], part[order])


def row_nodes(nodes):
    span = np.arange(nodes + 2 * SWEEPS) - SWEEPS
    return span.reshape(8, -1).T.reshape(-1)


def target_tables(nodes, patches):
    ring, _ = ring_nodes(nodes)
    spread = spread_weights(nodes, patches)

    def wide(positions):
        table = np.zeros((len(positions), 3, patches))
        for tile in range(3):
            at = positions - (tile - 1) * nodes
            hit = (at >= 0) & (at < nodes)
            table[hit, tile] = spread[at[hit]]
        return table

    shape = (3, 3, patches, patches)
    rows = wide(row_nodes(nodes))[:, None, :, :, None]
    cols = wide(ring).transpose(1, 2, 0)[:, None, None]
    left = np.broadcast_to(rows, (rows.shape[0],) + shape).reshape(rows.shape[0], -1)
    right = np.broadcast_to(cols, shape + (len(ring),)).reshape(-1, len(ring))
    return (left.astype(BF16), right.astype(BF16))


def ring_tables(nodes):
    ring, part = ring_nodes(nodes)
    place = np.arange(3 * nodes)[:, None] - nodes
    into = (place == ring[None]).astype(BF16)
    column = np.arange(2 * nodes)[None]
    out = ((ring[:, None] == column % nodes) & (part[:, None] == column // nodes)).astype(BF16)
    return (into, out)


def permuted(value, table):
    result = None
    for piece in range(3):
        part = value.astype(BF16)
        moved = dot(part, table)
        result = moved if result is None else result + moved
        value = value - part.astype(F32)
    return result


def ring_place(rows, lanes):
    lane = lax.broadcasted_iota(jnp.int32, (rows, lanes), 1)
    return lane % PATCH * (lanes // PATCH) + lane // PATCH


def tiles_beside(even_ref, odd_ref):
    at_even = lax.axis_index("tx") % 2 == 0
    even, odd = even_ref[...], odd_ref[...]
    return (jnp.where(at_even, odd, even), jnp.where(at_even, even, odd))


def gains_kernel(own_ref, even_ref, odd_ref, into_ref, gain_ref, pull_ref, rows_ref):
    strips = gain_ref.shape[0]
    nodes = own_ref.shape[1]
    before, after = tiles_beside(even_ref, odd_ref)
    weight = permuted(jnp.concatenate([before, own_ref[...], after], axis=1), into_ref[...])
    row_node = lax.broadcasted_iota(jnp.int32, weight.shape, 0) - SWEEPS
    row_node = row_node + lax.axis_index("ty") * nodes
    lanes = into_ref.shape[1]
    place = ring_place(1, lanes)
    shift = jnp.where(place < nodes + SWEEPS, 0, jnp.where(place < lanes - SWEEPS, nodes + 2 * SWEEPS, lanes))
    col_node = place - shift + lax.axis_index("tx") * nodes
    inside = (row_node >= 0) & (row_node < lax.axis_size("ty") * nodes)
    inside = inside & (col_node >= 0) & (col_node < lax.axis_size("tx") * nodes)
    gain = jnp.where(inside, 1.0 / (4.0 + weight), 0.0)
    for value, out in ((gain, gain_ref), (gain * weight, pull_ref)):
        rows_ref[...] = value.reshape(value.shape[0], -1, PATCH).transpose(1, 0, 2)
        for strip in range(strips):
            for tile in range(rows_ref.shape[0]):
                out[strip, :, tile * PATCH : (tile + 1) * PATCH] = rows_ref[tile, pl.ds(strip, 8, strips), :]


def gains(own, even, odd, nodes):
    into, _ = ring_tables(nodes)
    shape = jax.ShapeDtypeStruct((own.shape[0] // 8, 8, into.shape[1]), F32)
    return pl.pallas_call(
        gains_kernel,
        out_shape=(shape, shape),
        in_specs=[VMEM] * 4,
        out_specs=(VMEM, VMEM),
        scratch_shapes=[pltpu.VMEM((into.shape[1] // PATCH, own.shape[0], PATCH), F32)],
        compiler_params=PARAMS,
        cost_estimate=pl.CostEstimate(flops=10**9, bytes_accessed=2**20, transcendentals=0),
        name="gains",
    )(own, even, odd, jnp.asarray(into))


def relax_kernel(
    own_ref, even_ref, odd_ref, gain_ref, pull_ref, left_ref, right_ref, cols_table_ref, rows_table_ref,
    work_ref, landing_ref, base_ref,
):
    strips, _, lanes = work_ref.shape
    nodes = landing_ref.shape[1]
    patches = left_ref.shape[1] // 9
    before, after = tiles_beside(even_ref, odd_ref)
    rows = [before[:3], own_ref[:3], after[:3]]
    rows.append(jnp.zeros((PATCH - 9, PATCH), F32))
    columns = jnp.transpose(jnp.concatenate(rows, axis=0))

    def sources(part):
        lines = slice(part * patches, (part + 1) * patches)
        return jnp.concatenate([columns[lines, i : i + 1] for i in range(9)], axis=0)

    place = ring_place(1, lanes)
    second = (place >= nodes + SWEEPS) & (place < lanes - SWEEPS)
    spread = jnp.where(second, sources(1), sources(0)) * right_ref[...].astype(F32)
    target = None
    for piece in range(3):
        part = spread.astype(BF16)
        term = dot(left_ref[...], part)
        target = term if target is None else target + term
        spread = spread - part.astype(F32)
    target = target.reshape(strips, 8, lanes)
    base_ref[...] = pull_ref[...] * target
    work_ref[...] = jnp.where(gain_ref[...] > 0.0, target, 0.0)
    tiles = lanes // PATCH

    def row(strip):
        return [work_ref[strip, :, i * PATCH : (i + 1) * PATCH] for i in range(tiles)]

    def sweep(counter, carry):
        here = row(0)
        above = [pltpu.roll(value, 1, 0) for value in row(strips - 1)]
        around = [pltpu.roll(value, 7, 0) for value in here]
        for strip in range(strips):
            below = row(strip + 1) if strip + 1 < strips else around
            ring = [pltpu.roll(here[-1], 1, 1)] + here + [pltpu.roll(here[0], PATCH - 1, 1)]
            for tile in range(tiles):
                at = (strip, slice(None), slice(tile * PATCH, (tile + 1) * PATCH))
                total = (above[tile] + below[tile]) + (ring[tile] + ring[tile + 2])
                work_ref[at] = gain_ref[at] * total + base_ref[at]
            above, here = here, below
        return carry

    lax.fori_loop(0, SWEEPS, sweep, 0, unroll=32)
    mesh = work_ref[...].reshape(strips * 8, lanes)
    ones = jnp.where(ring_place(16, lanes) < nodes, 1.0, 0.0).astype(BF16)
    sums = None
    for piece in range(3):
        part = mesh.astype(BF16)
        term = lax.dot_general(ones, part, (((1,), (1,)), ((), ())), preferred_element_type=F32)
        sums = term if sums is None else sums + term
        mesh = mesh - part.astype(F32)
    down_mean = permuted(sums, rows_table_ref[...])[:1] / nodes
    strip = lax.broadcasted_iota(jnp.int32, (strips, 8, lanes), 0)
    row = lax.broadcasted_iota(jnp.int32, (strips, 8, lanes), 1) * strips + strip
    kept = jnp.where((row >= SWEEPS) & (row < SWEEPS + nodes), work_ref[...], 0.0)
    across = permuted(jnp.sum(kept, axis=0), cols_table_ref[...])
    across_mean = jnp.sum(across, axis=0, keepdims=True) / nodes
    line = lax.broadcasted_iota(jnp.int32, landing_ref.shape, 0)
    ramp = lax.broadcasted_iota(jnp.int32, landing_ref.shape, 1).astype(F32)
    profile = jnp.where(line == 0, down_mean, across_mean)
    landing_ref[...] = jnp.clip(ramp + profile, 0.0, nodes - 1.0)


def relax(targets, weights, nodes, patches):
    left, right = target_tables(nodes, patches)
    ring, ring_part = ring_nodes(nodes)
    node = np.arange(nodes)[None]
    cols_table = ((ring[:, None] == node) & (ring_part[:, None] == 1)).astype(BF16)
    rows_table = (row_nodes(nodes)[:, None] == node).astype(BF16)
    tables = map(jnp.asarray, (left, right, cols_table, rows_table))
    shape = weights[0].shape
    return pl.pallas_call(
        relax_kernel,
        out_shape=(jax.ShapeDtypeStruct(shape, F32), jax.ShapeDtypeStruct((8, nodes), F32)),
        in_specs=[VMEM] * 9,
        out_specs=(VMEM, VMEM),
        scratch_shapes=[pltpu.VMEM(shape, F32)],
        compiler_params=PARAMS,
        cost_estimate=pl.CostEstimate(flops=4 * 10**9, bytes_accessed=3 * 2**20, transcendentals=0),
        name="relax",
    )(*targets, *weights, *tables)


def mesh_kernel(ring_ref, table_ref, mesh_ref, rows_ref):
    strips, _, lanes = ring_ref.shape
    nodes = mesh_ref.shape[2]
    final = permuted(ring_ref[...].reshape(strips * 8, lanes), table_ref[...])
    for strip in range(strips):
        for part in range(2):
            columns = slice(part * nodes, (part + 1) * nodes)
            rows_ref[part, pl.ds(strip, 8, strips), :] = final[8 * strip : 8 * strip + 8, columns]
    mesh_ref[0] = rows_ref[:, SWEEPS : SWEEPS + nodes]


def natural_mesh(ring, nodes):
    _, table = ring_tables(nodes)
    return pl.pallas_call(
        mesh_kernel,
        out_shape=jax.ShapeDtypeStruct((1, 2, nodes, nodes), F32),
        in_specs=[VMEM] * 2,
        out_specs=VMEM,
        scratch_shapes=[pltpu.VMEM((2, ring.shape[0] * 8, nodes), F32)],
        compiler_params=PARAMS,
        cost_estimate=pl.CostEstimate(flops=10**9, bytes_accessed=2**20, transcendentals=0),
        name="natural_mesh",
    )(ring, jnp.asarray(table))


def compose_kernel(*refs):
    *landing_refs, out_ref = refs
    count = len(landing_refs)
    section = lax.axis_index("gz")
    received = [ref[...] for ref in landing_refs]
    nodes = received[0].shape[1]
    ramp = lax.broadcasted_iota(jnp.int32, received[0].shape, 1).astype(F32)
    value = received[0]
    for other in range(count - 2, -1, -1):
        landing = received[0]
        for code in range(1, count):
            landing = jnp.where(section == other ^ code, received[code], landing)
        floor = jnp.minimum(jnp.floor(landing), nodes - 2.0)
        index = floor.astype(jnp.int32)
        share = landing - floor
        below = jnp.take_along_axis(value, index, axis=1)
        above = jnp.take_along_axis(value, index + 1, axis=1)
        value = jnp.where(section > other, (1.0 - share) * below + share * above, value)
    out_ref[0, 0, 0] = (value - ramp)[:2]


def compose(landings):
    nodes = landings[0].shape[1]
    return pl.pallas_call(
        compose_kernel,
        out_shape=jax.ShapeDtypeStruct((1, 1, 1, 2, nodes), F32),
        in_specs=[VMEM] * len(landings),
        out_specs=VMEM,
        compiler_params=pltpu.CompilerParams(vmem_limit_bytes=2**20),
        name="compose",
    )(*landings)


def swap_pairs(value, axis, first, spare):
    count, other = lax.axis_size(axis), lax.axis_size(spare)
    axes = ("gz", "ty", "tx")
    flip = axes.index(axis) > axes.index(spare)

    def place(here, beside):
        return beside * count + here if flip else here * other + beside

    moves = []
    for here in range(count):
        there = ((here + first) ^ 1) - first
        for beside in range(other):
            target = place(there, beside) if 0 <= there < count else place(here, beside ^ 1)
            moves.append((place(here, beside), target))
    return lax.ppermute(value, (spare, axis) if flip else (axis, spare), moves)


def rows_beside(value):
    count = lax.axis_size("ty")
    if count == 2:
        other = swap_pairs(value, "ty", 0, "gz")
        return (other, other)
    even = swap_pairs(value, "ty", 0, "gz")
    odd = swap_pairs(value, "ty", 1, "gz")
    at_even = lax.axis_index("ty") % 2 == 0
    return (jnp.where(at_even, odd, even), jnp.where(at_even, even, odd))


def to_next(value, turn):
    count, rows = lax.axis_size("gz"), lax.axis_size("ty")
    if not turn:
        return lax.ppermute(value, "gz", [(i, (i + 1) % count) for i in range(count)])
    moves = [(i * rows + j, (i + 1) % count * rows + (j ^ 1)) for i in range(count) for j in range(rows)]
    return lax.ppermute(value, ("gz", "ty"), moves)


def patch_targets(flow):
    first = lax.axis_index("gz") <= 1
    before = to_next(flow, 0)

    def target(near, earlier):
        return jnp.where(first, near[0:1], 0.5 * (near[0:1] + earlier[1:2]))

    if lax.axis_size("ty") == 2:
        beside = target(rows_beside(flow)[0], to_next(flow, 1))
        lines = [beside, target(flow, before), beside]
    else:
        (up, down), (up_before, down_before) = rows_beside(flow), rows_beside(before)
        lines = [target(up, up_before), target(flow, before), target(down, down_before)]
    return jnp.concatenate(lines + [jnp.zeros((5, flow.shape[1]), F32)], axis=0)


def local(images, boundary, anchor):
    nodes = anchor.shape[1]
    own = images[0]
    patches = own.shape[0] // PATCH
    sections = lax.axis_size("gz")
    tables = transform_tables()
    far = swap_pairs(own, "gz", 1, "ty")
    near = swap_pairs(own, "gz", 0, "ty")
    up, down = rows_beside(anchor[0])
    near_spec, *pairs = near_spectra(near, tables)
    own_spec = own_spectra(own, pairs[0], tables)
    far, own_spec, near_spec = lax.optimization_barrier((far, own_spec, near_spec))
    flow = flows(far, boundary, own_spec, near_spec, pairs, tables)
    flow, up, down = lax.optimization_barrier((flow, up, down))
    rows = anchor_rows(up, anchor[0], down)
    weights = gains(rows, swap_pairs(rows, "tx", 0, "gz"), swap_pairs(rows, "tx", 1, "gz"), nodes)
    line = patch_targets(flow)
    targets = (line, swap_pairs(line, "tx", 0, "gz"), swap_pairs(line, "tx", 1, "gz"))
    ring, landing = relax(targets, weights, nodes, patches)
    landings = [landing]
    for code in range(1, sections):
        landings.append(lax.ppermute(landing, "gz", [(i, i ^ code) for i in range(sections)]))
    mesh = natural_mesh(ring, nodes)
    mesh, landings = lax.optimization_barrier((mesh, landings))
    drift = compose(landings)
    return (mesh, drift)


def solution(mesh):
    return jax.shard_map(
        local,
        mesh=mesh,
        in_specs=(P("gz", "ty", "tx"), P("ty", "tx"), P("gz", "ty", "tx")),
        out_specs=(P("gz", None, "ty", "tx"), P("gz", "ty", "tx", None, None)),
        check_vma=False,
    )
```
